128 devices in a mesh: tile: 4 (over x), tm: 16 (over y, z), mode: 2 (over core).
Axes of the slice: x: 4, y: 4, z: 4, core: 2. Of those that a mesh axis runs over, the one named last changes fastest.
Arguments:
- object_field: float32 [2, 1056, 4096], P(None, 'tile', 'tm'), may hold values from -4 to 4
- probe_modes: float32 [4, 2, 256, 256], P('mode'), may hold values from -3 to 3
- amplitudes: float32 [128, 256, 256], P(('tile', 'tm')), may hold values from 0.3 to 2.5
- anchors: int32 [128, 1], P(('tile', 'tm')), may hold values from 0 to 14, as said below
- row_offset: int32 [128], P(('tile', 'tm')), may hold values from 0 to 8
- col_offset: int32 [128], P(('tile', 'tm')), may hold values from 0 to 255
- live_counts: int32 [64], P(('tile', 'tm')), may hold values from 1 to 2, as said below
Outputs:
- object_out: float32 [2, 1056, 4096], P(None, 'tile', 'tm')
- probe_out: float32 [4, 2, 256, 256], P('mode')
The draws below stay inside these ranges and needn't reach their ends.
Inputs may be any that keep to these rules, and one draw needn't show every extreme that they name: The first position of group d has anchor min((d % 16 + 16 // 2) % 16, 14); the other positions' anchors may be any tile of the band up to 14. `live_counts`: some group has all 2 positions live.
All inputs are finite; a program needn't handle non-finite values.
Results may differ from the reference program's by a relative error of at most 0.0033.
Values may be sent and summed in bfloat16 or wider, within the bound.
No kernel may reach another device: no remote copies, remote signals or barrier semaphores. Data moves between devices by JAX's collectives and lax.ppermute only.
A program may use at most 128 MiB of HBM per device.

```python
import math
import jax
import jax.numpy as jnp
from jax import lax

PS = 256
MODES_DEV = 2
ITERS = 2
P_DEV = 2
BH = 264
TW = 256
GROUPS = 64
POS = 128
MODES = 4
OH = 1056
OW = 4096
N_TM = 16
N_MODE = 2


def draw_object_field(key, part):
    key = jax.random.fold_in(key, 13)
    key_scale, key_base = jax.random.split(key)
    magnitude = jnp.exp(jax.random.uniform(key_scale, (OH, OW), jnp.float32, math.log(0.06), math.log(2.4)))
    base = jnp.clip(0.8 * jax.random.normal(key_base, (2, OH, OW), jnp.float32), -3.2, 3.2)
    return jnp.clip(base * magnitude[None], -4.0, 4.0).astype(jnp.float32)


def draw_anchors(key, part):
    key = jax.random.fold_in(key, 7)
    positions = jnp.arange(POS, dtype=jnp.int32)
    column = positions // P_DEV % N_TM
    first_slot = positions % P_DEV == 0
    target = jnp.minimum((column + N_TM // 2) % N_TM, N_TM - 2)
    spread = jax.random.randint(key, (POS,), 0, N_TM - 1)
    return jnp.where(first_slot, target, spread).astype(jnp.int32)[:, None]


def draw_live_counts(key, part):
    key = jax.random.fold_in(key, 11)
    key_counts, key_pick = jax.random.split(key)
    counts = jax.random.randint(key_counts, (GROUPS,), max(1, P_DEV // 2), P_DEV + 1)
    chosen = jax.random.randint(key_pick, (), 0, GROUPS)
    return jnp.where(jnp.arange(GROUPS) == chosen, P_DEV, counts).astype(jnp.int32)


def plant(result, rng, least, top_value):
    longest = result.shape.index(max(result.shape))
    spots = []
    for shift in (0, 1):
        where = [jax.random.randint(jax.random.fold_in(rng, axis), (), 0, length) for axis, length in enumerate(result.shape)]
        where[longest] = (where[longest] + shift) % result.shape[longest]
        spots.append(tuple(where))
    return result.at[spots[0]].set(least).at[spots[1]].set(top_value)


def levels(stream_key, extent, cuts, smallest, high):
    def one(axis_at, shards_of):
        steps = jax.random.uniform(jax.random.fold_in(jax.random.fold_in(stream_key, 6), axis_at), (shards_of,), jnp.float32, smallest / len(cuts), high / len(cuts))
        return jnp.repeat(jnp.exp(steps), extent[axis_at] // shards_of).reshape((-1,) + (1,) * (len(extent) - axis_at - 1))

    loudness = one(*cuts[0])
    for cut in cuts[1:]:
        loudness = loudness * one(*cut)
    return loudness


def normal_values(rng, shape, deviation, limit, pieces=(), kind=jnp.bfloat16):
    factor_of = levels(rng, shape, pieces, -0.22, 0.18) if pieces else 1.0
    values = jax.random.normal(rng, shape, jnp.float32) * deviation * factor_of
    return jnp.minimum(jnp.maximum(values, -limit), limit).astype(kind)


def setup_inputs(seed: int = 0) -> dict:
    keys = jax.random.split(jax.random.key(seed), 8)
    object_field = draw_object_field(jax.random.fold_in(keys[7], 71), 0)
    probe_modes = normal_values(keys[1], (MODES, 2, PS, PS), 0.5, 3.0, ((0, 2),), jnp.float32)
    amplitudes = jnp.clip(0.3 + 2.2 * jax.random.uniform(keys[2], (POS, PS, PS), jnp.float32) ** levels(keys[2], (POS, PS, PS), ((0, 64),), -0.2, 0.2), 0.3, 2.5)
    anchors = draw_anchors(jax.random.fold_in(keys[7], 71), 0)
    row_offset = plant(jax.random.randint(keys[4], (POS,), 0, BH - PS + 1), jax.random.fold_in(keys[4], 1), 0, BH - PS).astype(jnp.int32)
    col_offset = plant(jax.random.randint(keys[5], (POS,), 0, TW), jax.random.fold_in(keys[5], 1), 0, TW - 1).astype(jnp.int32)
    live_counts = draw_live_counts(jax.random.fold_in(keys[7], 71), 0)
    return dict(object_field=object_field, probe_modes=probe_modes, amplitudes=amplitudes, anchors=anchors, row_offset=row_offset, col_offset=col_offset, live_counts=live_counts)


FLOOR_VALUE = 0.5
OBJECT_REG = 1.0
PROBE_REG = 1.0

def halve_round(values):
    grouped = lax.optimization_barrier(jnp.sum(values.reshape(N_MODE, MODES_DEV, PS, PS), axis=1))
    rounded = lax.optimization_barrier(grouped.astype(jnp.bfloat16)).astype(jnp.float32)
    return lax.optimization_barrier(jnp.sum(rounded, axis=0))

def reference(object_field, probe_modes, amplitudes, anchors, row_offset, col_offset, live_counts):
    positions = jnp.arange(POS, dtype=jnp.int32)
    bands = positions // (N_TM * P_DEV)
    owners = positions // P_DEV
    live = (positions % P_DEV < live_counts[owners]).astype(jnp.float32)
    row_start = (bands * BH + row_offset).astype(jnp.int32)
    col_start = (anchors[:, 0] * TW + col_offset).astype(jnp.int32)
    for iteration in range(ITERS):
        low_tile = lax.optimization_barrier(object_field.astype(jnp.bfloat16)).astype(jnp.float32)
        probe_re = probe_modes[:, 0]
        probe_im = probe_modes[:, 1]
        probe_power = lax.optimization_barrier(jnp.sum(probe_re * probe_re + probe_im * probe_im, axis=0))

        def visit(state_carry, inputs):
            accumulator, probe_num, probe_weight = state_carry
            row_at, col_at, alive, measured = inputs
            window = lax.dynamic_slice(low_tile, (jnp.int32(0), row_at, col_at), (2, PS, PS))
            obj_re = window[0]
            obj_im = window[1]
            wave_re = probe_re * obj_re - probe_im * obj_im
            wave_im = probe_re * obj_im + probe_im * obj_re
            far_field = jnp.fft.fft2(lax.complex(wave_re, wave_im), norm='ortho')
            far_power = jnp.real(far_field) ** 2 + jnp.imag(far_field) ** 2
            intensity = halve_round(far_power)
            factor = measured / jnp.sqrt(jnp.maximum(intensity, FLOOR_VALUE))
            back_wave = jnp.fft.ifft2(far_field * factor, norm='ortho')
            delta_re = (jnp.real(back_wave) - wave_re) * alive
            delta_im = (jnp.imag(back_wave) - wave_im) * alive
            num_re = halve_round(probe_re * delta_re + probe_im * delta_im)
            num_im = halve_round(probe_re * delta_im - probe_im * delta_re)
            region = lax.dynamic_slice(accumulator, (jnp.int32(0), row_at, col_at), (3, PS, PS))
            update = jnp.stack([num_re, num_im, probe_power * alive])
            accumulator = lax.dynamic_update_slice(accumulator, region + update, (jnp.int32(0), row_at, col_at))
            probe_num = probe_num + jnp.stack([obj_re * delta_re + obj_im * delta_im, obj_re * delta_im - obj_im * delta_re], axis=1)
            probe_weight = probe_weight + alive * (obj_re * obj_re + obj_im * obj_im)
            return ((accumulator, probe_num, probe_weight), None)
        initial = (jnp.zeros((3, OH, OW), jnp.float32), jnp.zeros((MODES, 2, PS, PS), jnp.float32), jnp.zeros((PS, PS), jnp.float32))
        finals, unused = lax.scan(visit, initial, (row_start, col_start, live, amplitudes))
        accumulator, probe_num, probe_weight = finals
        object_field = object_field + accumulator[:2] / (accumulator[2][None] + OBJECT_REG)
        probe_modes = probe_modes + probe_num / (probe_weight + PROBE_REG)
    return (object_field, probe_modes)
```

```python
import functools

import jax
import jax.numpy as jnp
import ml_dtypes
import numpy as np
from jax import lax
from jax.experimental import pallas as pl
from jax.experimental.pallas import tpu as pltpu
from jax.sharding import PartitionSpec as P

PS = 256
BH = 264
N_TM = 16
CH = 16
HALO = 24
FLOOR_VALUE = 0.5
OBJECT_REG = 1.0
PROBE_REG = 1.0
F32 = jnp.float32
BF16 = jnp.bfloat16
SWAP = [(0, 1), (1, 0)]

VM = pl.BlockSpec(memory_space=pltpu.VMEM)
SM = pl.BlockSpec(memory_space=pltpu.SMEM)


def dft_tables():
    k = np.arange(PS)
    angle = (k[:, None] * k[None, :] % PS) * (2.0 * np.pi / PS)
    re, im = np.cos(angle) / np.sqrt(PS), -np.sin(angle) / np.sqrt(PS)
    fwd = np.block([[re, -im], [im, re]]).astype(np.float32)
    bwd = np.block([[re, im], [-im, re]]).astype(np.float32)
    out = []
    for table in (fwd, bwd):
        high = table.astype(ml_dtypes.bfloat16)
        low = (table - high.astype(np.float32)).astype(ml_dtypes.bfloat16)
        out += [high, low]
    return out


def call(kernel, out_shape, in_specs, scratch=(), flops=0, nbytes=1 << 20):
    many = isinstance(out_shape, (tuple, list))
    return pl.pallas_call(
        kernel,
        out_shape=out_shape,
        in_specs=in_specs,
        out_specs=[VM] * len(out_shape) if many else VM,
        scratch_shapes=list(scratch),
        compiler_params=pltpu.CompilerParams(vmem_limit_bytes=48 << 20),
        cost_estimate=pl.CostEstimate(flops=flops, bytes_accessed=nbytes, transcendentals=0),
    )


def arr(shape, dtype):
    return jax.ShapeDtypeStruct(shape, dtype)


def lanes(rows):
    return lax.broadcasted_iota(jnp.int32, (rows, PS), 1)


def prep_kernel(idx, anchors, row_offset, col_offset, live_counts, obj, out):
    core = idx[0]
    lane = lanes(8)
    meta = jnp.zeros((8, PS), F32)
    for p in range(2):
        alive = jnp.where(p < live_counts[0], 1, 0)
        for k, value in enumerate((anchors[p, 0], col_offset[p], row_offset[p], alive)):
            meta = jnp.where(lane == 4 * p + k, value.astype(F32), meta)
    for i in range(N_TM):
        out[i, 0:HALO, :] = obj[core, CH * i : CH * i + HALO, :]
        out[i, HALO : HALO + 8, :] = meta


def cut_windows(meta, load, out):
    def visit(t, carry):
        for p in range(2):
            at, col, row = meta[t, 4 * p], meta[t, 4 * p + 1], meta[t, 4 * p + 2]
            both = jnp.where(lanes(HALO) >= col, load(at), load(at + 1))
            both = pltpu.roll(both, lax.rem(HALO - row, HALO), 0)
            out[t, CH * p : CH * p + CH, :] = both[0:CH].astype(BF16)
        return carry

    lax.fori_loop(0, N_TM, visit, 0)


def window_kernel(meta, obj, out):
    cut_windows(meta, lambda at: obj[at, 0:HALO, :], out)


def shift_rows(block, row):
    return pltpu.roll(block, lax.rem(HALO + row, 32), 0)[0:HALO]


def accumulate(meta, idx, parts, power, num, weight):
    num[...] = jnp.zeros_like(num)
    weight[...] = jnp.zeros_like(weight)
    first = pl.multiple_of(idx[1] * CH, CH)

    def visit(t, carry):
        both = parts[t, 80:128, :].astype(F32)
        for p in range(2):
            at, col, row, alive = (meta[t, 4 * p + k] for k in range(4))
            mask = lanes(HALO) >= col
            piece = both[HALO * p : HALO * p + HALO]
            num[at] += jnp.where(mask, piece, 0.0)
            num[at + 1] += jnp.where(mask, 0.0, piece)
            cover = pltpu.roll(shift_rows(power[pl.ds(first, 32), :], row), col, 1) * alive.astype(F32)
            weight[at] += jnp.where(mask, cover, 0.0)
            weight[at + 1] += jnp.where(mask, 0.0, cover)
        return carry

    lax.fori_loop(0, N_TM, visit, 0)


def update_kernel(meta, idx, parts, power, obj, out, upd, num, weight, fresh):
    accumulate(meta, idx, parts, power, num, weight)

    def visit(t, carry):
        step = num[t] / (weight[t] + OBJECT_REG)
        upd[t] = step
        fresh[t] = obj[t, 0:HALO, :] + step
        return carry

    lax.fori_loop(0, N_TM, visit, 0)
    cut_windows(meta, lambda at: fresh[at], out)


def last_update_kernel(meta, idx, parts, power, upd, out, num, weight):
    accumulate(meta, idx, parts, power, num, weight)

    def visit(t, carry):
        total = upd[t] + num[t] / (weight[t] + OBJECT_REG)
        out[t] = jnp.concatenate([total, jnp.zeros((8, PS), F32)], axis=0).astype(BF16)
        return carry

    lax.fori_loop(0, N_TM, visit, 0)


def probe_sum_kernel(parts, out):
    total = lax.fori_loop(0, N_TM, lambda t, acc: acc + parts[t, 0:80, :].astype(F32), jnp.zeros((80, PS), F32))
    out[...] = total.astype(BF16)


def probe_update_kernel(own, one, two, three, objs, out):
    total = (own[...].astype(F32) + two[...].astype(F32)) + (one[...].astype(F32) + three[...].astype(F32))
    scale = 1.0 / (total[64:80] + PROBE_REG)
    step = (total[0:64] * jnp.concatenate([scale] * 4, axis=0)).astype(BF16)

    def visit(t, carry):
        out[t, 0:32, :] = objs[t]
        out[t, 32:96, :] = step
        return carry

    lax.fori_loop(0, N_TM, visit, 0)


def pack_kernel(idx, keep, recv, out):
    first = idx[0] == 0

    def visit(t, carry):
        mine, theirs = keep[t].astype(F32), recv[t].astype(F32)
        out[t, 0:80, :] = (mine[0:80] + theirs[0:80]).astype(BF16)
        num_mine, num_theirs = mine[80 : 80 + HALO], theirs[80 : 80 + HALO]
        out[t, 80:128, :] = jnp.concatenate(
            [jnp.where(first, num_mine, num_theirs), jnp.where(first, num_theirs, num_mine)], axis=0
        ).astype(BF16)
        return carry

    lax.fori_loop(0, N_TM, visit, 0)


def split(value):
    high = value.astype(BF16)
    return high, (value - high.astype(F32)).astype(BF16)


def dot(a, b):
    return lax.dot_general(a, b, (((1,), (0,)), ((), ())), preferred_element_type=F32)


def position_kernel(
    with_update, idx, row_offset, col_offset, live_counts, mh, ml, nh, nl, p_own, p_oth, h_own, h_oth, amp,
    keep, send, power, obj, probe, far, xh, xl, yh, yl, res, factor, group, num, shifted,
):
    core = idx[0]
    first = core == 0
    col, row = col_offset[core], row_offset[core]
    alive = jnp.where(core < live_counts[0], 1, 0).astype(F32)
    back_col = lax.rem(PS - col, PS)

    def rows_of(i):
        return pl.ds(pl.multiple_of(i * CH, CH), CH)

    power[0:8, :] = jnp.zeros((8, PS), F32)
    power[264:272, :] = jnp.zeros((8, PS), F32)

    def stage(i, carry):
        rows = rows_of(i)
        mine = jnp.where(first, h_own[i, 0:CH, :].astype(F32), h_own[i, CH : 2 * CH, :].astype(F32))
        theirs = jnp.where(first, h_oth[i, 0:CH, :].astype(F32), h_oth[i, CH : 2 * CH, :].astype(F32))
        obj_re = pltpu.roll(jnp.where(first, mine, theirs), back_col, 1)
        obj_im = pltpu.roll(jnp.where(first, theirs, mine), back_col, 1)
        obj[0, rows, :] = obj_re
        obj[1, rows, :] = obj_im
        denom = ((obj_re * obj_re + obj_im * obj_im) * alive).astype(BF16)
        keep[i, 64:80, :] = denom
        send[i, 64:80, :] = denom
        total = jnp.zeros((CH, PS), F32)
        for m in range(4):
            src, chunk = (p_own, h_own) if m < 2 else (p_oth, h_oth)
            for k in range(2):
                value = src[m % 2, k, rows, :]
                if with_update:
                    at = 32 + CH * (2 * (m % 2) + k)
                    value = value + chunk[i, at : at + CH, :].astype(F32)
                probe[m, k, rows, :] = value
                total = total + value * value
        power[pl.ds(pl.multiple_of(i * CH + 8, 8), CH), :] = total
        return carry

    lax.fori_loop(0, N_TM, stage, 0)

    def wave(m, rows):
        pr, pi = probe[m, 0, rows, :], probe[m, 1, rows, :]
        o_r, o_i = obj[0, rows, :], obj[1, rows, :]
        return pr, pi, o_r, o_i, pr * o_r - pi * o_i, pr * o_i + pi * o_r

    def put_x(i, re, im):
        for k, value in enumerate((re, im)):
            rows = pl.ds(pl.multiple_of(i * CH + k * PS, CH), CH)
            xh[rows, :], xl[rows, :] = split(value)

    def transform(left_h, left_l, right_h, right_l, out):
        high, low = xh[...], xl[...]
        half = dot(left_h[...], high) + dot(left_h[...], low) + dot(left_l[...], high)
        for k in range(2):
            yh[:, k * PS : (k + 1) * PS], yl[:, k * PS : (k + 1) * PS] = split(half[k * PS : (k + 1) * PS])
        high, low = yh[...], yl[...]
        out[...] = dot(high, right_h[...]) + dot(low, right_h[...]) + dot(high, right_l[...])

    def forward(m, carry):
        def pre(i, carry):
            values = wave(m, rows_of(i))
            put_x(i, values[4], values[5])
            return carry

        lax.fori_loop(0, N_TM, pre, 0)
        transform(mh, ml, nh, nl, far.at[m])
        return carry

    lax.fori_loop(0, 4, forward, 0)

    def intensity(i, carry):
        rows = rows_of(i)
        total = jnp.zeros((CH, PS), F32)
        for g in range(2):
            part = jnp.zeros((CH, PS), F32)
            for m in (2 * g, 2 * g + 1):
                re, im = far[m, rows, 0:PS], far[m, rows, PS : 2 * PS]
                part = part + (re * re + im * im)
            total = total + part.astype(BF16).astype(F32)
        factor[rows, :] = amp[core, rows, :] * lax.rsqrt(jnp.maximum(total, FLOOR_VALUE))
        return carry

    lax.fori_loop(0, N_TM, intensity, 0)

    for g in range(2):
        target = (keep, send)[g]

        def backward(mm, carry, g=g, target=target):
            m = 2 * g + mm

            def pre(i, carry):
                rows = rows_of(i)
                f = factor[rows, :]
                put_x(i, far[m, rows, 0:PS] * f, far[m, rows, PS : 2 * PS] * f)
                return carry

            lax.fori_loop(0, N_TM, pre, 0)
            transform(nh, nl, mh, ml, res)

            def post(i, carry):
                rows = rows_of(i)
                pr, pi, o_r, o_i, wr, wi = wave(m, rows)
                dr = (res[rows, 0:PS] - wr) * alive
                di = (res[rows, PS : 2 * PS] - wi) * alive
                at = pl.multiple_of(mm * 2 * CH, 2 * CH)
                target[i, pl.ds(at, 2 * CH), :] = jnp.concatenate(
                    [o_r * dr + o_i * di, o_r * di - o_i * dr], axis=0
                ).astype(BF16)
                group[mm, 0, rows, :] = pr * dr + pi * di
                group[mm, 1, rows, :] = pr * di - pi * dr
                return carry

            lax.fori_loop(0, N_TM, post, 0)
            return carry

        lax.fori_loop(0, 2, backward, 0)

        def gather(i, carry, g=g):
            rows = rows_of(i)
            for k in range(2):
                part = (group[0, k, rows, :] + group[1, k, rows, :]).astype(BF16).astype(F32)
                num[k, rows, :] = part if g == 0 else num[k, rows, :] + part
            return carry

        lax.fori_loop(0, N_TM, gather, 0)

    shifted[:, 0:8, :] = jnp.zeros((2, 8, PS), F32)
    shifted[:, 264:272, :] = jnp.zeros((2, 8, PS), F32)

    def place(i, carry):
        for k in range(2):
            shifted[k, pl.ds(pl.multiple_of(i * CH + 8, 8), CH), :] = pltpu.roll(num[k, rows_of(i), :], col, 1)
        return carry

    lax.fori_loop(0, N_TM, place, 0)

    def emit(i, carry):
        rows = pl.ds(pl.multiple_of(i * CH, CH), 32)
        pad = jnp.zeros((8, PS), F32)
        re, im = (
            jnp.concatenate([shift_rows(shifted[k, rows, :], row), pad], axis=0) for k in range(2)
        )
        keep[i, 80:112, :] = jnp.where(first, re, im).astype(BF16)
        send[i, 80:112, :] = jnp.where(first, im, re).astype(BF16)
        return carry

    lax.fori_loop(0, N_TM, emit, 0)


def final_kernel(idx, obj, p_own, h_one, h_own, h_oth, obj_out, probe_out):
    core = idx[0]

    def visit(i, carry):
        rows = pl.ds(pl.multiple_of(i * CH, CH), CH)
        obj_out[core, rows, :] = obj[core, rows, :] + h_own[i, 0:CH, :].astype(F32)
        obj_out[1 - core, rows, :] = obj[1 - core, rows, :] + h_oth[i, 0:CH, :].astype(F32)
        for m in range(2):
            for k in range(2):
                at = 32 + CH * (2 * m + k)
                before = p_own[m, k, rows, :] + h_one[i, at : at + CH, :].astype(F32)
                probe_out[m, k, rows, :] = before + h_own[i, at : at + CH, :].astype(F32)
        return carry

    lax.fori_loop(0, N_TM, visit, 0)
    last = N_TM - 1
    obj_out[core, 256:264, :] = obj[core, 256:264, :] + h_own[last, 16:32, :].astype(F32)[0:8]
    obj_out[1 - core, 256:264, :] = obj[1 - core, 256:264, :] + h_oth[last, 16:32, :].astype(F32)[0:8]


def body(object_field, probe_modes, amplitudes, anchors, row_offset, col_offset, live_counts):
    idx = jnp.stack([lax.axis_index("mode"), lax.axis_index("tm")]).astype(jnp.int32)
    tables = [jnp.asarray(t) for t in dft_tables()]

    def exchange(x):
        return lax.all_to_all(x, "tm", 0, 0)

    def swap(x):
        return lax.ppermute(x, "mode", SWAP)

    def over_tiles(x):
        n = lax.axis_size("tile")
        return [lax.ppermute(x, "tile", [(i, (i + k) % n) for i in range(n)]) for k in (1, 2, 3)]

    probe_other = swap(probe_modes)
    slots = call(prep_kernel, arr((N_TM, 32, PS), F32), [SM] * 5 + [VM])(
        idx, anchors, row_offset, col_offset, live_counts, object_field
    )
    obj = exchange(slots)
    meta = obj[:, HALO, 0:8].astype(jnp.int32)
    windows = call(window_kernel, arr((N_TM, 32, PS), BF16), [SM, VM])(meta, obj)
    h_own = exchange(windows)
    h_first = h_own

    for iteration in range(2):
        h_oth = swap(h_own)
        part = arr((N_TM, 112, PS), BF16)
        keep, send, power = call(
            functools.partial(position_kernel, iteration > 0),
            (part, part, arr((272, PS), F32)),
            [SM] * 4 + [VM] * 9,
            scratch=[
                pltpu.VMEM((2, PS, PS), F32),
                pltpu.VMEM((4, 2, PS, PS), F32),
                pltpu.VMEM((4, PS, 2 * PS), F32),
                pltpu.VMEM((2 * PS, PS), BF16),
                pltpu.VMEM((2 * PS, PS), BF16),
                pltpu.VMEM((PS, 2 * PS), BF16),
                pltpu.VMEM((PS, 2 * PS), BF16),
                pltpu.VMEM((PS, 2 * PS), F32),
                pltpu.VMEM((PS, PS), F32),
                pltpu.VMEM((2, 2, PS, PS), F32),
                pltpu.VMEM((2, PS, PS), F32),
                pltpu.VMEM((2, 272, PS), F32),
            ],
            flops=16 * 3 * 2 * 512 * 512 * 256,
            nbytes=10 << 20,
        )(idx, row_offset, col_offset, live_counts, *tables, probe_modes, probe_other, h_own, h_oth, amplitudes)
        recv = swap(send)
        parts = call(pack_kernel, arr((N_TM, 128, PS), BF16), [SM, VM, VM])(idx, keep, recv)
        parts = exchange(parts)
        probe_part = call(probe_sum_kernel, arr((80, PS), BF16), [VM])(parts)
        others = over_tiles(probe_part)
        chunk = pltpu.VMEM((N_TM, HALO, PS), F32)
        if iteration == 0:
            objs, upd = call(
                update_kernel,
                (arr((N_TM, 32, PS), BF16), arr((N_TM, HALO, PS), F32)),
                [SM, SM, VM, VM, VM],
                scratch=[chunk] * 3,
                nbytes=8 << 20,
            )(meta, idx, parts, power, obj)
        else:
            objs = call(
                last_update_kernel,
                arr((N_TM, 32, PS), BF16),
                [SM, SM, VM, VM, VM],
                scratch=[chunk] * 2,
                nbytes=8 << 20,
            )(meta, idx, parts, power, upd)
        h_first = h_own
        h_own = exchange(
            call(probe_update_kernel, arr((N_TM, 96, PS), BF16), [VM] * 5)(probe_part, *others, objs)
        )

    return call(
        final_kernel, (arr((2, BH, PS), F32), arr((2, 2, PS, PS), F32)), [SM] + [VM] * 5
    )(idx, object_field, probe_modes, h_first, h_own, swap(h_own))


def solution(mesh):
    placed = (
        P(None, "tile", "tm"),
        P("mode", None, None, None),
        P(("tile", "tm"), None, None),
        P(("tile", "tm"), None),
        P(("tile", "tm")),
        P(("tile", "tm")),
        P(("tile", "tm")),
    )
    return jax.shard_map(
        body,
        mesh=mesh,
        in_specs=placed,
        out_specs=(P(None, "tile", "tm"), P("mode", None, None, None)),
        check_vma=False,
    )
```

```python
import functools

import jax
import jax.numpy as jnp
import ml_dtypes
import numpy as np
from jax import lax
from jax.experimental import pallas as pl
from jax.experimental.pallas import tpu as pltpu
from jax.sharding import PartitionSpec as P

PS = 256
HALF = 128
BH = 264
N_TM = 16
CH = 16
HALO = 24
FLOOR_VALUE = 0.5
OBJECT_REG = 1.0
PROBE_REG = 1.0
F32 = jnp.float32
BF16 = jnp.bfloat16
SWAP = [(0, 1), (1, 0)]

VM = pl.BlockSpec(memory_space=pltpu.VMEM)
SM = pl.BlockSpec(memory_space=pltpu.SMEM)


def real_form(matrix):
    return np.block([[matrix.real, -matrix.imag], [matrix.imag, matrix.real]]).astype(np.float32)


def halves(table):
    high = table.astype(ml_dtypes.bfloat16)
    return high, (table - high.astype(np.float32)).astype(ml_dtypes.bfloat16)


def dft_tables():
    n = np.arange(HALF)
    left, right = [], []
    for k in (2 * n, 2 * n + 1):
        table = real_form(np.exp(-2j * np.pi * ((k[:, None] * n[None, :]) % PS) / PS) / np.sqrt(PS))
        for form in (table, np.ascontiguousarray(table.T)):
            high, low = halves(form)
            left.append(np.concatenate([high, high, low], axis=1))
            right.append(np.concatenate([high, high, low], axis=0))
    return left + right


def order_table():
    picked = np.concatenate([np.arange(0, PS, 2), np.arange(1, PS, 2)])
    table = np.zeros((PS, PS), np.float32)
    table[np.arange(PS), picked] = 1.0
    return table.astype(ml_dtypes.bfloat16)


def call(kernel, out_shape, in_specs, scratch=(), flops=0, nbytes=1 << 20):
    many = isinstance(out_shape, (tuple, list))
    return pl.pallas_call(
        kernel,
        out_shape=out_shape,
        in_specs=in_specs,
        out_specs=[VM] * len(out_shape) if many else VM,
        scratch_shapes=list(scratch),
        compiler_params=pltpu.CompilerParams(vmem_limit_bytes=48 << 20),
        cost_estimate=pl.CostEstimate(flops=flops, bytes_accessed=nbytes, transcendentals=0),
    )


def arr(shape, dtype):
    return jax.ShapeDtypeStruct(shape, dtype)


def lanes(rows):
    return lax.broadcasted_iota(jnp.int32, (rows, PS), 1)


def split(value):
    high = value.astype(BF16)
    return high, (value - high.astype(F32)).astype(BF16)


def dot(a, b):
    return lax.dot_general(a, b, (((1,), (0,)), ((), ())), preferred_element_type=F32)


def prep_kernel(idx, anchors, row_offset, col_offset, live_counts, obj, high, low):
    core = idx[0]
    lane = lanes(8)
    meta = jnp.zeros((8, PS), F32)
    for p in range(2):
        alive = jnp.where(p < live_counts[0], 1, 0)
        for k, value in enumerate((anchors[p, 0], col_offset[p], row_offset[p], alive)):
            meta = jnp.where(lane == 4 * p + k, value.astype(F32), meta)
    for i in range(N_TM):
        chunk = obj[core, CH * i : CH * i + HALO, :]
        rounded = chunk.astype(BF16).astype(F32)
        high[i] = jnp.concatenate([rounded, meta], axis=0).astype(BF16)
        low[i] = jnp.concatenate([chunk - rounded, jnp.zeros((8, PS), F32)], axis=0).astype(BF16)


def order_kernel(idx, table, amp, out):
    def lines(value, product):
        high, low = split(value)
        return product(high) + product(low)

    rows = lines(amp[idx[0]], lambda x: dot(table[...], x))
    out[...] = lines(rows, lambda x: lax.dot_general(x, table[...], (((1,), (1,)), ((), ())), preferred_element_type=F32))


def cut_windows(meta, load, out, denom):
    def visit(t, total):
        for p in range(2):
            at, col, row, alive = (meta[t, 4 * p + k] for k in range(4))
            both = jnp.where(lanes(HALO) >= col, load(at), load(at + 1))
            both = pltpu.roll(both, lax.rem(HALO - row, HALO), 0)[0:CH].astype(BF16)
            out[t, CH * p : CH * p + CH, :] = both
            both = pltpu.roll(both.astype(F32), lax.rem(PS - col, PS), 1)
            total = total + both * both * alive.astype(F32)
        return total

    denom[...] = lax.fori_loop(0, N_TM, visit, jnp.zeros((CH, PS), F32))


def window_kernel(meta, high, low, out, denom):
    def visit(t, carry):
        out[t, 32:64, :] = low[t]
        return carry

    lax.fori_loop(0, N_TM, visit, 0)
    cut_windows(meta, lambda at: high[at].astype(F32)[0:HALO], out, denom)


def shift_rows(block, row):
    return pltpu.roll(block, lax.rem(HALO + row, 32), 0)[0:HALO]


def accumulate(meta, idx, parts, power, num, weight):
    num[...] = jnp.zeros_like(num)
    weight[...] = jnp.zeros_like(weight)
    first = pl.multiple_of(idx[1] * CH, CH)

    def visit(t, carry):
        both = parts[t, 64:112, :].astype(F32)
        for p in range(2):
            at, col, row, alive = (meta[t, 4 * p + k] for k in range(4))
            mask = lanes(HALO) >= col
            piece = both[HALO * p : HALO * p + HALO]
            num[at] += jnp.where(mask, piece, 0.0)
            num[at + 1] += jnp.where(mask, 0.0, piece)
            cover = pltpu.roll(shift_rows(power[pl.ds(first, 32), :], row), col, 1) * alive.astype(F32)
            weight[at] += jnp.where(mask, cover, 0.0)
            weight[at + 1] += jnp.where(mask, 0.0, cover)
        return carry

    lax.fori_loop(0, N_TM, visit, 0)


def update_kernel(meta, idx, parts, power, high, low, out, denom, upd, num, weight, fresh):
    accumulate(meta, idx, parts, power, num, weight)

    def visit(t, carry):
        step = num[t] / (weight[t] + OBJECT_REG)
        upd[t] = step
        fresh[t] = (high[t].astype(F32)[0:HALO] + low[t, 32:64, :].astype(F32)[0:HALO]) + step
        return carry

    lax.fori_loop(0, N_TM, visit, 0)
    cut_windows(meta, lambda at: fresh[at], out, denom)


def last_update_kernel(meta, idx, parts, power, upd, out, num, weight):
    accumulate(meta, idx, parts, power, num, weight)

    def visit(t, carry):
        total = upd[t] + num[t] / (weight[t] + OBJECT_REG)
        out[t] = jnp.concatenate([total, jnp.zeros((8, PS), F32)], axis=0).astype(BF16)
        return carry

    lax.fori_loop(0, N_TM, visit, 0)


def probe_sum_kernel(parts, denom_own, denom_oth, out):
    total = lax.fori_loop(0, N_TM, lambda t, acc: acc + parts[t, 0:64, :].astype(F32), jnp.zeros((64, PS), F32))
    out[0:64, :] = total.astype(BF16)
    out[64:80, :] = (denom_own[...] + denom_oth[...]).astype(BF16)


def probe_update_kernel(own, one, two, three, objs, out):
    total = (own[...].astype(F32) + two[...].astype(F32)) + (one[...].astype(F32) + three[...].astype(F32))
    scale = 1.0 / (total[64:80] + PROBE_REG)
    step = (total[0:64] * jnp.concatenate([scale] * 4, axis=0)).astype(BF16)

    def visit(t, carry):
        out[t, 0:32, :] = objs[t]
        out[t, 32:96, :] = step
        return carry

    lax.fori_loop(0, N_TM, visit, 0)


def pack_kernel(idx, keep, recv, out):
    first = idx[0] == 0

    def visit(t, carry):
        mine, theirs = keep[t].astype(F32), recv[t].astype(F32)
        out[t, 0:64, :] = (mine[0:64] + theirs[0:64]).astype(BF16)
        num_mine, num_theirs = mine[64 : 64 + HALO], theirs[64 : 64 + HALO]
        out[t, 64:112, :] = jnp.concatenate(
            [jnp.where(first, num_mine, num_theirs), jnp.where(first, num_theirs, num_mine)], axis=0
        ).astype(BF16)
        return carry

    lax.fori_loop(0, N_TM, visit, 0)


def put_left(ref, row, cols, value):
    high, low = split(value)
    for k, part in enumerate((high, low, high)):
        ref[pl.ds(pl.multiple_of(row + k * PS, CH), CH), cols] = part


def put_right(ref, rows, lane, value):
    high, low = split(value)
    for k, part in enumerate((high, low, high)):
        ref[rows, lane + k * PS : lane + k * PS + HALF] = part


def position_kernel(
    with_update, idx, row_offset, col_offset, live_counts,
    l_even, l_even_t, l_odd, l_odd_t, r_even, r_even_t, r_odd, r_odd_t, p_own, p_oth, h_own, h_oth, amp,
    keep, send, power, obj, probe, x_even, x_odd, y_even, y_odd, half_even, half_odd, far_even, far_odd, num, shifted,
):
    core = idx[0]
    first = core == 0
    col, row = col_offset[core], row_offset[core]
    alive = jnp.where(core < live_counts[0], 1, 0).astype(F32)
    back_col = lax.rem(PS - col, PS)

    def rows_of(i, base=0):
        return pl.ds(pl.multiple_of(i * CH + base, CH), CH)

    def mode_cols(m):
        return slice(m * PS, (m + 1) * PS)

    power[0:8, :] = jnp.zeros((8, PS), F32)
    power[264:272, :] = jnp.zeros((8, PS), F32)

    def stage(i, carry):
        rows = rows_of(i)
        mine = jnp.where(first, h_own[i, 0:CH, :].astype(F32), h_own[i, CH : 2 * CH, :].astype(F32))
        theirs = jnp.where(first, h_oth[i, 0:CH, :].astype(F32), h_oth[i, CH : 2 * CH, :].astype(F32))
        obj[0, rows, :] = pltpu.roll(jnp.where(first, mine, theirs), back_col, 1)
        obj[1, rows, :] = pltpu.roll(jnp.where(first, theirs, mine), back_col, 1)
        total = jnp.zeros((CH, PS), F32)
        for m in range(4):
            src, chunk = (p_own, h_own) if m < 2 else (p_oth, h_oth)
            for k in range(2):
                value = src[m % 2, k, rows, :]
                if with_update:
                    at = 32 + CH * (2 * (m % 2) + k)
                    value = value + chunk[i, at : at + CH, :].astype(F32)
                probe[m, k, rows, :] = value
                total = total + value * value
        power[pl.ds(pl.multiple_of(i * CH + 8, 8), CH), :] = total
        return carry

    lax.fori_loop(0, N_TM, stage, 0)

    def wave(m, rows):
        pr, pi = probe[m, 0, rows, :], probe[m, 1, rows, :]
        o_r, o_i = obj[0, rows, :], obj[1, rows, :]
        return pr, pi, o_r, o_i, pr * o_r - pi * o_i, pr * o_i + pi * o_r

    def forward_rows(i, carry):
        for m in range(4):
            upper, lower = wave(m, rows_of(i)), wave(m, rows_of(i, HALF))
            for k in range(2):
                a, b = upper[4 + k], lower[4 + k]
                put_left(x_even, i * CH + k * HALF, mode_cols(m), a + b)
                put_left(x_odd, i * CH + k * HALF, mode_cols(m), a - b)
        return carry

    lax.fori_loop(0, HALF // CH, forward_rows, 0)
    half_even[...] = dot(l_even[...], x_even[...])
    half_odd[...] = dot(l_odd[...], x_odd[...])

    def forward_cols(i, carry):
        for m in range(4):
            for b, half in enumerate((half_even, half_odd)):
                for k in range(2):
                    value = half[rows_of(i, k * HALF), mode_cols(m)]
                    rows = rows_of(i, m * PS + b * HALF)
                    put_right(y_even, rows, k * HALF, value[:, 0:HALF] + value[:, HALF:PS])
                    put_right(y_odd, rows, k * HALF, value[:, 0:HALF] - value[:, HALF:PS])
        return carry

    lax.fori_loop(0, HALF // CH, forward_cols, 0)
    far_even[...] = dot(y_even[...], r_even_t[...])
    far_odd[...] = dot(y_odd[...], r_odd_t[...])

    def rescale(i, carry):
        for b, (far, y) in enumerate(((far_even, y_even), (far_odd, y_odd))):
            values = [far[rows_of(i, m * PS), :] for m in range(4)]
            squares = [v[:, 0:HALF] * v[:, 0:HALF] + v[:, HALF:PS] * v[:, HALF:PS] for v in values]
            total = (squares[0] + squares[1]).astype(BF16).astype(F32) + (squares[2] + squares[3]).astype(
                BF16
            ).astype(F32)
            factor = amp[rows_of(i), b * HALF : (b + 1) * HALF] * lax.rsqrt(jnp.maximum(total, FLOOR_VALUE))
            for m in range(4):
                for k in range(2):
                    put_right(y, rows_of(i, m * PS), k * HALF, values[m][:, k * HALF : (k + 1) * HALF] * factor)
        return carry

    lax.fori_loop(0, N_TM, rescale, 0)
    far_even[...] = dot(y_even[...], r_even[...])
    far_odd[...] = dot(y_odd[...], r_odd[...])

    def backward_cols(i, carry):
        for m in range(4):
            for b, x in enumerate((x_even, x_odd)):
                rows = rows_of(i, m * PS + b * HALF)
                even, odd = far_even[rows, :], far_odd[rows, :]
                total, diff = even + odd, even - odd
                for k in range(2):
                    part = slice(k * HALF, (k + 1) * HALF)
                    put_left(x, i * CH + k * HALF, slice(m * PS, m * PS + HALF), total[:, part])
                    put_left(x, i * CH + k * HALF, slice(m * PS + HALF, (m + 1) * PS), diff[:, part])
        return carry

    lax.fori_loop(0, HALF // CH, backward_cols, 0)
    half_even[...] = dot(l_even_t[...], x_even[...])
    half_odd[...] = dot(l_odd_t[...], x_odd[...])

    def outputs(i, carry):
        for s in range(2):
            rows = rows_of(i, s * HALF)
            n_re, n_im = jnp.zeros((CH, PS), F32), jnp.zeros((CH, PS), F32)
            for g, target in enumerate((keep, send)):
                g_re, g_im = jnp.zeros((CH, PS), F32), jnp.zeros((CH, PS), F32)
                for mm in range(2):
                    m = 2 * g + mm
                    pr, pi, o_r, o_i, wr, wi = wave(m, rows)
                    res = []
                    for k in range(2):
                        at = rows_of(i, k * HALF)
                        even, odd = half_even[at, mode_cols(m)], half_odd[at, mode_cols(m)]
                        res.append(even + odd if s == 0 else even - odd)
                    dr, di = (res[0] - wr) * alive, (res[1] - wi) * alive
                    chunk = i + s * (HALF // CH)
                    target[chunk, 2 * mm * CH : (2 * mm + 1) * CH, :] = (o_r * dr + o_i * di).astype(BF16)
                    target[chunk, (2 * mm + 1) * CH : (2 * mm + 2) * CH, :] = (o_r * di - o_i * dr).astype(BF16)
                    g_re = g_re + (pr * dr + pi * di)
                    g_im = g_im + (pr * di - pi * dr)
                n_re = n_re + g_re.astype(BF16).astype(F32)
                n_im = n_im + g_im.astype(BF16).astype(F32)
            at = pl.ds(pl.multiple_of(i * CH + s * HALF + 8, 8), CH)
            shifted[0, at, :] = pltpu.roll(n_re, col, 1)
            shifted[1, at, :] = pltpu.roll(n_im, col, 1)
        return carry

    shifted[:, 0:8, :] = jnp.zeros((2, 8, PS), F32)
    shifted[:, 264:272, :] = jnp.zeros((2, 8, PS), F32)
    lax.fori_loop(0, HALF // CH, outputs, 0)

    def emit(i, carry):
        rows = pl.ds(pl.multiple_of(i * CH, CH), 32)
        pad = jnp.zeros((8, PS), F32)
        re, im = (
            jnp.concatenate([shift_rows(shifted[k, rows, :], row), pad], axis=0) for k in range(2)
        )
        keep[i, 64:96, :] = jnp.where(first, re, im).astype(BF16)
        send[i, 64:96, :] = jnp.where(first, im, re).astype(BF16)
        return carry

    lax.fori_loop(0, N_TM, emit, 0)


def final_kernel(idx, obj, p_own, h_one, h_own, h_oth, obj_out, probe_out):
    core = idx[0]

    def visit(i, carry):
        rows = pl.ds(pl.multiple_of(i * CH, CH), CH)
        obj_out[core, rows, :] = obj[core, rows, :] + h_own[i, 0:CH, :].astype(F32)
        obj_out[1 - core, rows, :] = obj[1 - core, rows, :] + h_oth[i, 0:CH, :].astype(F32)
        for m in range(2):
            for k in range(2):
                at = 32 + CH * (2 * m + k)
                before = p_own[m, k, rows, :] + h_one[i, at : at + CH, :].astype(F32)
                probe_out[m, k, rows, :] = before + h_own[i, at : at + CH, :].astype(F32)
        return carry

    lax.fori_loop(0, N_TM, visit, 0)
    last = N_TM - 1
    obj_out[core, 256:264, :] = obj[core, 256:264, :] + h_own[last, 16:32, :].astype(F32)[0:8]
    obj_out[1 - core, 256:264, :] = obj[1 - core, 256:264, :] + h_oth[last, 16:32, :].astype(F32)[0:8]


def body(object_field, probe_modes, amplitudes, anchors, row_offset, col_offset, live_counts):
    idx = jnp.stack([lax.axis_index("mode"), lax.axis_index("tm")]).astype(jnp.int32)
    tables = [jnp.asarray(t) for t in dft_tables()]

    def exchange(x):
        return lax.all_to_all(x, "tm", 0, 0)

    def swap(x):
        return lax.ppermute(x, "mode", SWAP)

    def over_tiles(x):
        n = lax.axis_size("tile")
        return [lax.ppermute(x, "tile", [(i, (i + k) % n) for i in range(n)]) for k in (1, 2, 3)]

    probe_other = swap(probe_modes)
    slot = arr((N_TM, 32, PS), BF16)
    denom_shape = arr((CH, PS), F32)
    high, low = call(prep_kernel, (slot, slot), [SM] * 5 + [VM])(
        idx, anchors, row_offset, col_offset, live_counts, object_field
    )
    high = exchange(high)
    amp = call(order_kernel, arr((PS, PS), F32), [SM, VM, VM])(idx, jnp.asarray(order_table()), amplitudes)
    meta = high[:, HALO, 0:8].astype(jnp.int32)
    windows, denom = call(window_kernel, (arr((N_TM, 64, PS), BF16), denom_shape), [SM, VM, VM])(meta, high, low)
    denom_other = swap(denom)
    h_own = exchange(windows)
    low = h_own

    for iteration in range(2):
        h_oth = swap(h_own)
        part = arr((N_TM, 96, PS), BF16)
        left, right = pltpu.VMEM((3 * PS, 4 * PS), BF16), pltpu.VMEM((4 * PS, 3 * PS), BF16)
        keep, send, power = call(
            functools.partial(position_kernel, iteration > 0),
            (part, part, arr((272, PS), F32)),
            [SM] * 4 + [VM] * 13,
            scratch=[
                pltpu.VMEM((2, PS, PS), F32),
                pltpu.VMEM((4, 2, PS, PS), F32),
                left,
                left,
                right,
                right,
                pltpu.VMEM((PS, 4 * PS), F32),
                pltpu.VMEM((PS, 4 * PS), F32),
                pltpu.VMEM((4 * PS, PS), F32),
                pltpu.VMEM((4 * PS, PS), F32),
                pltpu.VMEM((2, PS, PS), F32),
                pltpu.VMEM((2, 272, PS), F32),
            ],
            flops=32 * 3 * 2 * 256 * 256 * 256,
            nbytes=10 << 20,
        )(idx, row_offset, col_offset, live_counts, *tables, probe_modes, probe_other, h_own, h_oth, amp)
        recv = swap(send)
        parts = call(pack_kernel, arr((N_TM, 112, PS), BF16), [SM, VM, VM])(idx, keep, recv)
        parts = exchange(parts)
        probe_part = call(probe_sum_kernel, arr((80, PS), BF16), [VM] * 3)(parts, denom, denom_other)
        others = over_tiles(probe_part)
        chunk = pltpu.VMEM((N_TM, HALO, PS), F32)
        if iteration == 0:
            objs, denom, upd = call(
                update_kernel,
                (slot, denom_shape, arr((N_TM, HALO, PS), F32)),
                [SM, SM, VM, VM, VM, VM],
                scratch=[chunk] * 3,
                nbytes=8 << 20,
            )(meta, idx, parts, power, high, low)
            denom_other = swap(denom)
        else:
            objs = call(
                last_update_kernel,
                slot,
                [SM, SM, VM, VM, VM],
                scratch=[chunk] * 2,
                nbytes=8 << 20,
            )(meta, idx, parts, power, upd)
        h_first = h_own
        h_own = exchange(
            call(probe_update_kernel, arr((N_TM, 96, PS), BF16), [VM] * 5)(probe_part, *others, objs)
        )

    return call(
        final_kernel, (arr((2, BH, PS), F32), arr((2, 2, PS, PS), F32)), [SM] + [VM] * 5
    )(idx, object_field, probe_modes, h_first, h_own, swap(h_own))


def solution(mesh):
    placed = (
        P(None, "tile", "tm"),
        P("mode", None, None, None),
        P(("tile", "tm"), None, None),
        P(("tile", "tm"), None),
        P(("tile", "tm")),
        P(("tile", "tm")),
        P(("tile", "tm")),
    )
    return jax.shard_map(
        body,
        mesh=mesh,
        in_specs=placed,
        out_specs=(P(None, "tile", "tm"), P("mode", None, None, None)),
        check_vma=False,
    )
```

```python
import functools

import jax
import jax.numpy as jnp
import ml_dtypes
import numpy as np
from jax import lax
from jax.experimental import pallas as pl
from jax.experimental.pallas import tpu as pltpu
from jax.sharding import PartitionSpec as P

PS = 256
HALF = 128
PARTS = 1
BH = 264
N_TM = 16
CH = 16
HALO = 24
FLOOR_VALUE = 0.5
OBJECT_REG = 1.0
PROBE_REG = 1.0
F32 = jnp.float32
BF16 = jnp.bfloat16
SWAP = [(0, 1), (1, 0)]

VM = pl.BlockSpec(memory_space=pltpu.VMEM)
SM = pl.BlockSpec(memory_space=pltpu.SMEM)


def real_form(matrix):
    return np.block([[matrix.real, -matrix.imag], [matrix.imag, matrix.real]]).astype(np.float32)


def halves(table):
    high = table.astype(ml_dtypes.bfloat16)
    return high, (table - high.astype(np.float32)).astype(ml_dtypes.bfloat16)


def dft_tables():
    n = np.arange(HALF)
    left, right = [], []
    for k in (2 * n, 2 * n + 1):
        table = real_form(np.exp(-2j * np.pi * ((k[:, None] * n[None, :]) % PS) / PS) / np.sqrt(PS))
        for form in (table, np.ascontiguousarray(table.T)):
            high, low = halves(form)
            left.append(np.concatenate([high, low][:PARTS], axis=1))
            right.append(np.concatenate([high, low][:PARTS], axis=0))
    return left + right


def order_table():
    picked = np.concatenate([np.arange(0, PS, 2), np.arange(1, PS, 2)])
    table = np.zeros((PS, PS), np.float32)
    table[np.arange(PS), picked] = 1.0
    return table.astype(ml_dtypes.bfloat16)


def call(kernel, out_shape, in_specs, scratch=(), flops=0, nbytes=1 << 20, vmem=12):
    many = isinstance(out_shape, (tuple, list))
    return pl.pallas_call(
        kernel,
        out_shape=out_shape,
        in_specs=in_specs,
        out_specs=[VM] * len(out_shape) if many else VM,
        scratch_shapes=list(scratch),
        compiler_params=pltpu.CompilerParams(vmem_limit_bytes=vmem << 20),
        cost_estimate=pl.CostEstimate(flops=flops, bytes_accessed=nbytes, transcendentals=0),
    )


def arr(shape, dtype):
    return jax.ShapeDtypeStruct(shape, dtype)


def lanes(rows):
    return lax.broadcasted_iota(jnp.int32, (rows, PS), 1)


def split(value):
    high = value.astype(BF16)
    return high, (value - high.astype(F32)).astype(BF16)


def dot(a, b):
    return lax.dot_general(a, b, (((1,), (0,)), ((), ())), preferred_element_type=F32)


def prep_kernel(anchors, row_offset, col_offset, live_counts, obj, high, low, field, ints, sems):
    copies = [pltpu.make_async_copy(obj.at[lax.axis_index("mode")], field, sems.at[0])]
    for k, ref in enumerate((anchors, col_offset, row_offset, live_counts)):
        copies.append(pltpu.make_async_copy(ref, ints[k], sems.at[k + 1]))
    for copy in copies:
        copy.start()
    for copy in copies[1:]:
        copy.wait()
    lane = lanes(8)
    meta = jnp.zeros((8, PS), F32)
    for p in range(2):
        alive = jnp.where(p < ints[3][0], 1, 0)
        for k, value in enumerate((ints[0][p], ints[1][p], ints[2][p], alive)):
            meta = jnp.where(lane == 4 * p + k, value.astype(F32), meta)
    copies[0].wait()
    for i in range(N_TM):
        chunk = field[CH * i : CH * i + HALO, :]
        rounded = chunk.astype(BF16).astype(F32)
        high[i] = jnp.concatenate([rounded, meta], axis=0).astype(BF16)
        low[i] = jnp.concatenate([chunk - rounded, jnp.zeros((8, PS), F32)], axis=0).astype(BF16)


def order_kernel(table, amp, out):
    def lines(value, product):
        high, low = split(value)
        return product(high) + product(low)

    rows = lines(amp[lax.axis_index("mode")], lambda x: dot(table[...], x))
    out[...] = lines(rows, lambda x: lax.dot_general(x, table[...], (((1,), (1,)), ((), ())), preferred_element_type=F32))


def cut_windows(meta, load, out, denom):
    def visit(t, total):
        for p in range(2):
            at, col, row, alive = (meta[t, 4 * p + k] for k in range(4))
            both = jnp.where(lanes(HALO) >= col, load(at), load(at + 1))
            both = pltpu.roll(both, lax.rem(HALO - row, HALO), 0)[0:CH].astype(BF16)
            out[t, CH * p : CH * p + CH, :] = both
            both = pltpu.roll(both.astype(F32), lax.rem(PS - col, PS), 1)
            total = total + both * both * alive.astype(F32)
        return total

    denom[...] = lax.fori_loop(0, N_TM, visit, jnp.zeros((CH, PS), F32))


def window_kernel(meta, high, low, out, denom):
    def visit(t, carry):
        out[t, 32:64, :] = low[t]
        return carry

    lax.fori_loop(0, N_TM, visit, 0)
    cut_windows(meta, lambda at: high[at].astype(F32)[0:HALO], out, denom)


def shift_rows(block, row):
    return pltpu.roll(block, lax.rem(HALO + row, 32), 0)[0:HALO]


def weight_kernel(meta, power, out):
    out[...] = jnp.full_like(out, OBJECT_REG)
    first = pl.multiple_of(lax.axis_index("tm") * CH, CH)

    def visit(t, carry):
        block = power[pl.ds(first, 32), :]
        for p in range(2):
            at, col, row, alive = (meta[t, 4 * p + k] for k in range(4))
            mask = lanes(HALO) >= col
            cover = pltpu.roll(shift_rows(block, row), col, 1) * alive.astype(F32)
            out[at] += jnp.where(mask, cover, 0.0)
            out[at + 1] += jnp.where(mask, 0.0, cover)
        return carry

    lax.fori_loop(0, N_TM, visit, 0)

    def invert(t, carry):
        out[t] = 1.0 / out[t]
        return carry

    lax.fori_loop(0, N_TM, invert, 0)


def accumulate(meta, parts, num):
    num[...] = jnp.zeros_like(num)

    def visit(t, carry):
        both = parts[t, 64:112, :].astype(F32)
        for p in range(2):
            at, col = meta[t, 4 * p], meta[t, 4 * p + 1]
            mask = lanes(HALO) >= col
            piece = both[HALO * p : HALO * p + HALO]
            num[at] += jnp.where(mask, piece, 0.0)
            num[at + 1] += jnp.where(mask, 0.0, piece)
        return carry

    lax.fori_loop(0, N_TM, visit, 0)


def update_kernel(meta, parts, scale, high, low, out, denom, upd, fresh):
    accumulate(meta, parts, upd)

    def visit(t, carry):
        step = upd[t] * scale[t]
        upd[t] = step
        fresh[t] = (high[t].astype(F32)[0:HALO] + low[t, 32:64, :].astype(F32)[0:HALO]) + step
        return carry

    lax.fori_loop(0, N_TM, visit, 0)
    cut_windows(meta, lambda at: fresh[at], out, denom)


def last_update_kernel(meta, parts, scale, upd, out, num):
    accumulate(meta, parts, num)

    def visit(t, carry):
        total = upd[t] + num[t] * scale[t]
        out[t] = jnp.concatenate([total, jnp.zeros((8, PS), F32)], axis=0).astype(BF16)
        return carry

    lax.fori_loop(0, N_TM, visit, 0)


def probe_sum_kernel(parts, denom, out):
    total = lax.fori_loop(0, N_TM, lambda t, acc: acc + parts[t, 0:64, :].astype(F32), jnp.zeros((64, PS), F32))
    out[0:64, :] = total.astype(BF16)
    out[64:80, :] = denom[...]


def probe_update_kernel(own, one, two, three, objs, out):
    total = (own[...].astype(F32) + two[...].astype(F32)) + (one[...].astype(F32) + three[...].astype(F32))
    scale = 1.0 / (total[64:80] + PROBE_REG)
    step = (total[0:64] * jnp.concatenate([scale] * 4, axis=0)).astype(BF16)

    def visit(t, carry):
        out[t, 0:32, :] = objs[t]
        out[t, 32:96, :] = step
        return carry

    lax.fori_loop(0, N_TM, visit, 0)


def pack_kernel(keep, recv, denom, out, denom_out):
    first = lax.axis_index("mode") == 0

    def visit(t, carry):
        mine, theirs = keep[t].astype(F32), recv[t].astype(F32)
        out[t, 0:64, :] = (mine[0:64] + theirs[0:64]).astype(BF16)
        num_mine, num_theirs = mine[64 : 64 + HALO], theirs[64 : 64 + HALO]
        out[t, 64:112, :] = jnp.concatenate(
            [jnp.where(first, num_mine, num_theirs), jnp.where(first, num_theirs, num_mine)], axis=0
        ).astype(BF16)
        return carry

    lax.fori_loop(0, N_TM, visit, 0)
    theirs = [recv[t, 64:96, :].astype(F32)[HALO:32] for t in range(2)]
    denom_out[...] = (denom[...] + jnp.concatenate(theirs, axis=0)).astype(BF16)


def put_left(ref, row, cols, value):
    for k in range(PARTS):
        ref[pl.ds(pl.multiple_of(row + k * PS, CH), CH), cols] = value.astype(BF16)


def put_right(ref, rows, lane, value):
    for k in range(PARTS):
        ref[rows, lane + k * PS : lane + k * PS + HALF] = value.astype(BF16)


def position_kernel(
    with_update, meta,
    l_even, l_even_t, l_odd, l_odd_t, r_even, r_even_t, r_odd, r_odd_t, p_own, p_oth, h_own, h_oth, amp, denom,
    keep, send, power, obj, probe, x_even, x_odd, y_even, y_odd, half_even, half_odd, far_even, far_odd, shifted,
):
    core = lax.axis_index("mode")
    first = core == 0
    col, row, alive = (meta[lax.axis_index("tm"), 4 * core + k] for k in (1, 2, 3))
    alive = alive.astype(F32)
    back_col = lax.rem(PS - col, PS)

    def rows_of(i, base=0):
        return pl.ds(pl.multiple_of(i * CH + base, CH), CH)

    def mode_cols(m):
        return slice(m * PS, (m + 1) * PS)

    power[0:8, :] = jnp.zeros((8, PS), F32)
    power[264:272, :] = jnp.zeros((8, PS), F32)

    def stage(i, carry):
        rows = rows_of(i)
        mine = jnp.where(first, h_own[i, 0:CH, :].astype(F32), h_own[i, CH : 2 * CH, :].astype(F32))
        theirs = jnp.where(first, h_oth[i, 0:CH, :].astype(F32), h_oth[i, CH : 2 * CH, :].astype(F32))
        obj[0, rows, :] = pltpu.roll(jnp.where(first, mine, theirs), back_col, 1)
        obj[1, rows, :] = pltpu.roll(jnp.where(first, theirs, mine), back_col, 1)
        total = jnp.zeros((CH, PS), F32)
        for m in range(4):
            src, chunk = (p_own, h_own) if m < 2 else (p_oth, h_oth)
            for k in range(2):
                value = src[m % 2, k, rows, :]
                if with_update:
                    at = 32 + CH * (2 * (m % 2) + k)
                    value = value + chunk[i, at : at + CH, :].astype(F32)
                probe[m, k, rows, :] = value
                total = total + value * value
        power[pl.ds(pl.multiple_of(i * CH + 8, 8), CH), :] = total
        return carry

    lax.fori_loop(0, N_TM, stage, 0)

    def wave(m, rows):
        pr, pi = probe[m, 0, rows, :], probe[m, 1, rows, :]
        o_r, o_i = obj[0, rows, :], obj[1, rows, :]
        return pr * o_r - pi * o_i, pr * o_i + pi * o_r

    def forward_rows(i, carry):
        for m in range(4):
            upper, lower = wave(m, rows_of(i)), wave(m, rows_of(i, HALF))
            for k in range(2):
                a, b = upper[k], lower[k]
                put_left(x_even, i * CH + k * HALF, mode_cols(m), a + b)
                put_left(x_odd, i * CH + k * HALF, mode_cols(m), a - b)
        return carry

    lax.fori_loop(0, HALF // CH, forward_rows, 0)
    half_even[...] = dot(l_even[...], x_even[...])
    half_odd[...] = dot(l_odd[...], x_odd[...])

    def forward_cols(i, carry):
        for m in range(4):
            for b, half in enumerate((half_even, half_odd)):
                for k in range(2):
                    value = half[rows_of(i, k * HALF), mode_cols(m)]
                    rows = rows_of(i, m * PS + b * HALF)
                    put_right(y_even, rows, k * HALF, value[:, 0:HALF] + value[:, HALF:PS])
                    put_right(y_odd, rows, k * HALF, value[:, 0:HALF] - value[:, HALF:PS])
        return carry

    lax.fori_loop(0, HALF // CH, forward_cols, 0)
    far_even[...] = dot(y_even[...], r_even_t[...])
    far_odd[...] = dot(y_odd[...], r_odd_t[...])

    def rescale(i, carry):
        for b, (far, y) in enumerate(((far_even, y_even), (far_odd, y_odd))):
            values = [far[rows_of(i, m * PS), :] for m in range(4)]
            squares = [v[:, 0:HALF] * v[:, 0:HALF] + v[:, HALF:PS] * v[:, HALF:PS] for v in values]
            total = (squares[0] + squares[1]).astype(BF16).astype(F32) + (squares[2] + squares[3]).astype(
                BF16
            ).astype(F32)
            factor = amp[rows_of(i), b * HALF : (b + 1) * HALF] * lax.rsqrt(jnp.maximum(total, FLOOR_VALUE)) - 1.0
            for m in range(4):
                for k in range(2):
                    put_right(y, rows_of(i, m * PS), k * HALF, values[m][:, k * HALF : (k + 1) * HALF] * factor)
        return carry

    lax.fori_loop(0, N_TM, rescale, 0)
    far_even[...] = dot(y_even[...], r_even[...])
    far_odd[...] = dot(y_odd[...], r_odd[...])

    def backward_cols(i, carry):
        for m in range(4):
            for b, x in enumerate((x_even, x_odd)):
                rows = rows_of(i, m * PS + b * HALF)
                even, odd = far_even[rows, :], far_odd[rows, :]
                total, diff = even + odd, even - odd
                for k in range(2):
                    part = slice(k * HALF, (k + 1) * HALF)
                    put_left(x, i * CH + k * HALF, slice(m * PS, m * PS + HALF), total[:, part])
                    put_left(x, i * CH + k * HALF, slice(m * PS + HALF, (m + 1) * PS), diff[:, part])
        return carry

    lax.fori_loop(0, HALF // CH, backward_cols, 0)
    half_even[...] = dot(l_even_t[...], x_even[...])
    half_odd[...] = dot(l_odd_t[...], x_odd[...])

    def outputs(i, carry):
        for s in range(2):
            rows = rows_of(i, s * HALF)
            n_re, n_im = jnp.zeros((CH, PS), F32), jnp.zeros((CH, PS), F32)
            for g, target in enumerate((keep, send)):
                g_re, g_im = jnp.zeros((CH, PS), F32), jnp.zeros((CH, PS), F32)
                for mm in range(2):
                    m = 2 * g + mm
                    pr, pi, o_r, o_i = probe[m, 0, rows, :], probe[m, 1, rows, :], obj[0, rows, :], obj[1, rows, :]
                    res = []
                    for k in range(2):
                        at = rows_of(i, k * HALF)
                        even, odd = half_even[at, mode_cols(m)], half_odd[at, mode_cols(m)]
                        res.append(even + odd if s == 0 else even - odd)
                    dr, di = res[0] * alive, res[1] * alive
                    chunk = i + s * (HALF // CH)
                    target[chunk, 2 * mm * CH : (2 * mm + 1) * CH, :] = (o_r * dr + o_i * di).astype(BF16)
                    target[chunk, (2 * mm + 1) * CH : (2 * mm + 2) * CH, :] = (o_r * di - o_i * dr).astype(BF16)
                    g_re = g_re + (pr * dr + pi * di)
                    g_im = g_im + (pr * di - pi * dr)
                n_re = n_re + g_re.astype(BF16).astype(F32)
                n_im = n_im + g_im.astype(BF16).astype(F32)
            at = pl.ds(pl.multiple_of(i * CH + s * HALF + 8, 8), CH)
            shifted[0, at, :] = pltpu.roll(n_re, col, 1)
            shifted[1, at, :] = pltpu.roll(n_im, col, 1)
        return carry

    shifted[:, 0:8, :] = jnp.zeros((2, 8, PS), F32)
    shifted[:, 264:272, :] = jnp.zeros((2, 8, PS), F32)
    lax.fori_loop(0, HALF // CH, outputs, 0)

    def emit(i, carry):
        rows = pl.ds(pl.multiple_of(i * CH, CH), 32)
        pad = jnp.where(i == 0, denom[0:8, :], jnp.where(i == 1, denom[8:16, :], 0.0))
        re, im = (
            jnp.concatenate([shift_rows(shifted[k, rows, :], row), pad], axis=0) for k in range(2)
        )
        keep[i, 64:96, :] = jnp.where(first, re, im).astype(BF16)
        send[i, 64:96, :] = jnp.where(first, im, re).astype(BF16)
        return carry

    lax.fori_loop(0, N_TM, emit, 0)


def final_probe_kernel(p_own, h_one, h_two, out):
    def visit(i, carry):
        rows = pl.ds(pl.multiple_of(i * CH, CH), CH)
        for m in range(2):
            for k in range(2):
                at = 32 + CH * (2 * m + k)
                before = p_own[m, k, rows, :] + h_one[i, at : at + CH, :].astype(F32)
                out[m, k, rows, :] = before + h_two[i, at : at + CH, :].astype(F32)
        return carry

    lax.fori_loop(0, N_TM, visit, 0)


def final_object_kernel(obj, h_own, h_oth, out):
    core = lax.axis_index("mode")

    def visit(i, carry):
        rows = pl.ds(pl.multiple_of(i * CH, CH), CH)
        out[core, rows, :] = obj[core, rows, :] + h_own[i, 0:CH, :].astype(F32)
        out[1 - core, rows, :] = obj[1 - core, rows, :] + h_oth[i, 0:CH, :].astype(F32)
        return carry

    lax.fori_loop(0, N_TM, visit, 0)
    last = N_TM - 1
    out[core, 256:264, :] = obj[core, 256:264, :] + h_own[last, 16:32, :].astype(F32)[0:8]
    out[1 - core, 256:264, :] = obj[1 - core, 256:264, :] + h_oth[last, 16:32, :].astype(F32)[0:8]


def body(object_field, probe_modes, amplitudes, anchors, row_offset, col_offset, live_counts):
    tables = [jnp.asarray(t) for t in dft_tables()]

    def exchange(x):
        return lax.all_to_all(x, "tm", 0, 0)

    def swap(x):
        return lax.ppermute(x, "mode", SWAP)

    def over_tiles(x):
        n = lax.axis_size("tile")
        return [lax.ppermute(x, "tile", [(i, (i + k) % n) for i in range(n)]) for k in (1, 2, 3)]

    slot = arr((N_TM, 32, PS), BF16)
    denom_shape = arr((CH, PS), F32)
    chunk = (N_TM, HALO, PS)
    high, low = call(
        prep_kernel,
        (slot, slot),
        [pl.BlockSpec(memory_space=pltpu.HBM)] * 5,
        scratch=[
            pltpu.VMEM((BH, PS), F32),
            [pltpu.SMEM((n,), jnp.int32) for n in (2, 2, 2, 1)],
            pltpu.SemaphoreType.DMA((5,)),
        ],
    )(anchors.reshape(-1), row_offset, col_offset, live_counts, object_field)
    probe_other = swap(probe_modes)
    high = exchange(high)
    amp = call(order_kernel, arr((PS, PS), F32), [VM, VM])(jnp.asarray(order_table()), amplitudes)
    meta = high[:, HALO, 0:8].astype(jnp.int32)
    windows, denom = call(window_kernel, (arr((N_TM, 64, PS), BF16), denom_shape), [SM, VM, VM])(meta, high, low)
    h_own = exchange(windows)
    low = h_own

    for iteration in range(2):
        h_oth = swap(h_own)
        part = arr((N_TM, 96, PS), BF16)
        left, right = pltpu.VMEM((PARTS * PS, 4 * PS), BF16), pltpu.VMEM((4 * PS, PARTS * PS), BF16)
        keep, send, power = call(
            functools.partial(position_kernel, iteration > 0),
            (part, part, arr((272, PS), F32)),
            [SM] + [VM] * 14,
            scratch=[
                pltpu.VMEM((2, PS, PS), F32),
                pltpu.VMEM((4, 2, PS, PS), F32),
                left,
                left,
                right,
                right,
                pltpu.VMEM((PS, 4 * PS), F32),
                pltpu.VMEM((PS, 4 * PS), F32),
                pltpu.VMEM((4 * PS, PS), F32),
                pltpu.VMEM((4 * PS, PS), F32),
                pltpu.VMEM((2, 272, PS), F32),
            ],
            flops=32 * PARTS * 2 * 256 * 256 * 256,
            nbytes=10 << 20,
            vmem=24,
        )(meta, *tables, probe_modes, probe_other, h_own, h_oth, amp, denom)
        recv = swap(send)
        scale = call(weight_kernel, arr(chunk, F32), [SM, VM])(meta, power)
        recv, scale = lax.optimization_barrier((recv, scale))
        parts, denom = call(pack_kernel, (arr((N_TM, 112, PS), BF16), arr((CH, PS), BF16)), [VM] * 3)(
            keep, recv, denom
        )
        parts = exchange(parts)
        probe_part = call(probe_sum_kernel, arr((80, PS), BF16), [VM] * 2)(parts, denom)
        others = over_tiles(probe_part)
        if iteration == 0:
            objs, denom, upd = call(
                update_kernel,
                (slot, denom_shape, arr(chunk, F32)),
                [SM] + [VM] * 4,
                scratch=[pltpu.VMEM(chunk, F32)],
            )(meta, parts, scale, high, low)
        else:
            objs = call(last_update_kernel, slot, [SM] + [VM] * 3, scratch=[pltpu.VMEM(chunk, F32)])(
                meta, parts, scale, upd
            )
        h_first = h_own
        h_own = exchange(
            call(probe_update_kernel, arr((N_TM, 96, PS), BF16), [VM] * 5)(probe_part, *others, objs)
        )

    h_oth = swap(h_own)
    probe_out = call(final_probe_kernel, arr((2, 2, PS, PS), F32), [VM] * 3)(probe_modes, h_first, h_own)
    object_out = call(final_object_kernel, arr((2, BH, PS), F32), [VM] * 3)(object_field, h_own, h_oth)
    return (object_out, probe_out)


def solution(mesh):
    placed = (
        P(None, "tile", "tm"),
        P("mode", None, None, None),
        P(("tile", "tm"), None, None),
        P(("tile", "tm"), None),
        P(("tile", "tm")),
        P(("tile", "tm")),
        P(("tile", "tm")),
    )
    return jax.shard_map(
        body,
        mesh=mesh,
        in_specs=placed,
        out_specs=(P(None, "tile", "tm"), P("mode", None, None, None)),
        check_vma=False,
    )
```

```python
import functools

import jax
import jax.numpy as jnp
import ml_dtypes
import numpy as np
from jax import lax
from jax.experimental import pallas as pl
from jax.experimental.pallas import tpu as pltpu
from jax.sharding import PartitionSpec as P

PS = 256
HALF = 128
PARTS = 1
BH = 264
N_TM = 16
UNROLL = 8
CH = 16
HALO = 24
FLOOR_VALUE = 0.5
OBJECT_REG = 1.0
PROBE_REG = 1.0
F32 = jnp.float32
BF16 = jnp.bfloat16
SWAP = [(0, 1), (1, 0)]

VM = pl.BlockSpec(memory_space=pltpu.VMEM)
SM = pl.BlockSpec(memory_space=pltpu.SMEM)


def real_form(matrix):
    return np.block([[matrix.real, -matrix.imag], [matrix.imag, matrix.real]]).astype(np.float32)


def halves(table):
    high = table.astype(ml_dtypes.bfloat16)
    return high, (table - high.astype(np.float32)).astype(ml_dtypes.bfloat16)


def dft_tables():
    n = np.arange(HALF)
    left, right = [], []
    for k in (2 * n, 2 * n + 1):
        table = real_form(np.exp(-2j * np.pi * ((k[:, None] * n[None, :]) % PS) / PS) / np.sqrt(PS))
        for form in (table, np.ascontiguousarray(table.T)):
            high, low = halves(form)
            left.append(np.concatenate([high, low][:PARTS], axis=1))
            right.append(np.concatenate([high, low][:PARTS], axis=0))
    return left + right


def order_table():
    picked = np.concatenate([np.arange(0, PS, 2), np.arange(1, PS, 2)])
    table = np.zeros((PS, PS), np.float32)
    table[np.arange(PS), picked] = 1.0
    return table.astype(ml_dtypes.bfloat16)


def call(kernel, out_shape, in_specs, scratch=(), flops=0, nbytes=1 << 20, vmem=12):
    many = isinstance(out_shape, (tuple, list))
    return pl.pallas_call(
        kernel,
        out_shape=out_shape,
        in_specs=in_specs,
        out_specs=[VM] * len(out_shape) if many else VM,
        scratch_shapes=list(scratch),
        compiler_params=pltpu.CompilerParams(vmem_limit_bytes=vmem << 20),
        cost_estimate=pl.CostEstimate(flops=flops, bytes_accessed=nbytes, transcendentals=0),
    )


def arr(shape, dtype):
    return jax.ShapeDtypeStruct(shape, dtype)


def lanes(rows):
    return lax.broadcasted_iota(jnp.int32, (rows, PS), 1)


def split(value):
    high = value.astype(BF16)
    return high, (value - high.astype(F32)).astype(BF16)


def dot(a, b):
    return lax.dot_general(a, b, (((1,), (0,)), ((), ())), preferred_element_type=F32)


def prep_kernel(anchors, row_offset, col_offset, live_counts, obj, high, field, ints, sems):
    copies = [pltpu.make_async_copy(obj.at[lax.axis_index("mode")], field, sems.at[0])]
    for k, ref in enumerate((anchors, col_offset, row_offset, live_counts)):
        copies.append(pltpu.make_async_copy(ref, ints[k], sems.at[k + 1]))
    for copy in copies:
        copy.start()
    for copy in copies[1:]:
        copy.wait()
    lane = lanes(8)
    meta = jnp.zeros((8, PS), F32)
    for p in range(2):
        alive = jnp.where(p < ints[3][0], 1, 0)
        for k, value in enumerate((ints[0][p], ints[1][p], ints[2][p], alive)):
            meta = jnp.where(lane == 4 * p + k, value.astype(F32), meta)
    copies[0].wait()
    for i in range(N_TM):
        chunk = field[CH * i : CH * i + HALO, :]
        high[i] = jnp.concatenate([chunk, meta], axis=0).astype(BF16)


def order_kernel(table, amp, out):
    def lines(value, product):
        high, low = split(value)
        return product(high) + product(low)

    rows = lines(amp[lax.axis_index("mode")], lambda x: dot(table[...], x))
    out[...] = lines(rows, lambda x: lax.dot_general(x, table[...], (((1,), (1,)), ((), ())), preferred_element_type=F32))


def cut_windows(meta, load, store, denom):
    def visit(t, total):
        for p in range(2):
            at, col, row, alive = (meta[t, 4 * p + k] for k in range(4))
            both = jnp.where(lanes(HALO) >= col, load(at), load(at + 1))
            both = pltpu.roll(both, lax.rem(HALO - row, HALO), 0)[0:CH].astype(BF16)
            store(t, p, both)
            both = pltpu.roll(both.astype(F32), lax.rem(PS - col, PS), 1)
            total = total + both * both * alive.astype(F32)
        return total

    denom[...] = lax.fori_loop(0, N_TM, visit, jnp.zeros((CH, PS), F32), unroll=4)


def window_kernel(meta, high, out, denom):
    def store(t, p, piece):
        out[2 * t + p] = piece

    cut_windows(meta, lambda at: high[at].astype(F32)[0:HALO], store, denom)


def shift_rows(block, row):
    return pltpu.roll(block, lax.rem(HALO + row, 32), 0)[0:HALO]


def weight_kernel(meta, power, out):
    out[...] = jnp.full_like(out, OBJECT_REG)
    first = pl.multiple_of(lax.axis_index("tm") * CH, CH)

    def visit(t, carry):
        block = power[pl.ds(first, 32), :]
        for p in range(2):
            at, col, row, alive = (meta[t, 4 * p + k] for k in range(4))
            mask = lanes(HALO) >= col
            cover = pltpu.roll(shift_rows(block, row), col, 1) * alive.astype(F32)
            out[at] += jnp.where(mask, cover, 0.0)
            out[at + 1] += jnp.where(mask, 0.0, cover)
        return carry

    lax.fori_loop(0, N_TM, visit, 0, unroll=UNROLL)

    def invert(t, carry):
        out[t] = 1.0 / out[t]
        return carry

    lax.fori_loop(0, N_TM, invert, 0, unroll=UNROLL)


def accumulate(meta, parts, num):
    num[...] = jnp.zeros_like(num)

    def visit(t, carry):
        both = parts[t, 64:112, :].astype(F32)
        for p in range(2):
            at, col = meta[t, 4 * p], meta[t, 4 * p + 1]
            mask = lanes(HALO) >= col
            piece = both[HALO * p : HALO * p + HALO]
            num[at] += jnp.where(mask, piece, 0.0)
            num[at + 1] += jnp.where(mask, 0.0, piece)
        return carry

    lax.fori_loop(0, N_TM, visit, 0, unroll=UNROLL)


def update_kernel(meta, parts, scale, high, out, denom, upd, fresh):
    accumulate(meta, parts, upd)

    def visit(t, carry):
        step = upd[t] * scale[t]
        upd[t] = step
        fresh[t] = high[t].astype(F32)[0:HALO] + step
        return carry

    lax.fori_loop(0, N_TM, visit, 0, unroll=UNROLL)

    def store(t, p, piece):
        out[t, CH * p : CH * p + CH, :] = piece

    cut_windows(meta, lambda at: fresh[at], store, denom)


def last_update_kernel(meta, parts, scale, upd, out, num):
    accumulate(meta, parts, num)

    def visit(t, carry):
        total = upd[t] + num[t] * scale[t]
        out[t] = jnp.concatenate([total, jnp.zeros((8, PS), F32)], axis=0).astype(BF16)
        return carry

    lax.fori_loop(0, N_TM, visit, 0, unroll=UNROLL)


def probe_sum_kernel(parts, denom, out):
    total = lax.fori_loop(0, N_TM, lambda t, acc: acc + parts[t, 0:64, :].astype(F32), jnp.zeros((64, PS), F32))
    out[0:64, :] = total.astype(BF16)
    out[64:80, :] = denom[...]


def probe_update_kernel(own, one, two, three, objs, out):
    total = (own[...].astype(F32) + two[...].astype(F32)) + (one[...].astype(F32) + three[...].astype(F32))
    scale = 1.0 / (total[64:80] + PROBE_REG)
    step = (total[0:64] * jnp.concatenate([scale] * 4, axis=0)).astype(BF16)

    def visit(t, carry):
        out[t, 0:32, :] = objs[t]
        out[t, 32:96, :] = step
        return carry

    lax.fori_loop(0, N_TM, visit, 0, unroll=UNROLL)


def pack_kernel(keep, recv, denom, out, denom_out):
    first = lax.axis_index("mode") == 0

    def visit(t, carry):
        mine, theirs = keep[t].astype(F32), recv[t].astype(F32)
        out[t, 0:64, :] = (mine[0:64] + theirs[0:64]).astype(BF16)
        num_mine, num_theirs = mine[64 : 64 + HALO], theirs[64 : 64 + HALO]
        out[t, 64:112, :] = jnp.concatenate(
            [jnp.where(first, num_mine, num_theirs), jnp.where(first, num_theirs, num_mine)], axis=0
        ).astype(BF16)
        return carry

    lax.fori_loop(0, N_TM, visit, 0, unroll=UNROLL)
    theirs = [recv[t, 64:96, :].astype(F32)[HALO:32] for t in range(2)]
    denom_out[...] = (denom[...] + jnp.concatenate(theirs, axis=0)).astype(BF16)


def put_left(ref, row, cols, value):
    for k in range(PARTS):
        ref[pl.ds(pl.multiple_of(row + k * PS, CH), CH), cols] = value.astype(BF16)


def put_right(ref, rows, lane, value):
    for k in range(PARTS):
        ref[rows, lane + k * PS : lane + k * PS + HALF] = value.astype(BF16)


def position_kernel(
    with_update, meta,
    l_even, l_even_t, l_odd, l_odd_t, r_even, r_even_t, r_odd, r_odd_t, p_own, p_oth, h_own, h_oth, amp, denom,
    keep, send, power, obj, probe, x_even, x_odd, y_even, y_odd, half_even, half_odd, far_even, far_odd, shifted,
):
    core = lax.axis_index("mode")
    first = core == 0
    col, row, alive = (meta[lax.axis_index("tm"), 4 * core + k] for k in (1, 2, 3))
    alive = alive.astype(F32)
    back_col = lax.rem(PS - col, PS)

    def rows_of(i, base=0):
        return pl.ds(pl.multiple_of(i * CH + base, CH), CH)

    def mode_cols(m):
        return slice(m * PS, (m + 1) * PS)

    power[0:8, :] = jnp.zeros((8, PS), F32)
    power[264:272, :] = jnp.zeros((8, PS), F32)

    def stage(i, carry):
        rows = rows_of(i)
        if with_update:
            mine = jnp.where(first, h_own[i, 0:CH, :].astype(F32), h_own[i, CH : 2 * CH, :].astype(F32))
            theirs = jnp.where(first, h_oth[i, 0:CH, :].astype(F32), h_oth[i, CH : 2 * CH, :].astype(F32))
            window = (jnp.where(first, mine, theirs), jnp.where(first, theirs, mine))
        else:
            window = [h_own[2 * i + k].astype(F32) for k in range(2)]
        for k in range(2):
            obj[k, rows, :] = pltpu.roll(window[k], back_col, 1)
        total = jnp.zeros((CH, PS), F32)
        for m in range(4):
            src, chunk = (p_own, h_own) if m < 2 else (p_oth, h_oth)
            for k in range(2):
                value = src[m % 2, k, rows, :]
                if with_update:
                    at = 32 + CH * (2 * (m % 2) + k)
                    value = value + chunk[i, at : at + CH, :].astype(F32)
                probe[m, k, rows, :] = value
                total = total + value * value
        power[pl.ds(pl.multiple_of(i * CH + 8, 8), CH), :] = total
        return carry

    lax.fori_loop(0, N_TM, stage, 0, unroll=UNROLL)

    def wave(m, rows):
        pr, pi = probe[m, 0, rows, :], probe[m, 1, rows, :]
        o_r, o_i = obj[0, rows, :], obj[1, rows, :]
        return pr * o_r - pi * o_i, pr * o_i + pi * o_r

    def forward_rows(i, carry):
        for m in range(4):
            upper, lower = wave(m, rows_of(i)), wave(m, rows_of(i, HALF))
            for k in range(2):
                a, b = upper[k], lower[k]
                put_left(x_even, i * CH + k * HALF, mode_cols(m), a + b)
                put_left(x_odd, i * CH + k * HALF, mode_cols(m), a - b)
        return carry

    lax.fori_loop(0, HALF // CH, forward_rows, 0, unroll=UNROLL)
    half_even[...] = dot(l_even[...], x_even[...])
    half_odd[...] = dot(l_odd[...], x_odd[...])

    def forward_cols(i, carry):
        for m in range(4):
            for b, half in enumerate((half_even, half_odd)):
                for k in range(2):
                    value = half[rows_of(i, k * HALF), mode_cols(m)]
                    rows = rows_of(i, m * PS + b * HALF)
                    put_right(y_even, rows, k * HALF, value[:, 0:HALF] + value[:, HALF:PS])
                    put_right(y_odd, rows, k * HALF, value[:, 0:HALF] - value[:, HALF:PS])
        return carry

    lax.fori_loop(0, HALF // CH, forward_cols, 0, unroll=UNROLL)
    far_even[...] = dot(y_even[...], r_even_t[...])
    far_odd[...] = dot(y_odd[...], r_odd_t[...])

    def rescale(i, carry):
        for b, (far, y) in enumerate(((far_even, y_even), (far_odd, y_odd))):
            values = [far[rows_of(i, m * PS), :] for m in range(4)]
            squares = [v[:, 0:HALF] * v[:, 0:HALF] + v[:, HALF:PS] * v[:, HALF:PS] for v in values]
            total = (squares[0] + squares[1]).astype(BF16).astype(F32) + (squares[2] + squares[3]).astype(
                BF16
            ).astype(F32)
            factor = amp[rows_of(i), b * HALF : (b + 1) * HALF] * lax.rsqrt(jnp.maximum(total, FLOOR_VALUE)) - 1.0
            for m in range(4):
                for k in range(2):
                    put_right(y, rows_of(i, m * PS), k * HALF, values[m][:, k * HALF : (k + 1) * HALF] * factor)
        return carry

    lax.fori_loop(0, N_TM, rescale, 0, unroll=UNROLL)
    far_even[...] = dot(y_even[...], r_even[...])
    far_odd[...] = dot(y_odd[...], r_odd[...])

    def backward_cols(i, carry):
        for m in range(4):
            for b, x in enumerate((x_even, x_odd)):
                rows = rows_of(i, m * PS + b * HALF)
                even, odd = far_even[rows, :], far_odd[rows, :]
                total, diff = even + odd, even - odd
                for k in range(2):
                    part = slice(k * HALF, (k + 1) * HALF)
                    put_left(x, i * CH + k * HALF, slice(m * PS, m * PS + HALF), total[:, part])
                    put_left(x, i * CH + k * HALF, slice(m * PS + HALF, (m + 1) * PS), diff[:, part])
        return carry

    lax.fori_loop(0, HALF // CH, backward_cols, 0, unroll=UNROLL)
    half_even[...] = dot(l_even_t[...], x_even[...])
    half_odd[...] = dot(l_odd_t[...], x_odd[...])

    def outputs(i, carry):
        for s in range(2):
            rows = rows_of(i, s * HALF)
            n_re, n_im = jnp.zeros((CH, PS), F32), jnp.zeros((CH, PS), F32)
            for g, target in enumerate((keep, send)):
                g_re, g_im = jnp.zeros((CH, PS), F32), jnp.zeros((CH, PS), F32)
                for mm in range(2):
                    m = 2 * g + mm
                    pr, pi, o_r, o_i = probe[m, 0, rows, :], probe[m, 1, rows, :], obj[0, rows, :], obj[1, rows, :]
                    res = []
                    for k in range(2):
                        at = rows_of(i, k * HALF)
                        even, odd = half_even[at, mode_cols(m)], half_odd[at, mode_cols(m)]
                        res.append(even + odd if s == 0 else even - odd)
                    dr, di = res[0] * alive, res[1] * alive
                    chunk = i + s * (HALF // CH)
                    target[chunk, 2 * mm * CH : (2 * mm + 1) * CH, :] = (o_r * dr + o_i * di).astype(BF16)
                    target[chunk, (2 * mm + 1) * CH : (2 * mm + 2) * CH, :] = (o_r * di - o_i * dr).astype(BF16)
                    g_re = g_re + (pr * dr + pi * di)
                    g_im = g_im + (pr * di - pi * dr)
                n_re = n_re + g_re.astype(BF16).astype(F32)
                n_im = n_im + g_im.astype(BF16).astype(F32)
            at = pl.ds(pl.multiple_of(i * CH + s * HALF + 8, 8), CH)
            shifted[0, at, :] = pltpu.roll(n_re, col, 1)
            shifted[1, at, :] = pltpu.roll(n_im, col, 1)
        return carry

    shifted[:, 0:8, :] = jnp.zeros((2, 8, PS), F32)
    shifted[:, 264:272, :] = jnp.zeros((2, 8, PS), F32)
    lax.fori_loop(0, HALF // CH, outputs, 0, unroll=UNROLL)

    def emit(i, carry):
        rows = pl.ds(pl.multiple_of(i * CH, CH), 32)
        pad = jnp.where(i == 0, denom[0:8, :], jnp.where(i == 1, denom[8:16, :], 0.0))
        re, im = (
            jnp.concatenate([shift_rows(shifted[k, rows, :], row), pad], axis=0) for k in range(2)
        )
        keep[i, 64:96, :] = jnp.where(first, re, im).astype(BF16)
        send[i, 64:96, :] = jnp.where(first, im, re).astype(BF16)
        return carry

    lax.fori_loop(0, N_TM, emit, 0, unroll=UNROLL)


def position(with_update, *args):
    part = arr((N_TM, 96, PS), BF16)
    left, right = pltpu.VMEM((PARTS * PS, 4 * PS), BF16), pltpu.VMEM((4 * PS, PARTS * PS), BF16)
    return call(
        functools.partial(position_kernel, with_update),
        (part, part, arr((272, PS), F32)),
        [SM] + [VM] * 14,
        scratch=[
            pltpu.VMEM((2, PS, PS), F32),
            pltpu.VMEM((4, 2, PS, PS), F32),
            left,
            left,
            right,
            right,
            pltpu.VMEM((PS, 4 * PS), F32),
            pltpu.VMEM((PS, 4 * PS), F32),
            pltpu.VMEM((4 * PS, PS), F32),
            pltpu.VMEM((4 * PS, PS), F32),
            pltpu.VMEM((2, 272, PS), F32),
        ],
        flops=32 * PARTS * 2 * 256 * 256 * 256,
        nbytes=10 << 20,
        vmem=24,
    )(*args)


def final_probe_kernel(p_own, h_one, h_two, out):
    def visit(i, carry):
        rows = pl.ds(pl.multiple_of(i * CH, CH), CH)
        for m in range(2):
            for k in range(2):
                at = 32 + CH * (2 * m + k)
                before = p_own[m, k, rows, :] + h_one[i, at : at + CH, :].astype(F32)
                out[m, k, rows, :] = before + h_two[i, at : at + CH, :].astype(F32)
        return carry

    lax.fori_loop(0, N_TM, visit, 0, unroll=UNROLL)


def final_object_kernel(obj, h_own, h_oth, out):
    core = lax.axis_index("mode")

    def visit(i, carry):
        rows = pl.ds(pl.multiple_of(i * CH, CH), CH)
        out[core, rows, :] = obj[core, rows, :] + h_own[i, 0:CH, :].astype(F32)
        out[1 - core, rows, :] = obj[1 - core, rows, :] + h_oth[i, 0:CH, :].astype(F32)
        return carry

    lax.fori_loop(0, N_TM, visit, 0, unroll=UNROLL)
    last = N_TM - 1
    out[core, 256:264, :] = obj[core, 256:264, :] + h_own[last, 16:32, :].astype(F32)[0:8]
    out[1 - core, 256:264, :] = obj[1 - core, 256:264, :] + h_oth[last, 16:32, :].astype(F32)[0:8]


def body(object_field, probe_modes, amplitudes, anchors, row_offset, col_offset, live_counts):
    tables = [jnp.asarray(t) for t in dft_tables()]

    def exchange(x):
        return lax.all_to_all(x, "tm", 0, 0)

    def swap(x):
        return lax.ppermute(x, "mode", SWAP)

    def over_tiles(x):
        n = lax.axis_size("tile")
        return [lax.ppermute(x, "tile", [(i, (i + k) % n) for i in range(n)]) for k in (1, 2, 3)]

    slot = arr((N_TM, 32, PS), BF16)
    denom_shape = arr((CH, PS), F32)
    chunk = (N_TM, HALO, PS)
    high = call(
        prep_kernel,
        slot,
        [pl.BlockSpec(memory_space=pltpu.HBM)] * 5,
        scratch=[
            pltpu.VMEM((BH, PS), F32),
            [pltpu.SMEM((n,), jnp.int32) for n in (2, 2, 2, 1)],
            pltpu.SemaphoreType.DMA((5,)),
        ],
        vmem=60,
    )(anchors.reshape(-1), row_offset, col_offset, live_counts, object_field)
    probe_other = swap(probe_modes)
    high = exchange(high)
    amp = call(order_kernel, arr((PS, PS), F32), [VM, VM])(jnp.asarray(order_table()), amplitudes)
    high, amp = lax.optimization_barrier((high, amp))
    meta = high[:, HALO, 0:8].astype(jnp.int32)
    windows, denom = call(window_kernel, (arr((2 * N_TM, CH, PS), BF16), denom_shape), [SM, VM])(meta, high)
    h_own = h_oth = lax.all_to_all(windows, ("tm", "mode"), 0, 0)

    for iteration in range(2):
        if iteration > 0:
            h_oth = swap(h_own)
        keep, send, power = position(
            iteration > 0, meta, *tables, probe_modes, probe_other, h_own, h_oth, amp, denom
        )
        recv = swap(send)
        scale = call(weight_kernel, arr(chunk, F32), [SM, VM])(meta, power)
        recv, scale = lax.optimization_barrier((recv, scale))
        parts, denom = call(pack_kernel, (arr((N_TM, 112, PS), BF16), arr((CH, PS), BF16)), [VM] * 3)(
            keep, recv, denom
        )
        parts = exchange(parts)
        probe_part = call(probe_sum_kernel, arr((80, PS), BF16), [VM] * 2)(parts, denom)
        others = over_tiles(probe_part)
        if iteration == 0:
            objs, denom, upd = call(
                update_kernel,
                (slot, denom_shape, arr(chunk, F32)),
                [SM] + [VM] * 3,
                scratch=[pltpu.VMEM(chunk, F32)],
            )(meta, parts, scale, high)
        else:
            objs = call(last_update_kernel, slot, [SM] + [VM] * 3, scratch=[pltpu.VMEM(chunk, F32)])(
                meta, parts, scale, upd
            )
        h_first = h_own
        h_own = exchange(
            call(probe_update_kernel, arr((N_TM, 96, PS), BF16), [VM] * 5)(probe_part, *others, objs)
        )

    h_oth = swap(h_own)
    probe_out = call(final_probe_kernel, arr((2, 2, PS, PS), F32), [VM] * 3)(probe_modes, h_first, h_own)
    object_out = call(final_object_kernel, arr((2, BH, PS), F32), [VM] * 3)(object_field, h_own, h_oth)
    return (object_out, probe_out)


def solution(mesh):
    placed = (
        P(None, "tile", "tm"),
        P("mode", None, None, None),
        P(("tile", "tm"), None, None),
        P(("tile", "tm"), None),
        P(("tile", "tm")),
        P(("tile", "tm")),
        P(("tile", "tm")),
    )
    return jax.shard_map(
        body,
        mesh=mesh,
        in_specs=placed,
        out_specs=(P(None, "tile", "tm"), P("mode", None, None, None)),
        check_vma=False,
    )
```

```python
import functools

import jax
import jax.numpy as jnp
import ml_dtypes
import numpy as np
from jax import lax
from jax.experimental import pallas as pl
from jax.experimental.pallas import tpu as pltpu
from jax.sharding import PartitionSpec as P

PS = 256
HALF = 128
PARTS = 1
BH = 264
N_TM = 16
UNROLL = 16
CH = 16
HALO = 24
FLOOR_VALUE = 0.5
OBJECT_REG = 1.0
PROBE_REG = 1.0
F32 = jnp.float32
BF16 = jnp.bfloat16
SWAP = [(0, 1), (1, 0)]

VM = pl.BlockSpec(memory_space=pltpu.VMEM)
SM = pl.BlockSpec(memory_space=pltpu.SMEM)


def real_form(matrix):
    return np.block([[matrix.real, -matrix.imag], [matrix.imag, matrix.real]]).astype(np.float32)


def halves(table):
    high = table.astype(ml_dtypes.bfloat16)
    return high, (table - high.astype(np.float32)).astype(ml_dtypes.bfloat16)


def dft_tables():
    n = np.arange(HALF)
    left, right = [], []
    for k in (2 * n, 2 * n + 1):
        table = real_form(np.exp(-2j * np.pi * ((k[:, None] * n[None, :]) % PS) / PS) / np.sqrt(PS))
        for form in (table, np.ascontiguousarray(table.T)):
            high, low = halves(form)
            left.append(np.concatenate([high, low][:PARTS], axis=1))
            right.append(np.concatenate([high, low][:PARTS], axis=0))
    return left + right


def order_table():
    picked = np.concatenate([np.arange(0, PS, 2), np.arange(1, PS, 2)])
    table = np.zeros((PS, PS), np.float32)
    table[np.arange(PS), picked] = 1.0
    return table.astype(ml_dtypes.bfloat16)


def call(kernel, out_shape, in_specs, scratch=(), flops=0, nbytes=1 << 20, vmem=12):
    many = isinstance(out_shape, (tuple, list))
    return pl.pallas_call(
        kernel,
        out_shape=out_shape,
        in_specs=in_specs,
        out_specs=[VM] * len(out_shape) if many else VM,
        scratch_shapes=list(scratch),
        compiler_params=pltpu.CompilerParams(vmem_limit_bytes=vmem << 20),
        cost_estimate=pl.CostEstimate(flops=flops, bytes_accessed=nbytes, transcendentals=0),
    )


def arr(shape, dtype):
    return jax.ShapeDtypeStruct(shape, dtype)


def lanes(rows):
    return lax.broadcasted_iota(jnp.int32, (rows, PS), 1)


def split(value):
    high = value.astype(BF16)
    return high, (value - high.astype(F32)).astype(BF16)


def dot(a, b):
    return lax.dot_general(a, b, (((1,), (0,)), ((), ())), preferred_element_type=F32)


def prep_kernel(anchors, row_offset, col_offset, live_counts, obj, high, field, ints, sems):
    copies = [pltpu.make_async_copy(obj.at[lax.axis_index("mode")], field, sems.at[0])]
    for k, ref in enumerate((anchors, col_offset, row_offset, live_counts)):
        copies.append(pltpu.make_async_copy(ref, ints[k], sems.at[k + 1]))
    for copy in copies:
        copy.start()
    for copy in copies[1:]:
        copy.wait()
    lane = lanes(8)
    meta = jnp.zeros((8, PS), F32)
    for p in range(2):
        alive = jnp.where(p < ints[3][0, 0], 1, 0)
        for k, value in enumerate((ints[0][p], ints[1][p], ints[2][p], alive)):
            meta = jnp.where(lane == 4 * p + k, value.astype(F32), meta)
    copies[0].wait()
    for i in range(N_TM):
        chunk = field[CH * i : CH * i + HALO, :]
        high[i] = jnp.concatenate([chunk, meta], axis=0).astype(BF16)


def order_kernel(table, amp, out):
    def lines(value, product):
        high, low = split(value)
        return product(high) + product(low)

    rows = lines(amp[lax.axis_index("mode")], lambda x: dot(table[...], x))
    out[...] = lines(rows, lambda x: lax.dot_general(x, table[...], (((1,), (1,)), ((), ())), preferred_element_type=F32))


def cut_windows(meta, load, store, denom):
    def visit(t, total):
        for p in range(2):
            at, col, row, alive = (meta[t, 4 * p + k] for k in range(4))
            both = jnp.where(lanes(HALO) >= col, load(at), load(at + 1))
            both = pltpu.roll(both, lax.rem(HALO - row, HALO), 0)[0:CH].astype(BF16)
            store(t, p, both)
            both = pltpu.roll(both.astype(F32), lax.rem(PS - col, PS), 1)
            total = total + both * both * alive.astype(F32)
        return total

    denom[...] = lax.fori_loop(0, N_TM, visit, jnp.zeros((CH, PS), F32), unroll=4)


def window_kernel(meta, high, out, denom):
    def store(t, p, piece):
        out[2 * t + p] = piece

    cut_windows(meta, lambda at: high[at].astype(F32)[0:HALO], store, denom)


def shift_rows(block, row):
    return pltpu.roll(block, lax.rem(HALO + row, 32), 0)[0:HALO]


def weight_kernel(meta, power, out):
    out[...] = jnp.full_like(out, OBJECT_REG)
    first = pl.multiple_of(lax.axis_index("tm") * CH, CH)

    def visit(t, carry):
        block = power[pl.ds(first, 32), :]
        for p in range(2):
            at, col, row, alive = (meta[t, 4 * p + k] for k in range(4))
            mask = lanes(HALO) >= col
            cover = pltpu.roll(shift_rows(block, row), col, 1) * alive.astype(F32)
            out[at] += jnp.where(mask, cover, 0.0)
            out[at + 1] += jnp.where(mask, 0.0, cover)
        return carry

    lax.fori_loop(0, N_TM, visit, 0, unroll=UNROLL)

    def invert(t, carry):
        out[t] = 1.0 / out[t]
        return carry

    lax.fori_loop(0, N_TM, invert, 0, unroll=UNROLL)


def accumulate(meta, parts, num):
    num[...] = jnp.zeros_like(num)

    def visit(t, carry):
        both = parts[t, 64:112, :].astype(F32)
        for p in range(2):
            at, col = meta[t, 4 * p], meta[t, 4 * p + 1]
            mask = lanes(HALO) >= col
            piece = both[HALO * p : HALO * p + HALO]
            num[at] += jnp.where(mask, piece, 0.0)
            num[at + 1] += jnp.where(mask, 0.0, piece)
        return carry

    lax.fori_loop(0, N_TM, visit, 0, unroll=UNROLL)


def update_kernel(meta, parts, scale, high, out, denom, upd, fresh):
    accumulate(meta, parts, upd)

    def visit(t, carry):
        step = upd[t] * scale[t]
        upd[t] = step
        fresh[t] = high[t].astype(F32)[0:HALO] + step
        return carry

    lax.fori_loop(0, N_TM, visit, 0, unroll=UNROLL)

    def store(t, p, piece):
        out[t, CH * p : CH * p + CH, :] = piece

    cut_windows(meta, lambda at: fresh[at], store, denom)


def last_update_kernel(meta, parts, scale, upd, out, num):
    accumulate(meta, parts, num)

    def visit(t, carry):
        total = upd[t] + num[t] * scale[t]
        out[t] = jnp.concatenate([total, jnp.zeros((8, PS), F32)], axis=0).astype(BF16)
        return carry

    lax.fori_loop(0, N_TM, visit, 0, unroll=UNROLL)


def probe_sum_kernel(parts, denom, out):
    total = lax.fori_loop(0, N_TM, lambda t, acc: acc + parts[t, 0:64, :].astype(F32), jnp.zeros((64, PS), F32))
    out[0:64, :] = total.astype(BF16)
    out[64:80, :] = denom[...]


def probe_update_kernel(own, one, two, three, objs, out):
    total = (own[...].astype(F32) + two[...].astype(F32)) + (one[...].astype(F32) + three[...].astype(F32))
    scale = 1.0 / (total[64:80] + PROBE_REG)
    step = (total[0:64] * jnp.concatenate([scale] * 4, axis=0)).astype(BF16)

    def visit(t, carry):
        out[t, 0:32, :] = objs[t]
        out[t, 32:96, :] = step
        return carry

    lax.fori_loop(0, N_TM, visit, 0, unroll=UNROLL)


def pack_kernel(keep, recv, denom, out, denom_out):
    first = lax.axis_index("mode") == 0

    def visit(t, carry):
        mine, theirs = keep[t].astype(F32), recv[t].astype(F32)
        out[t, 0:64, :] = (mine[0:64] + theirs[0:64]).astype(BF16)
        num_mine, num_theirs = mine[64 : 64 + HALO], theirs[64 : 64 + HALO]
        out[t, 64:112, :] = jnp.concatenate(
            [jnp.where(first, num_mine, num_theirs), jnp.where(first, num_theirs, num_mine)], axis=0
        ).astype(BF16)
        return carry

    lax.fori_loop(0, N_TM, visit, 0, unroll=UNROLL)
    theirs = [recv[t, 64:96, :].astype(F32)[HALO:32] for t in range(2)]
    denom_out[...] = (denom[...] + jnp.concatenate(theirs, axis=0)).astype(BF16)


def put_left(ref, row, cols, value):
    for k in range(PARTS):
        ref[pl.ds(pl.multiple_of(row + k * PS, CH), CH), cols] = value.astype(BF16)


def put_right(ref, rows, lane, value):
    for k in range(PARTS):
        ref[rows, lane + k * PS : lane + k * PS + HALF] = value.astype(BF16)


def position_kernel(
    with_update, meta,
    l_even, l_even_t, l_odd, l_odd_t, r_even, r_even_t, r_odd, r_odd_t, p_own, p_oth, h_own, h_oth, amp, denom,
    keep, send, power, obj, probe, x_even, x_odd, y_even, y_odd, half_even, half_odd, far_even, far_odd, shifted,
):
    core = lax.axis_index("mode")
    first = core == 0
    col, row, alive = (meta[lax.axis_index("tm"), 4 * core + k] for k in (1, 2, 3))
    alive = alive.astype(F32)
    back_col = lax.rem(PS - col, PS)

    def rows_of(i, base=0):
        return pl.ds(pl.multiple_of(i * CH + base, CH), CH)

    def mode_cols(m):
        return slice(m * PS, (m + 1) * PS)

    power[0:8, :] = jnp.zeros((8, PS), F32)
    power[264:272, :] = jnp.zeros((8, PS), F32)

    def stage(i, carry):
        rows = rows_of(i)
        if with_update:
            mine = jnp.where(first, h_own[i, 0:CH, :].astype(F32), h_own[i, CH : 2 * CH, :].astype(F32))
            theirs = jnp.where(first, h_oth[i, 0:CH, :].astype(F32), h_oth[i, CH : 2 * CH, :].astype(F32))
            window = (jnp.where(first, mine, theirs), jnp.where(first, theirs, mine))
        else:
            window = [h_own[2 * i + k].astype(F32) for k in range(2)]
        for k in range(2):
            obj[k, rows, :] = pltpu.roll(window[k], back_col, 1)
        total = jnp.zeros((CH, PS), F32)
        for m in range(4):
            src, chunk = (p_own, h_own) if m < 2 else (p_oth, h_oth)
            for k in range(2):
                value = src[m % 2, k, rows, :]
                if with_update:
                    at = 32 + CH * (2 * (m % 2) + k)
                    value = value + chunk[i, at : at + CH, :].astype(F32)
                probe[m, k, rows, :] = value
                total = total + value * value
        power[pl.ds(pl.multiple_of(i * CH + 8, 8), CH), :] = total
        return carry

    lax.fori_loop(0, N_TM, stage, 0, unroll=UNROLL)

    def wave(m, rows):
        pr, pi = probe[m, 0, rows, :], probe[m, 1, rows, :]
        o_r, o_i = obj[0, rows, :], obj[1, rows, :]
        return pr * o_r - pi * o_i, pr * o_i + pi * o_r

    def forward_rows(i, carry):
        for m in range(4):
            upper, lower = wave(m, rows_of(i)), wave(m, rows_of(i, HALF))
            for k in range(2):
                a, b = upper[k], lower[k]
                put_left(x_even, i * CH + k * HALF, mode_cols(m), a + b)
                put_left(x_odd, i * CH + k * HALF, mode_cols(m), a - b)
        return carry

    lax.fori_loop(0, HALF // CH, forward_rows, 0, unroll=8)
    half_even[...] = dot(l_even[...], x_even[...])
    half_odd[...] = dot(l_odd[...], x_odd[...])

    def forward_cols(i, carry):
        for m in range(4):
            for b, half in enumerate((half_even, half_odd)):
                for k in range(2):
                    value = half[rows_of(i, k * HALF), mode_cols(m)]
                    rows = rows_of(i, m * PS + b * HALF)
                    put_right(y_even, rows, k * HALF, value[:, 0:HALF] + value[:, HALF:PS])
                    put_right(y_odd, rows, k * HALF, value[:, 0:HALF] - value[:, HALF:PS])
        return carry

    lax.fori_loop(0, HALF // CH, forward_cols, 0, unroll=8)
    far_even[...] = dot(y_even[...], r_even_t[...])
    far_odd[...] = dot(y_odd[...], r_odd_t[...])

    def rescale(i, carry):
        for b, (far, y) in enumerate(((far_even, y_even), (far_odd, y_odd))):
            values = [far[rows_of(i, m * PS), :] for m in range(4)]
            squares = [v[:, 0:HALF] * v[:, 0:HALF] + v[:, HALF:PS] * v[:, HALF:PS] for v in values]
            total = (squares[0] + squares[1]).astype(BF16).astype(F32) + (squares[2] + squares[3]).astype(
                BF16
            ).astype(F32)
            factor = amp[rows_of(i), b * HALF : (b + 1) * HALF] * lax.rsqrt(jnp.maximum(total, FLOOR_VALUE)) - 1.0
            for m in range(4):
                for k in range(2):
                    put_right(y, rows_of(i, m * PS), k * HALF, values[m][:, k * HALF : (k + 1) * HALF] * factor)
        return carry

    lax.fori_loop(0, N_TM, rescale, 0, unroll=UNROLL)
    far_even[...] = dot(y_even[...], r_even[...])
    far_odd[...] = dot(y_odd[...], r_odd[...])

    def backward_cols(i, carry):
        for m in range(4):
            for b, x in enumerate((x_even, x_odd)):
                rows = rows_of(i, m * PS + b * HALF)
                even, odd = far_even[rows, :], far_odd[rows, :]
                total, diff = even + odd, even - odd
                for k in range(2):
                    part = slice(k * HALF, (k + 1) * HALF)
                    put_left(x, i * CH + k * HALF, slice(m * PS, m * PS + HALF), total[:, part])
                    put_left(x, i * CH + k * HALF, slice(m * PS + HALF, (m + 1) * PS), diff[:, part])
        return carry

    lax.fori_loop(0, HALF // CH, backward_cols, 0, unroll=8)
    half_even[...] = dot(l_even_t[...], x_even[...])
    half_odd[...] = dot(l_odd_t[...], x_odd[...])

    def outputs(i, carry):
        for s in range(2):
            rows = rows_of(i, s * HALF)
            n_re, n_im = jnp.zeros((CH, PS), F32), jnp.zeros((CH, PS), F32)
            for g, target in enumerate((keep, send)):
                g_re, g_im = jnp.zeros((CH, PS), F32), jnp.zeros((CH, PS), F32)
                for mm in range(2):
                    m = 2 * g + mm
                    pr, pi, o_r, o_i = probe[m, 0, rows, :], probe[m, 1, rows, :], obj[0, rows, :], obj[1, rows, :]
                    res = []
                    for k in range(2):
                        at = rows_of(i, k * HALF)
                        even, odd = half_even[at, mode_cols(m)], half_odd[at, mode_cols(m)]
                        res.append(even + odd if s == 0 else even - odd)
                    dr, di = res[0] * alive, res[1] * alive
                    chunk = i + s * (HALF // CH)
                    target[chunk, 2 * mm * CH : (2 * mm + 1) * CH, :] = (o_r * dr + o_i * di).astype(BF16)
                    target[chunk, (2 * mm + 1) * CH : (2 * mm + 2) * CH, :] = (o_r * di - o_i * dr).astype(BF16)
                    g_re = g_re + (pr * dr + pi * di)
                    g_im = g_im + (pr * di - pi * dr)
                n_re = n_re + g_re.astype(BF16).astype(F32)
                n_im = n_im + g_im.astype(BF16).astype(F32)
            at = pl.ds(pl.multiple_of(i * CH + s * HALF + 8, 8), CH)
            shifted[0, at, :] = pltpu.roll(n_re, col, 1)
            shifted[1, at, :] = pltpu.roll(n_im, col, 1)
        return carry

    shifted[:, 0:8, :] = jnp.zeros((2, 8, PS), F32)
    shifted[:, 264:272, :] = jnp.zeros((2, 8, PS), F32)
    lax.fori_loop(0, HALF // CH, outputs, 0, unroll=8)

    def emit(i, carry):
        rows = pl.ds(pl.multiple_of(i * CH, CH), 32)
        pad = jnp.where(i == 0, denom[0:8, :], jnp.where(i == 1, denom[8:16, :], 0.0))
        re, im = (
            jnp.concatenate([shift_rows(shifted[k, rows, :], row), pad], axis=0) for k in range(2)
        )
        keep[i, 64:96, :] = jnp.where(first, re, im).astype(BF16)
        send[i, 64:96, :] = jnp.where(first, im, re).astype(BF16)
        return carry

    lax.fori_loop(0, N_TM, emit, 0, unroll=UNROLL)


def position(with_update, *args):
    part = arr((N_TM, 96, PS), BF16)
    left, right = pltpu.VMEM((PARTS * PS, 4 * PS), BF16), pltpu.VMEM((4 * PS, PARTS * PS), BF16)
    return call(
        functools.partial(position_kernel, with_update),
        (part, part, arr((272, PS), F32)),
        [SM] + [VM] * 14,
        scratch=[
            pltpu.VMEM((2, PS, PS), F32),
            pltpu.VMEM((4, 2, PS, PS), F32),
            left,
            left,
            right,
            right,
            pltpu.VMEM((PS, 4 * PS), F32),
            pltpu.VMEM((PS, 4 * PS), F32),
            pltpu.VMEM((4 * PS, PS), F32),
            pltpu.VMEM((4 * PS, PS), F32),
            pltpu.VMEM((2, 272, PS), F32),
        ],
        flops=32 * PARTS * 2 * 256 * 256 * 256,
        nbytes=10 << 20,
        vmem=24,
    )(*args)


def final_probe_kernel(p_own, h_one, h_two, out):
    def visit(i, carry):
        rows = pl.ds(pl.multiple_of(i * CH, CH), CH)
        for m in range(2):
            for k in range(2):
                at = 32 + CH * (2 * m + k)
                before = p_own[m, k, rows, :] + h_one[i, at : at + CH, :].astype(F32)
                out[m, k, rows, :] = before + h_two[i, at : at + CH, :].astype(F32)
        return carry

    lax.fori_loop(0, N_TM, visit, 0, unroll=UNROLL)


def final_object_kernel(obj, h_own, h_oth, out):
    core = lax.axis_index("mode")

    def visit(i, carry):
        rows = pl.ds(pl.multiple_of(i * CH, CH), CH)
        out[core, rows, :] = obj[core, rows, :] + h_own[i, 0:CH, :].astype(F32)
        out[1 - core, rows, :] = obj[1 - core, rows, :] + h_oth[i, 0:CH, :].astype(F32)
        return carry

    lax.fori_loop(0, N_TM, visit, 0, unroll=UNROLL)
    last = N_TM - 1
    out[core, 256:264, :] = obj[core, 256:264, :] + h_own[last, 16:32, :].astype(F32)[0:8]
    out[1 - core, 256:264, :] = obj[1 - core, 256:264, :] + h_oth[last, 16:32, :].astype(F32)[0:8]


def body(object_field, probe_modes, amplitudes, anchors, row_offset, col_offset, live_counts):
    tables = [jnp.asarray(t) for t in dft_tables()]

    def exchange(x):
        return lax.all_to_all(x, "tm", 0, 0)

    def swap(x):
        return lax.ppermute(x, "mode", SWAP)

    def over_tiles(x):
        n = lax.axis_size("tile")
        return [lax.ppermute(x, "tile", [(i, (i + k) % n) for i in range(n)]) for k in (1, 2, 3)]

    slot = arr((N_TM, 32, PS), BF16)
    denom_shape = arr((CH, PS), F32)
    chunk = (N_TM, HALO, PS)
    high = call(
        prep_kernel,
        slot,
        [pl.BlockSpec(memory_space=pltpu.HBM)] * 5,
        scratch=[
            pltpu.VMEM((BH, PS), F32),
            [pltpu.SMEM(shape, jnp.int32) for shape in ((2,), (2,), (2,), (1, 1))],
            pltpu.SemaphoreType.DMA((5,)),
        ],
        vmem=60,
    )(anchors.reshape(-1), row_offset, col_offset, live_counts.reshape(1, 1), object_field)
    high = exchange(high)
    amp = call(order_kernel, arr((PS, PS), F32), [VM, VM])(jnp.asarray(order_table()), amplitudes)
    high, amp = lax.optimization_barrier((high, amp))
    meta = high[:, HALO, 0:8].astype(jnp.int32)
    windows, denom = call(window_kernel, (arr((2 * N_TM, CH, PS), BF16), denom_shape), [SM, VM])(meta, high)
    windows, own = lax.optimization_barrier((windows, probe_modes))
    probe_other = swap(own)
    h_own = h_oth = lax.all_to_all(windows, ("tm", "mode"), 0, 0)

    for iteration in range(2):
        if iteration > 0:
            h_oth = swap(h_own)
        keep, send, power = position(
            iteration > 0, meta, *tables, probe_modes, probe_other, h_own, h_oth, amp, denom
        )
        recv = swap(send)
        scale = call(weight_kernel, arr(chunk, F32), [SM, VM])(meta, power)
        recv, scale = lax.optimization_barrier((recv, scale))
        parts, denom = call(pack_kernel, (arr((N_TM, 112, PS), BF16), arr((CH, PS), BF16)), [VM] * 3)(
            keep, recv, denom
        )
        parts = exchange(parts)
        probe_part = call(probe_sum_kernel, arr((80, PS), BF16), [VM] * 2)(parts, denom)
        others = over_tiles(probe_part)
        if iteration == 0:
            objs, denom, upd = call(
                update_kernel,
                (slot, denom_shape, arr(chunk, F32)),
                [SM] + [VM] * 3,
                scratch=[pltpu.VMEM(chunk, F32)],
            )(meta, parts, scale, high)
        else:
            objs = call(last_update_kernel, slot, [SM] + [VM] * 3, scratch=[pltpu.VMEM(chunk, F32)])(
                meta, parts, scale, upd
            )
        h_first = h_own
        h_own = exchange(
            call(probe_update_kernel, arr((N_TM, 96, PS), BF16), [VM] * 5)(probe_part, *others, objs)
        )

    h_oth = swap(h_own)
    probe_out = call(final_probe_kernel, arr((2, 2, PS, PS), F32), [VM] * 3)(probe_modes, h_first, h_own)
    object_out = call(final_object_kernel, arr((2, BH, PS), F32), [VM] * 3)(object_field, h_own, h_oth)
    return (object_out, probe_out)


def solution(mesh):
    placed = (
        P(None, "tile", "tm"),
        P("mode", None, None, None),
        P(("tile", "tm"), None, None),
        P(("tile", "tm"), None),
        P(("tile", "tm")),
        P(("tile", "tm")),
        P(("tile", "tm")),
    )
    return jax.shard_map(
        body,
        mesh=mesh,
        in_specs=placed,
        out_specs=(P(None, "tile", "tm"), P("mode", None, None, None)),
        check_vma=False,
    )
```

```python
import functools

import jax
import jax.numpy as jnp
import ml_dtypes
import numpy as np
from jax import lax
from jax.experimental import pallas as pl
from jax.experimental.pallas import tpu as pltpu
from jax.sharding import PartitionSpec as P

PS = 256
HALF = 128
PARTS = 3
BH = 264
N_TM = 16
UNROLL = 16
CH = 16
HALO = 24
FLOOR_VALUE = 0.5
OBJECT_REG = 1.0
PROBE_REG = 1.0
F32 = jnp.float32
BF16 = jnp.bfloat16
SWAP = [(0, 1), (1, 0)]

VM = pl.BlockSpec(memory_space=pltpu.VMEM)
SM = pl.BlockSpec(memory_space=pltpu.SMEM)


def real_form(matrix):
    return np.block([[matrix.real, -matrix.imag], [matrix.imag, matrix.real]]).astype(np.float32)


def halves(table):
    high = table.astype(ml_dtypes.bfloat16)
    return high, (table - high.astype(np.float32)).astype(ml_dtypes.bfloat16)


def dft_tables():
    n = np.arange(HALF)
    parts = []
    for k in (2 * n, 2 * n + 1):
        table = real_form(np.exp(-2j * np.pi * ((k[:, None] * n[None, :]) % PS) / PS) / np.sqrt(PS))
        parts += [halves(table), halves(table.T)]
    return np.stack([np.stack([p[k] for p in parts]) for k in range(min(PARTS, 2))])


def order_table():
    picked = np.concatenate([np.arange(0, PS, 2), np.arange(1, PS, 2)])
    table = np.zeros((PS, PS), np.float32)
    table[np.arange(PS), picked] = 1.0
    return table.astype(ml_dtypes.bfloat16)


def call(kernel, out_shape, in_specs, scratch=(), flops=0, nbytes=1 << 20, vmem=12):
    many = isinstance(out_shape, (tuple, list))
    return pl.pallas_call(
        kernel,
        out_shape=out_shape,
        in_specs=in_specs,
        out_specs=[VM] * len(out_shape) if many else VM,
        scratch_shapes=list(scratch),
        compiler_params=pltpu.CompilerParams(vmem_limit_bytes=vmem << 20),
        cost_estimate=pl.CostEstimate(flops=flops, bytes_accessed=nbytes, transcendentals=0),
    )


def arr(shape, dtype):
    return jax.ShapeDtypeStruct(shape, dtype)


def lanes(rows):
    return lax.broadcasted_iota(jnp.int32, (rows, PS), 1)


def split(value):
    high = value.astype(BF16)
    return high, (value - high.astype(F32)).astype(BF16)


def dot(a, b):
    return lax.dot_general(a, b, (((1,), (0,)), ((), ())), preferred_element_type=F32)


def prep_kernel(anchors, row_offset, col_offset, live_counts, obj, high, field, ints, sems):
    copies = [pltpu.make_async_copy(obj.at[lax.axis_index("mode")], field, sems.at[0])]
    for k, ref in enumerate((anchors, col_offset, row_offset, live_counts)):
        copies.append(pltpu.make_async_copy(ref, ints[k], sems.at[k + 1]))
    for copy in copies:
        copy.start()
    for copy in copies[1:]:
        copy.wait()
    lane = lanes(8)
    meta = jnp.zeros((8, PS), F32)
    for p in range(2):
        alive = jnp.where(p < ints[3][0, 0], 1, 0)
        for k, value in enumerate((ints[0][p], ints[1][p], ints[2][p], alive)):
            meta = jnp.where(lane == 4 * p + k, value.astype(F32), meta)
    copies[0].wait()
    for i in range(N_TM):
        chunk = field[CH * i : CH * i + HALO, :]
        high[i] = jnp.concatenate([chunk, meta], axis=0).astype(BF16)


def order_kernel(table, amp, out):
    def lines(value, product):
        high, low = split(value)
        return product(high) + product(low)

    rows = lines(amp[lax.axis_index("mode")], lambda x: dot(table[...], x))
    out[...] = lines(rows, lambda x: lax.dot_general(x, table[...], (((1,), (1,)), ((), ())), preferred_element_type=F32))


def cut_windows(meta, load, store, denom):
    def visit(t, total):
        for p in range(2):
            at, col, row, alive = (meta[t, 4 * p + k] for k in range(4))
            both = jnp.where(lanes(HALO) >= col, load(at), load(at + 1))
            both = pltpu.roll(both, lax.rem(HALO - row, HALO), 0)[0:CH].astype(BF16)
            store(t, p, both)
            both = pltpu.roll(both.astype(F32), lax.rem(PS - col, PS), 1)
            total = total + both * both * alive.astype(F32)
        return total

    denom[...] = lax.fori_loop(0, N_TM, visit, jnp.zeros((CH, PS), F32), unroll=4)


def window_kernel(meta, high, out, denom):
    def store(t, p, piece):
        out[2 * t + p] = piece

    cut_windows(meta, lambda at: high[at].astype(F32)[0:HALO], store, denom)


def shift_rows(block, row):
    return pltpu.roll(block, lax.rem(HALO + row, 32), 0)[0:HALO]


def weight_kernel(meta, power, out):
    out[...] = jnp.full_like(out, OBJECT_REG)
    first = pl.multiple_of(lax.axis_index("tm") * CH, CH)

    def visit(t, carry):
        block = power[pl.ds(first, 32), :]
        for p in range(2):
            at, col, row, alive = (meta[t, 4 * p + k] for k in range(4))
            mask = lanes(HALO) >= col
            cover = pltpu.roll(shift_rows(block, row), col, 1) * alive.astype(F32)
            out[at] += jnp.where(mask, cover, 0.0)
            out[at + 1] += jnp.where(mask, 0.0, cover)
        return carry

    lax.fori_loop(0, N_TM, visit, 0, unroll=UNROLL)

    def invert(t, carry):
        out[t] = 1.0 / out[t]
        return carry

    lax.fori_loop(0, N_TM, invert, 0, unroll=UNROLL)


def accumulate(meta, parts, num):
    num[...] = jnp.zeros_like(num)

    def visit(t, carry):
        both = parts[t, 64:112, :].astype(F32)
        for p in range(2):
            at, col = meta[t, 4 * p], meta[t, 4 * p + 1]
            mask = lanes(HALO) >= col
            piece = both[HALO * p : HALO * p + HALO]
            num[at] += jnp.where(mask, piece, 0.0)
            num[at + 1] += jnp.where(mask, 0.0, piece)
        return carry

    lax.fori_loop(0, N_TM, visit, 0, unroll=UNROLL)


def update_kernel(meta, parts, scale, high, out, denom, upd, fresh):
    accumulate(meta, parts, upd)

    def visit(t, carry):
        step = upd[t] * scale[t]
        upd[t] = step
        fresh[t] = high[t].astype(F32)[0:HALO] + step
        return carry

    lax.fori_loop(0, N_TM, visit, 0, unroll=UNROLL)

    def store(t, p, piece):
        out[t, CH * p : CH * p + CH, :] = piece

    cut_windows(meta, lambda at: fresh[at], store, denom)


def last_update_kernel(meta, parts, scale, upd, out, num):
    accumulate(meta, parts, num)

    def visit(t, carry):
        total = upd[t] + num[t] * scale[t]
        out[t] = jnp.concatenate([total, jnp.zeros((8, PS), F32)], axis=0).astype(BF16)
        return carry

    lax.fori_loop(0, N_TM, visit, 0, unroll=UNROLL)


def probe_sum_kernel(parts, denom, out):
    total = lax.fori_loop(0, N_TM, lambda t, acc: acc + parts[t, 0:64, :].astype(F32), jnp.zeros((64, PS), F32))
    out[0:64, :] = total.astype(BF16)
    out[64:80, :] = denom[...]


def probe_update_kernel(own, one, two, three, objs, out):
    total = (own[...].astype(F32) + two[...].astype(F32)) + (one[...].astype(F32) + three[...].astype(F32))
    scale = 1.0 / (total[64:80] + PROBE_REG)
    step = (total[0:64] * jnp.concatenate([scale] * 4, axis=0)).astype(BF16)

    def visit(t, carry):
        out[t, 0:32, :] = objs[t]
        out[t, 32:96, :] = step
        return carry

    lax.fori_loop(0, N_TM, visit, 0, unroll=UNROLL)


def pack_kernel(keep, recv, denom, out, denom_out):
    first = lax.axis_index("mode") == 0

    def visit(t, carry):
        mine, theirs = keep[t].astype(F32), recv[t].astype(F32)
        out[t, 0:64, :] = (mine[0:64] + theirs[0:64]).astype(BF16)
        num_mine, num_theirs = mine[64 : 64 + HALO], theirs[64 : 64 + HALO]
        out[t, 64:112, :] = jnp.concatenate(
            [jnp.where(first, num_mine, num_theirs), jnp.where(first, num_theirs, num_mine)], axis=0
        ).astype(BF16)
        return carry

    lax.fori_loop(0, N_TM, visit, 0, unroll=UNROLL)
    theirs = [recv[t, 64:96, :].astype(F32)[HALO:32] for t in range(2)]
    denom_out[...] = (denom[...] + jnp.concatenate(theirs, axis=0)).astype(BF16)


def parts_of(value):
    high, low = split(value)
    return (high, low, high)[:PARTS]


def put_left(ref, row, cols, value):
    for k, part in enumerate(parts_of(value)):
        ref[pl.ds(pl.multiple_of(row + k * PS, CH), CH), cols] = part


def put_right(ref, rows, lane, value):
    for k, part in enumerate(parts_of(value)):
        ref[rows, lane + k * PS : lane + k * PS + HALF] = part


def position_kernel(
    with_update, meta, tables, p_own, p_oth, h_own, h_oth, amp, denom,
    keep, send, power, obj, probe, x_even, x_odd, y_even, y_odd, half_even, half_odd, far_even, far_odd, shifted,
    left, right,
):
    for k in range(4):
        for part, which in enumerate((0, 0, 1)[:PARTS]):
            left[k, :, part * PS : (part + 1) * PS] = tables[which, k]
            right[k, part * PS : (part + 1) * PS, :] = tables[which, k]
    even, even_t, odd, odd_t = range(4)
    core = lax.axis_index("mode")
    first = core == 0
    col, row, alive = (meta[lax.axis_index("tm"), 4 * core + k] for k in (1, 2, 3))
    alive = alive.astype(F32)
    back_col = lax.rem(PS - col, PS)

    def rows_of(i, base=0):
        return pl.ds(pl.multiple_of(i * CH + base, CH), CH)

    def mode_cols(m):
        return slice(m * PS, (m + 1) * PS)

    power[0:8, :] = jnp.zeros((8, PS), F32)
    power[264:272, :] = jnp.zeros((8, PS), F32)

    def stage(i, carry):
        rows = rows_of(i)
        if with_update:
            mine = jnp.where(first, h_own[i, 0:CH, :].astype(F32), h_own[i, CH : 2 * CH, :].astype(F32))
            theirs = jnp.where(first, h_oth[i, 0:CH, :].astype(F32), h_oth[i, CH : 2 * CH, :].astype(F32))
            window = (jnp.where(first, mine, theirs), jnp.where(first, theirs, mine))
        else:
            window = [h_own[2 * i + k].astype(F32) for k in range(2)]
        for k in range(2):
            obj[k, rows, :] = pltpu.roll(window[k], back_col, 1)
        total = jnp.zeros((CH, PS), F32)
        for m in range(4):
            src, chunk = (p_own, h_own) if m < 2 else (p_oth, h_oth)
            for k in range(2):
                value = src[m % 2, k, rows, :]
                if with_update:
                    at = 32 + CH * (2 * (m % 2) + k)
                    value = value + chunk[i, at : at + CH, :].astype(F32)
                probe[m, k, rows, :] = value
                total = total + value * value
        power[pl.ds(pl.multiple_of(i * CH + 8, 8), CH), :] = total
        return carry

    lax.fori_loop(0, N_TM, stage, 0, unroll=UNROLL)

    def wave(m, rows):
        pr, pi = probe[m, 0, rows, :], probe[m, 1, rows, :]
        o_r, o_i = obj[0, rows, :], obj[1, rows, :]
        return pr * o_r - pi * o_i, pr * o_i + pi * o_r

    def forward_rows(i, carry):
        for m in range(4):
            upper, lower = wave(m, rows_of(i)), wave(m, rows_of(i, HALF))
            for k in range(2):
                a, b = upper[k], lower[k]
                put_left(x_even, i * CH + k * HALF, mode_cols(m), a + b)
                put_left(x_odd, i * CH + k * HALF, mode_cols(m), a - b)
        return carry

    lax.fori_loop(0, HALF // CH, forward_rows, 0, unroll=8)
    half_even[...] = dot(left[even], x_even[...])
    half_odd[...] = dot(left[odd], x_odd[...])

    def forward_cols(i, carry):
        for m in range(4):
            for b, half in enumerate((half_even, half_odd)):
                for k in range(2):
                    value = half[rows_of(i, k * HALF), mode_cols(m)]
                    rows = rows_of(i, m * PS + b * HALF)
                    put_right(y_even, rows, k * HALF, value[:, 0:HALF] + value[:, HALF:PS])
                    put_right(y_odd, rows, k * HALF, value[:, 0:HALF] - value[:, HALF:PS])
        return carry

    lax.fori_loop(0, HALF // CH, forward_cols, 0, unroll=8)
    far_even[...] = dot(y_even[...], right[even_t])
    far_odd[...] = dot(y_odd[...], right[odd_t])

    def rescale(i, carry):
        for b, (far, y) in enumerate(((far_even, y_even), (far_odd, y_odd))):
            values = [far[rows_of(i, m * PS), :] for m in range(4)]
            squares = [v[:, 0:HALF] * v[:, 0:HALF] + v[:, HALF:PS] * v[:, HALF:PS] for v in values]
            total = (squares[0] + squares[1]).astype(BF16).astype(F32) + (squares[2] + squares[3]).astype(
                BF16
            ).astype(F32)
            factor = amp[rows_of(i), b * HALF : (b + 1) * HALF] * lax.rsqrt(jnp.maximum(total, FLOOR_VALUE)) - 1.0
            for m in range(4):
                for k in range(2):
                    put_right(y, rows_of(i, m * PS), k * HALF, values[m][:, k * HALF : (k + 1) * HALF] * factor)
        return carry

    lax.fori_loop(0, N_TM, rescale, 0, unroll=UNROLL)
    far_even[...] = dot(y_even[...], right[even])
    far_odd[...] = dot(y_odd[...], right[odd])

    def backward_cols(i, carry):
        for m in range(4):
            for b, x in enumerate((x_even, x_odd)):
                rows = rows_of(i, m * PS + b * HALF)
                one, two = far_even[rows, :], far_odd[rows, :]
                total, diff = one + two, one - two
                for k in range(2):
                    part = slice(k * HALF, (k + 1) * HALF)
                    put_left(x, i * CH + k * HALF, slice(m * PS, m * PS + HALF), total[:, part])
                    put_left(x, i * CH + k * HALF, slice(m * PS + HALF, (m + 1) * PS), diff[:, part])
        return carry

    lax.fori_loop(0, HALF // CH, backward_cols, 0, unroll=8)
    half_even[...] = dot(left[even_t], x_even[...])
    half_odd[...] = dot(left[odd_t], x_odd[...])

    def outputs(i, carry):
        for s in range(2):
            rows = rows_of(i, s * HALF)
            n_re, n_im = jnp.zeros((CH, PS), F32), jnp.zeros((CH, PS), F32)
            for g, target in enumerate((keep, send)):
                g_re, g_im = jnp.zeros((CH, PS), F32), jnp.zeros((CH, PS), F32)
                for mm in range(2):
                    m = 2 * g + mm
                    pr, pi, o_r, o_i = probe[m, 0, rows, :], probe[m, 1, rows, :], obj[0, rows, :], obj[1, rows, :]
                    res = []
                    for k in range(2):
                        at = rows_of(i, k * HALF)
                        one, two = half_even[at, mode_cols(m)], half_odd[at, mode_cols(m)]
                        res.append(one + two if s == 0 else one - two)
                    dr, di = res[0] * alive, res[1] * alive
                    chunk = i + s * (HALF // CH)
                    target[chunk, 2 * mm * CH : (2 * mm + 1) * CH, :] = (o_r * dr + o_i * di).astype(BF16)
                    target[chunk, (2 * mm + 1) * CH : (2 * mm + 2) * CH, :] = (o_r * di - o_i * dr).astype(BF16)
                    g_re = g_re + (pr * dr + pi * di)
                    g_im = g_im + (pr * di - pi * dr)
                n_re = n_re + g_re.astype(BF16).astype(F32)
                n_im = n_im + g_im.astype(BF16).astype(F32)
            at = pl.ds(pl.multiple_of(i * CH + s * HALF + 8, 8), CH)
            shifted[0, at, :] = pltpu.roll(n_re, col, 1)
            shifted[1, at, :] = pltpu.roll(n_im, col, 1)
        return carry

    shifted[:, 0:8, :] = jnp.zeros((2, 8, PS), F32)
    shifted[:, 264:272, :] = jnp.zeros((2, 8, PS), F32)
    lax.fori_loop(0, HALF // CH, outputs, 0, unroll=8)

    def emit(i, carry):
        rows = pl.ds(pl.multiple_of(i * CH, CH), 32)
        pad = jnp.where(i == 0, denom[0:8, :], jnp.where(i == 1, denom[8:16, :], 0.0))
        re, im = (
            jnp.concatenate([shift_rows(shifted[k, rows, :], row), pad], axis=0) for k in range(2)
        )
        keep[i, 64:96, :] = jnp.where(first, re, im).astype(BF16)
        send[i, 64:96, :] = jnp.where(first, im, re).astype(BF16)
        return carry

    lax.fori_loop(0, N_TM, emit, 0, unroll=UNROLL)


def position(with_update, *args):
    part = arr((N_TM, 96, PS), BF16)
    left, right = pltpu.VMEM((PARTS * PS, 4 * PS), BF16), pltpu.VMEM((4 * PS, PARTS * PS), BF16)
    return call(
        functools.partial(position_kernel, with_update),
        (part, part, arr((272, PS), F32)),
        [SM] + [VM] * 7,
        scratch=[
            pltpu.VMEM((2, PS, PS), F32),
            pltpu.VMEM((4, 2, PS, PS), F32),
            left,
            left,
            right,
            right,
            pltpu.VMEM((PS, 4 * PS), F32),
            pltpu.VMEM((PS, 4 * PS), F32),
            pltpu.VMEM((4 * PS, PS), F32),
            pltpu.VMEM((4 * PS, PS), F32),
            pltpu.VMEM((2, 272, PS), F32),
            pltpu.VMEM((4, PS, PARTS * PS), BF16),
            pltpu.VMEM((4, PARTS * PS, PS), BF16),
        ],
        flops=32 * PARTS * 2 * 256 * 256 * 256,
        nbytes=10 << 20,
        vmem=32,
    )(*args)


def final_probe_kernel(p_own, h_one, h_two, out):
    def visit(i, carry):
        rows = pl.ds(pl.multiple_of(i * CH, CH), CH)
        for m in range(2):
            for k in range(2):
                at = 32 + CH * (2 * m + k)
                before = p_own[m, k, rows, :] + h_one[i, at : at + CH, :].astype(F32)
                out[m, k, rows, :] = before + h_two[i, at : at + CH, :].astype(F32)
        return carry

    lax.fori_loop(0, N_TM, visit, 0, unroll=UNROLL)


def final_object_kernel(obj, h_own, h_oth, out):
    core = lax.axis_index("mode")

    def visit(i, carry):
        rows = pl.ds(pl.multiple_of(i * CH, CH), CH)
        out[core, rows, :] = obj[core, rows, :] + h_own[i, 0:CH, :].astype(F32)
        out[1 - core, rows, :] = obj[1 - core, rows, :] + h_oth[i, 0:CH, :].astype(F32)
        return carry

    lax.fori_loop(0, N_TM, visit, 0, unroll=UNROLL)
    last = N_TM - 1
    out[core, 256:264, :] = obj[core, 256:264, :] + h_own[last, 16:32, :].astype(F32)[0:8]
    out[1 - core, 256:264, :] = obj[1 - core, 256:264, :] + h_oth[last, 16:32, :].astype(F32)[0:8]


def body(object_field, probe_modes, amplitudes, anchors, row_offset, col_offset, live_counts):
    tables = jnp.asarray(dft_tables())

    def exchange(x):
        return lax.all_to_all(x, "tm", 0, 0)

    def swap(x):
        return lax.ppermute(x, "mode", SWAP)

    def over_tiles(x):
        n = lax.axis_size("tile")
        return [lax.ppermute(x, "tile", [(i, (i + k) % n) for i in range(n)]) for k in (1, 2, 3)]

    slot = arr((N_TM, 32, PS), BF16)
    denom_shape = arr((CH, PS), F32)
    chunk = (N_TM, HALO, PS)
    high = call(
        prep_kernel,
        slot,
        [pl.BlockSpec(memory_space=pltpu.HBM)] * 5,
        scratch=[
            pltpu.VMEM((BH, PS), F32),
            [pltpu.SMEM(shape, jnp.int32) for shape in ((2,), (2,), (2,), (1, 1))],
            pltpu.SemaphoreType.DMA((5,)),
        ],
        vmem=60,
    )(anchors.reshape(-1), row_offset, col_offset, live_counts.reshape(1, 1), object_field)
    high = exchange(high)
    amp = call(order_kernel, arr((PS, PS), F32), [VM, VM])(jnp.asarray(order_table()), amplitudes)
    high, amp = lax.optimization_barrier((high, amp))
    meta = high[:, HALO, 0:8].astype(jnp.int32)
    windows, denom = call(window_kernel, (arr((2 * N_TM, CH, PS), BF16), denom_shape), [SM, VM])(meta, high)
    windows, own = lax.optimization_barrier((windows, probe_modes))
    probe_other = swap(own)
    h_own = h_oth = lax.all_to_all(windows, ("tm", "mode"), 0, 0)

    for iteration in range(2):
        if iteration > 0:
            h_oth = swap(h_own)
        keep, send, power = position(
            iteration > 0, meta, tables, probe_modes, probe_other, h_own, h_oth, amp, denom
        )
        recv = swap(send)
        scale = call(weight_kernel, arr(chunk, F32), [SM, VM])(meta, power)
        recv, scale = lax.optimization_barrier((recv, scale))
        parts, denom = call(pack_kernel, (arr((N_TM, 112, PS), BF16), arr((CH, PS), BF16)), [VM] * 3)(
            keep, recv, denom
        )
        parts = exchange(parts)
        probe_part = call(probe_sum_kernel, arr((80, PS), BF16), [VM] * 2)(parts, denom)
        others = over_tiles(probe_part)
        if iteration == 0:
            objs, denom, upd = call(
                update_kernel,
                (slot, denom_shape, arr(chunk, F32)),
                [SM] + [VM] * 3,
                scratch=[pltpu.VMEM(chunk, F32)],
            )(meta, parts, scale, high)
        else:
            objs = call(last_update_kernel, slot, [SM] + [VM] * 3, scratch=[pltpu.VMEM(chunk, F32)])(
                meta, parts, scale, upd
            )
        h_first = h_own
        h_own = exchange(
            call(probe_update_kernel, arr((N_TM, 96, PS), BF16), [VM] * 5)(probe_part, *others, objs)
        )

    h_oth = swap(h_own)
    probe_out = call(final_probe_kernel, arr((2, 2, PS, PS), F32), [VM] * 3)(probe_modes, h_first, h_own)
    object_out = call(final_object_kernel, arr((2, BH, PS), F32), [VM] * 3)(object_field, h_own, h_oth)
    return (object_out, probe_out)


def solution(mesh):
    placed = (
        P(None, "tile", "tm"),
        P("mode", None, None, None),
        P(("tile", "tm"), None, None),
        P(("tile", "tm"), None),
        P(("tile", "tm")),
        P(("tile", "tm")),
        P(("tile", "tm")),
    )
    return jax.shard_map(
        body,
        mesh=mesh,
        in_specs=placed,
        out_specs=(P(None, "tile", "tm"), P("mode", None, None, None)),
        check_vma=False,
    )
```

```python
import functools

import jax
import jax.numpy as jnp
import ml_dtypes
import numpy as np
from jax import lax
from jax.experimental import pallas as pl
from jax.experimental.pallas import tpu as pltpu
from jax.sharding import PartitionSpec as P

PS = 256
HALF = 128
PARTS = 3
BH = 264
N_TM = 16
UNROLL = 16
CH = 16
HALO = 24
FLOOR_VALUE = 0.5
OBJECT_REG = 1.0
PROBE_REG = 1.0
F32 = jnp.float32
BF16 = jnp.bfloat16
SWAP = [(0, 1), (1, 0)]

VM = pl.BlockSpec(memory_space=pltpu.VMEM)
SM = pl.BlockSpec(memory_space=pltpu.SMEM)


def real_form(matrix):
    return np.block([[matrix.real, -matrix.imag], [matrix.imag, matrix.real]]).astype(np.float32)


def halves(table):
    high = table.astype(ml_dtypes.bfloat16)
    return high, (table - high.astype(np.float32)).astype(ml_dtypes.bfloat16)


def dft_tables():
    n = np.arange(HALF)
    parts = []
    for k in (2 * n, 2 * n + 1):
        table = real_form(np.exp(-2j * np.pi * ((k[:, None] * n[None, :]) % PS) / PS) / np.sqrt(PS))
        parts += [halves(table), halves(table.T)]
    return np.stack([np.stack([p[k] for p in parts]) for k in range(min(PARTS, 2))])


def order_table():
    picked = np.concatenate([np.arange(0, PS, 2), np.arange(1, PS, 2)])
    table = np.zeros((PS, PS), np.float32)
    table[np.arange(PS), picked] = 1.0
    return table.astype(ml_dtypes.bfloat16)


def call(kernel, out_shape, in_specs, scratch=(), flops=0, nbytes=1 << 20, vmem=12):
    many = isinstance(out_shape, (tuple, list))
    return pl.pallas_call(
        kernel,
        out_shape=out_shape,
        in_specs=in_specs,
        out_specs=[VM] * len(out_shape) if many else VM,
        scratch_shapes=list(scratch),
        compiler_params=pltpu.CompilerParams(vmem_limit_bytes=vmem << 20),
        cost_estimate=pl.CostEstimate(flops=flops, bytes_accessed=nbytes, transcendentals=0),
    )


def arr(shape, dtype):
    return jax.ShapeDtypeStruct(shape, dtype)


def lanes(rows):
    return lax.broadcasted_iota(jnp.int32, (rows, PS), 1)


def split(value):
    high = value.astype(BF16)
    return high, (value - high.astype(F32)).astype(BF16)


def dot(a, b):
    return lax.dot_general(a, b, (((1,), (0,)), ((), ())), preferred_element_type=F32)


def prep_kernel(anchors, row_offset, col_offset, live_counts, obj, high, field, ints, sems):
    copies = [pltpu.make_async_copy(obj.at[lax.axis_index("mode")], field, sems.at[0])]
    for k, ref in enumerate((anchors, col_offset, row_offset, live_counts)):
        copies.append(pltpu.make_async_copy(ref, ints[k], sems.at[k + 1]))
    for copy in copies:
        copy.start()
    for copy in copies[1:]:
        copy.wait()
    lane = lanes(8)
    meta = jnp.zeros((8, PS), F32)
    for p in range(2):
        alive = jnp.where(p < ints[3][0, 0], 1, 0)
        for k, value in enumerate((ints[0][p], ints[1][p], ints[2][p], alive)):
            meta = jnp.where(lane == 4 * p + k, value.astype(F32), meta)
    copies[0].wait()
    for i in range(N_TM):
        chunk = field[CH * i : CH * i + HALO, :]
        high[i] = jnp.concatenate([chunk, meta], axis=0).astype(BF16)


def order_kernel(table, amp, out):
    def lines(value, product):
        high, low = split(value)
        return product(high) + product(low)

    rows = lines(amp[lax.axis_index("mode")], lambda x: dot(table[...], x))
    out[...] = lines(rows, lambda x: lax.dot_general(x, table[...], (((1,), (1,)), ((), ())), preferred_element_type=F32))


def cut_windows(meta, load, store, denom):
    def visit(t, total):
        for p in range(2):
            at, col, row, alive = (meta[t, 4 * p + k] for k in range(4))
            both = jnp.where(lanes(HALO) >= col, load(at), load(at + 1))
            both = pltpu.roll(both, lax.rem(HALO - row, HALO), 0)[0:CH].astype(BF16)
            store(t, p, both)
            both = pltpu.roll(both.astype(F32), lax.rem(PS - col, PS), 1)
            total = total + both * both * alive.astype(F32)
        return total

    denom[...] = lax.fori_loop(0, N_TM, visit, jnp.zeros((CH, PS), F32), unroll=4)


def window_kernel(meta, high, out, denom):
    def store(t, p, piece):
        out[2 * t + p] = piece

    cut_windows(meta, lambda at: high[at].astype(F32)[0:HALO], store, denom)


def shift_rows(block, row):
    return pltpu.roll(block, lax.rem(HALO + row, 32), 0)[0:HALO]


def weight_kernel(meta, power, out):
    out[...] = jnp.full_like(out, OBJECT_REG)
    first = pl.multiple_of(lax.axis_index("tm") * CH, CH)

    def visit(t, carry):
        block = power[pl.ds(first, 32), :]
        for p in range(2):
            at, col, row, alive = (meta[t, 4 * p + k] for k in range(4))
            mask = lanes(HALO) >= col
            cover = pltpu.roll(shift_rows(block, row), col, 1) * alive.astype(F32)
            out[at] += jnp.where(mask, cover, 0.0)
            out[at + 1] += jnp.where(mask, 0.0, cover)
        return carry

    lax.fori_loop(0, N_TM, visit, 0, unroll=UNROLL)

    def invert(t, carry):
        out[t] = 1.0 / out[t]
        return carry

    lax.fori_loop(0, N_TM, invert, 0, unroll=UNROLL)


def accumulate(meta, parts, num):
    num[...] = jnp.zeros_like(num)

    def visit(t, carry):
        both = parts[t, 64:112, :].astype(F32)
        for p in range(2):
            at, col = meta[t, 4 * p], meta[t, 4 * p + 1]
            mask = lanes(HALO) >= col
            piece = both[HALO * p : HALO * p + HALO]
            num[at] += jnp.where(mask, piece, 0.0)
            num[at + 1] += jnp.where(mask, 0.0, piece)
        return carry

    lax.fori_loop(0, N_TM, visit, 0, unroll=UNROLL)


def update_kernel(meta, parts, scale, high, out, denom, upd, fresh):
    accumulate(meta, parts, upd)

    def visit(t, carry):
        step = upd[t] * scale[t]
        upd[t] = step
        fresh[t] = high[t].astype(F32)[0:HALO] + step
        return carry

    lax.fori_loop(0, N_TM, visit, 0, unroll=UNROLL)

    def store(t, p, piece):
        out[t, CH * p : CH * p + CH, :] = piece

    cut_windows(meta, lambda at: fresh[at], store, denom)


def last_update_kernel(meta, parts, scale, upd, out, num):
    accumulate(meta, parts, num)

    def visit(t, carry):
        total = upd[t] + num[t] * scale[t]
        out[t] = jnp.concatenate([total, jnp.zeros((8, PS), F32)], axis=0).astype(BF16)
        return carry

    lax.fori_loop(0, N_TM, visit, 0, unroll=UNROLL)


def probe_sum_kernel(parts, denom, out):
    total = lax.fori_loop(0, N_TM, lambda t, acc: acc + parts[t, 0:64, :].astype(F32), jnp.zeros((64, PS), F32))
    out[0:64, :] = total.astype(BF16)
    out[64:80, :] = denom[...]


def probe_update_kernel(own, one, two, three, objs, left_out, out, left_out_now):
    total = (own[...].astype(F32) + two[...].astype(F32)) + (one[...].astype(F32) + three[...].astype(F32))
    scale = 1.0 / (total[64:80] + PROBE_REG)
    exact = total[0:64] * jnp.concatenate([scale] * 4, axis=0) + left_out[...]
    step = exact.astype(BF16)
    left_out_now[...] = exact - step.astype(F32)

    def visit(t, carry):
        out[t, 0:32, :] = objs[t]
        out[t, 32:96, :] = step
        return carry

    lax.fori_loop(0, N_TM, visit, 0, unroll=UNROLL)


def pack_kernel(keep, recv, denom, out, denom_out):
    first = lax.axis_index("mode") == 0

    def visit(t, carry):
        mine, theirs = keep[t].astype(F32), recv[t].astype(F32)
        out[t, 0:64, :] = (mine[0:64] + theirs[0:64]).astype(BF16)
        num_mine, num_theirs = mine[64 : 64 + HALO], theirs[64 : 64 + HALO]
        out[t, 64:112, :] = jnp.concatenate(
            [jnp.where(first, num_mine, num_theirs), jnp.where(first, num_theirs, num_mine)], axis=0
        ).astype(BF16)
        return carry

    lax.fori_loop(0, N_TM, visit, 0, unroll=UNROLL)
    theirs = [recv[t, 64:96, :].astype(F32)[HALO:32] for t in range(2)]
    denom_out[...] = (denom[...] + jnp.concatenate(theirs, axis=0)).astype(BF16)


def parts_of(value):
    high, low = split(value)
    return (high, low, high)[:PARTS]


def put_left(ref, row, cols, value):
    for k, part in enumerate(parts_of(value)):
        ref[pl.ds(pl.multiple_of(row + k * PS, CH), CH), cols] = part


def put_right(ref, rows, lane, value):
    for k, part in enumerate(parts_of(value)):
        ref[rows, lane + k * PS : lane + k * PS + HALF] = part


def position_kernel(
    with_update, meta, tables, p_own, p_oth, h_own, h_oth, amp, denom,
    keep, send, power, obj, probe, x_even, x_odd, y_even, y_odd, half_even, half_odd, far_even, far_odd, shifted,
    left, right,
):
    for k in range(4):
        for part, which in enumerate((0, 0, 1)[:PARTS]):
            left[k, :, part * PS : (part + 1) * PS] = tables[which, k]
            right[k, part * PS : (part + 1) * PS, :] = tables[which, k]
    even, even_t, odd, odd_t = range(4)
    core = lax.axis_index("mode")
    first = core == 0
    col, row, alive = (meta[lax.axis_index("tm"), 4 * core + k] for k in (1, 2, 3))
    alive = alive.astype(F32)
    back_col = lax.rem(PS - col, PS)

    def rows_of(i, base=0):
        return pl.ds(pl.multiple_of(i * CH + base, CH), CH)

    def mode_cols(m):
        return slice(m * PS, (m + 1) * PS)

    power[0:8, :] = jnp.zeros((8, PS), F32)
    power[264:272, :] = jnp.zeros((8, PS), F32)

    def stage(i, carry):
        rows = rows_of(i)
        if with_update:
            mine = jnp.where(first, h_own[i, 0:CH, :].astype(F32), h_own[i, CH : 2 * CH, :].astype(F32))
            theirs = jnp.where(first, h_oth[i, 0:CH, :].astype(F32), h_oth[i, CH : 2 * CH, :].astype(F32))
            window = (jnp.where(first, mine, theirs), jnp.where(first, theirs, mine))
        else:
            window = [h_own[2 * i + k].astype(F32) for k in range(2)]
        for k in range(2):
            obj[k, rows, :] = pltpu.roll(window[k], back_col, 1)
        total = jnp.zeros((CH, PS), F32)
        for m in range(4):
            src, chunk = (p_own, h_own) if m < 2 else (p_oth, h_oth)
            for k in range(2):
                value = src[m % 2, k, rows, :]
                if with_update:
                    at = 32 + CH * (2 * (m % 2) + k)
                    value = value + chunk[i, at : at + CH, :].astype(F32)
                probe[m, k, rows, :] = value
                total = total + value * value
        power[pl.ds(pl.multiple_of(i * CH + 8, 8), CH), :] = total
        return carry

    lax.fori_loop(0, N_TM, stage, 0, unroll=UNROLL)

    def wave(m, rows):
        pr, pi = probe[m, 0, rows, :], probe[m, 1, rows, :]
        o_r, o_i = obj[0, rows, :], obj[1, rows, :]
        return pr * o_r - pi * o_i, pr * o_i + pi * o_r

    def forward_rows(i, carry):
        for m in range(4):
            upper, lower = wave(m, rows_of(i)), wave(m, rows_of(i, HALF))
            for k in range(2):
                a, b = upper[k], lower[k]
                put_left(x_even, i * CH + k * HALF, mode_cols(m), a + b)
                put_left(x_odd, i * CH + k * HALF, mode_cols(m), a - b)
        return carry

    lax.fori_loop(0, HALF // CH, forward_rows, 0, unroll=8)
    half_even[...] = dot(left[even], x_even[...])
    half_odd[...] = dot(left[odd], x_odd[...])

    def forward_cols(i, carry):
        for m in range(4):
            for b, half in enumerate((half_even, half_odd)):
                for k in range(2):
                    value = half[rows_of(i, k * HALF), mode_cols(m)]
                    rows = rows_of(i, m * PS + b * HALF)
                    put_right(y_even, rows, k * HALF, value[:, 0:HALF] + value[:, HALF:PS])
                    put_right(y_odd, rows, k * HALF, value[:, 0:HALF] - value[:, HALF:PS])
        return carry

    lax.fori_loop(0, HALF // CH, forward_cols, 0, unroll=8)
    far_even[...] = dot(y_even[...], right[even_t])
    far_odd[...] = dot(y_odd[...], right[odd_t])

    def rescale(i, carry):
        for b, (far, y) in enumerate(((far_even, y_even), (far_odd, y_odd))):
            values = [far[rows_of(i, m * PS), :] for m in range(4)]
            squares = [v[:, 0:HALF] * v[:, 0:HALF] + v[:, HALF:PS] * v[:, HALF:PS] for v in values]
            total = (squares[0] + squares[1]).astype(BF16).astype(F32) + (squares[2] + squares[3]).astype(
                BF16
            ).astype(F32)
            factor = amp[rows_of(i), b * HALF : (b + 1) * HALF] * lax.rsqrt(jnp.maximum(total, FLOOR_VALUE)) - 1.0
            for m in range(4):
                for k in range(2):
                    put_right(y, rows_of(i, m * PS), k * HALF, values[m][:, k * HALF : (k + 1) * HALF] * factor)
        return carry

    lax.fori_loop(0, N_TM, rescale, 0, unroll=UNROLL)
    far_even[...] = dot(y_even[...], right[even])
    far_odd[...] = dot(y_odd[...], right[odd])

    def backward_cols(i, carry):
        for m in range(4):
            for b, x in enumerate((x_even, x_odd)):
                rows = rows_of(i, m * PS + b * HALF)
                one, two = far_even[rows, :], far_odd[rows, :]
                total, diff = one + two, one - two
                for k in range(2):
                    part = slice(k * HALF, (k + 1) * HALF)
                    put_left(x, i * CH + k * HALF, slice(m * PS, m * PS + HALF), total[:, part])
                    put_left(x, i * CH + k * HALF, slice(m * PS + HALF, (m + 1) * PS), diff[:, part])
        return carry

    lax.fori_loop(0, HALF // CH, backward_cols, 0, unroll=8)
    half_even[...] = dot(left[even_t], x_even[...])
    half_odd[...] = dot(left[odd_t], x_odd[...])

    def outputs(i, carry):
        for s in range(2):
            rows = rows_of(i, s * HALF)
            n_re, n_im = jnp.zeros((CH, PS), F32), jnp.zeros((CH, PS), F32)
            for g, target in enumerate((keep, send)):
                g_re, g_im = jnp.zeros((CH, PS), F32), jnp.zeros((CH, PS), F32)
                for mm in range(2):
                    m = 2 * g + mm
                    pr, pi, o_r, o_i = probe[m, 0, rows, :], probe[m, 1, rows, :], obj[0, rows, :], obj[1, rows, :]
                    res = []
                    for k in range(2):
                        at = rows_of(i, k * HALF)
                        one, two = half_even[at, mode_cols(m)], half_odd[at, mode_cols(m)]
                        res.append(one + two if s == 0 else one - two)
                    dr, di = res[0] * alive, res[1] * alive
                    chunk = i + s * (HALF // CH)
                    target[chunk, 2 * mm * CH : (2 * mm + 1) * CH, :] = (o_r * dr + o_i * di).astype(BF16)
                    target[chunk, (2 * mm + 1) * CH : (2 * mm + 2) * CH, :] = (o_r * di - o_i * dr).astype(BF16)
                    g_re = g_re + (pr * dr + pi * di)
                    g_im = g_im + (pr * di - pi * dr)
                n_re = n_re + g_re.astype(BF16).astype(F32)
                n_im = n_im + g_im.astype(BF16).astype(F32)
            at = pl.ds(pl.multiple_of(i * CH + s * HALF + 8, 8), CH)
            shifted[0, at, :] = pltpu.roll(n_re, col, 1)
            shifted[1, at, :] = pltpu.roll(n_im, col, 1)
        return carry

    shifted[:, 0:8, :] = jnp.zeros((2, 8, PS), F32)
    shifted[:, 264:272, :] = jnp.zeros((2, 8, PS), F32)
    lax.fori_loop(0, HALF // CH, outputs, 0, unroll=8)

    def emit(i, carry):
        rows = pl.ds(pl.multiple_of(i * CH, CH), 32)
        pad = jnp.where(i == 0, denom[0:8, :], jnp.where(i == 1, denom[8:16, :], 0.0))
        re, im = (
            jnp.concatenate([shift_rows(shifted[k, rows, :], row), pad], axis=0) for k in range(2)
        )
        keep[i, 64:96, :] = jnp.where(first, re, im).astype(BF16)
        send[i, 64:96, :] = jnp.where(first, im, re).astype(BF16)
        return carry

    lax.fori_loop(0, N_TM, emit, 0, unroll=UNROLL)


def position(with_update, *args):
    part = arr((N_TM, 96, PS), BF16)
    left, right = pltpu.VMEM((PARTS * PS, 4 * PS), BF16), pltpu.VMEM((4 * PS, PARTS * PS), BF16)
    return call(
        functools.partial(position_kernel, with_update),
        (part, part, arr((272, PS), F32)),
        [SM] + [VM] * 7,
        scratch=[
            pltpu.VMEM((2, PS, PS), F32),
            pltpu.VMEM((4, 2, PS, PS), F32),
            left,
            left,
            right,
            right,
            pltpu.VMEM((PS, 4 * PS), F32),
            pltpu.VMEM((PS, 4 * PS), F32),
            pltpu.VMEM((4 * PS, PS), F32),
            pltpu.VMEM((4 * PS, PS), F32),
            pltpu.VMEM((2, 272, PS), F32),
            pltpu.VMEM((4, PS, PARTS * PS), BF16),
            pltpu.VMEM((4, PARTS * PS, PS), BF16),
        ],
        flops=32 * PARTS * 2 * 256 * 256 * 256,
        nbytes=10 << 20,
        vmem=32,
    )(*args)


def final_probe_kernel(p_own, h_one, h_two, out):
    def visit(i, carry):
        rows = pl.ds(pl.multiple_of(i * CH, CH), CH)
        for m in range(2):
            for k in range(2):
                at = 32 + CH * (2 * m + k)
                before = p_own[m, k, rows, :] + h_one[i, at : at + CH, :].astype(F32)
                out[m, k, rows, :] = before + h_two[i, at : at + CH, :].astype(F32)
        return carry

    lax.fori_loop(0, N_TM, visit, 0, unroll=UNROLL)


def final_object_kernel(obj, h_own, h_oth, out):
    core = lax.axis_index("mode")

    def visit(i, carry):
        rows = pl.ds(pl.multiple_of(i * CH, CH), CH)
        out[core, rows, :] = obj[core, rows, :] + h_own[i, 0:CH, :].astype(F32)
        out[1 - core, rows, :] = obj[1 - core, rows, :] + h_oth[i, 0:CH, :].astype(F32)
        return carry

    lax.fori_loop(0, N_TM, visit, 0, unroll=UNROLL)
    last = N_TM - 1
    out[core, 256:264, :] = obj[core, 256:264, :] + h_own[last, 16:32, :].astype(F32)[0:8]
    out[1 - core, 256:264, :] = obj[1 - core, 256:264, :] + h_oth[last, 16:32, :].astype(F32)[0:8]


def body(object_field, probe_modes, amplitudes, anchors, row_offset, col_offset, live_counts):
    tables = jnp.asarray(dft_tables())

    def exchange(x):
        return lax.all_to_all(x, "tm", 0, 0)

    def swap(x):
        return lax.ppermute(x, "mode", SWAP)

    def over_tiles(x):
        n = lax.axis_size("tile")
        return [lax.ppermute(x, "tile", [(i, (i + k) % n) for i in range(n)]) for k in (1, 2, 3)]

    slot = arr((N_TM, 32, PS), BF16)
    denom_shape = arr((CH, PS), F32)
    chunk = (N_TM, HALO, PS)
    high = call(
        prep_kernel,
        slot,
        [pl.BlockSpec(memory_space=pltpu.HBM)] * 5,
        scratch=[
            pltpu.VMEM((BH, PS), F32),
            [pltpu.SMEM(shape, jnp.int32) for shape in ((2,), (2,), (2,), (1, 1))],
            pltpu.SemaphoreType.DMA((5,)),
        ],
        vmem=60,
    )(anchors.reshape(-1), row_offset, col_offset, live_counts.reshape(1, 1), object_field)
    high = exchange(high)
    amp = call(order_kernel, arr((PS, PS), F32), [VM, VM])(jnp.asarray(order_table()), amplitudes)
    high, amp = lax.optimization_barrier((high, amp))
    meta = high[:, HALO, 0:8].astype(jnp.int32)
    windows, denom = call(window_kernel, (arr((2 * N_TM, CH, PS), BF16), denom_shape), [SM, VM])(meta, high)
    windows, own = lax.optimization_barrier((windows, probe_modes))
    probe_other = swap(own)
    h_own = h_oth = lax.all_to_all(windows, ("tm", "mode"), 0, 0)

    left_out = jnp.zeros((64, PS), F32)
    for iteration in range(2):
        if iteration > 0:
            h_oth = swap(h_own)
        keep, send, power = position(
            iteration > 0, meta, tables, probe_modes, probe_other, h_own, h_oth, amp, denom
        )
        recv = swap(send)
        scale = call(weight_kernel, arr(chunk, F32), [SM, VM])(meta, power)
        recv, scale = lax.optimization_barrier((recv, scale))
        parts, denom = call(pack_kernel, (arr((N_TM, 112, PS), BF16), arr((CH, PS), BF16)), [VM] * 3)(
            keep, recv, denom
        )
        parts = exchange(parts)
        probe_part = call(probe_sum_kernel, arr((80, PS), BF16), [VM] * 2)(parts, denom)
        others = over_tiles(probe_part)
        if iteration == 0:
            objs, denom, upd = call(
                update_kernel,
                (slot, denom_shape, arr(chunk, F32)),
                [SM] + [VM] * 3,
                scratch=[pltpu.VMEM(chunk, F32)],
            )(meta, parts, scale, high)
        else:
            objs = call(last_update_kernel, slot, [SM] + [VM] * 3, scratch=[pltpu.VMEM(chunk, F32)])(
                meta, parts, scale, upd
            )
        h_first = h_own
        updates, left_out = call(
            probe_update_kernel, (arr((N_TM, 96, PS), BF16), arr((64, PS), F32)), [VM] * 6
        )(probe_part, *others, objs, left_out)
        h_own = exchange(updates)

    h_oth = swap(h_own)
    probe_out = call(final_probe_kernel, arr((2, 2, PS, PS), F32), [VM] * 3)(probe_modes, h_first, h_own)
    object_out = call(final_object_kernel, arr((2, BH, PS), F32), [VM] * 3)(object_field, h_own, h_oth)
    return (object_out, probe_out)


def solution(mesh):
    placed = (
        P(None, "tile", "tm"),
        P("mode", None, None, None),
        P(("tile", "tm"), None, None),
        P(("tile", "tm"), None),
        P(("tile", "tm")),
        P(("tile", "tm")),
        P(("tile", "tm")),
    )
    return jax.shard_map(
        body,
        mesh=mesh,
        in_specs=placed,
        out_specs=(P(None, "tile", "tm"), P("mode", None, None, None)),
        check_vma=False,
    )
```

```python
import functools

import jax
import jax.numpy as jnp
import ml_dtypes
import numpy as np
from jax import lax
from jax.experimental import pallas as pl
from jax.experimental.pallas import tpu as pltpu
from jax.sharding import PartitionSpec as P

PS = 256
HALF = 128
PARTS = 1
BH = 264
N_TM = 16
UNROLL = 16
CH = 16
HALO = 24
FLOOR_VALUE = 0.5
OBJECT_REG = 1.0
PROBE_REG = 1.0
F32 = jnp.float32
BF16 = jnp.bfloat16
SWAP = [(0, 1), (1, 0)]

VM = pl.BlockSpec(memory_space=pltpu.VMEM)
SM = pl.BlockSpec(memory_space=pltpu.SMEM)


def real_form(matrix):
    return np.block([[matrix.real, -matrix.imag], [matrix.imag, matrix.real]]).astype(np.float32)


def halves(table):
    high = table.astype(ml_dtypes.bfloat16)
    return high, (table - high.astype(np.float32)).astype(ml_dtypes.bfloat16)


def dft_tables():
    n = np.arange(HALF)
    parts = []
    for k in (2 * n, 2 * n + 1):
        table = real_form(np.exp(-2j * np.pi * ((k[:, None] * n[None, :]) % PS) / PS) / np.sqrt(PS))
        parts += [halves(table), halves(table.T)]
    return np.stack([np.stack([p[k] for p in parts]) for k in range(min(PARTS, 2))])


def order_table():
    picked = np.concatenate([np.arange(0, PS, 2), np.arange(1, PS, 2)])
    table = np.zeros((PS, PS), np.float32)
    table[np.arange(PS), picked] = 1.0
    return table.astype(ml_dtypes.bfloat16)


def call(kernel, out_shape, in_specs, scratch=(), flops=0, nbytes=1 << 20, vmem=12):
    many = isinstance(out_shape, (tuple, list))
    return pl.pallas_call(
        kernel,
        out_shape=out_shape,
        in_specs=in_specs,
        out_specs=[VM] * len(out_shape) if many else VM,
        scratch_shapes=list(scratch),
        compiler_params=pltpu.CompilerParams(vmem_limit_bytes=vmem << 20),
        cost_estimate=pl.CostEstimate(flops=flops, bytes_accessed=nbytes, transcendentals=0),
    )


def arr(shape, dtype):
    return jax.ShapeDtypeStruct(shape, dtype)


def lanes(rows):
    return lax.broadcasted_iota(jnp.int32, (rows, PS), 1)


def split(value):
    high = value.astype(BF16)
    return high, (value - high.astype(F32)).astype(BF16)


def dot(a, b):
    return lax.dot_general(a, b, (((1,), (0,)), ((), ())), preferred_element_type=F32)


def prep_kernel(anchors, row_offset, col_offset, live_counts, obj, high, field, ints, sems):
    copies = [pltpu.make_async_copy(obj.at[lax.axis_index("mode")], field, sems.at[0])]
    for k, ref in enumerate((anchors, col_offset, row_offset, live_counts)):
        copies.append(pltpu.make_async_copy(ref, ints[k], sems.at[k + 1]))
    for copy in copies:
        copy.start()
    for copy in copies[1:]:
        copy.wait()
    lane = lanes(8)
    meta = jnp.zeros((8, PS), F32)
    for p in range(2):
        alive = jnp.where(p < ints[3][0, 0], 1, 0)
        for k, value in enumerate((ints[0][p], ints[1][p], ints[2][p], alive)):
            meta = jnp.where(lane == 4 * p + k, value.astype(F32), meta)
    copies[0].wait()
    for i in range(N_TM):
        chunk = field[CH * i : CH * i + HALO, :]
        high[i] = jnp.concatenate([chunk, meta], axis=0).astype(BF16)


def order_kernel(table, amp, out):
    def lines(value, product):
        high, low = split(value)
        return product(high) + product(low)

    rows = lines(amp[lax.axis_index("mode")], lambda x: dot(table[...], x))
    out[...] = lines(rows, lambda x: lax.dot_general(x, table[...], (((1,), (1,)), ((), ())), preferred_element_type=F32))


def cut_windows(meta, load, store, denom):
    def visit(t, total):
        for p in range(2):
            at, col, row, alive = (meta[t, 4 * p + k] for k in range(4))
            both = jnp.where(lanes(HALO) >= col, load(at), load(at + 1))
            both = pltpu.roll(both, lax.rem(HALO - row, HALO), 0)[0:CH].astype(BF16)
            store(t, p, both)
            both = pltpu.roll(both.astype(F32), lax.rem(PS - col, PS), 1)
            total = total + both * both * alive.astype(F32)
        return total

    denom[...] = lax.fori_loop(0, N_TM, visit, jnp.zeros((CH, PS), F32), unroll=4)


def window_kernel(meta, high, out, denom):
    def store(t, p, piece):
        out[2 * t + p] = piece

    cut_windows(meta, lambda at: high[at].astype(F32)[0:HALO], store, denom)


def shift_rows(block, row):
    return pltpu.roll(block, lax.rem(HALO + row, 32), 0)[0:HALO]


def weight_kernel(meta, power, out):
    out[...] = jnp.full_like(out, OBJECT_REG)
    first = pl.multiple_of(lax.axis_index("tm") * CH, CH)

    def visit(t, carry):
        block = power[pl.ds(first, 32), :]
        for p in range(2):
            at, col, row, alive = (meta[t, 4 * p + k] for k in range(4))
            mask = lanes(HALO) >= col
            cover = pltpu.roll(shift_rows(block, row), col, 1) * alive.astype(F32)
            out[at] += jnp.where(mask, cover, 0.0)
            out[at + 1] += jnp.where(mask, 0.0, cover)
        return carry

    lax.fori_loop(0, N_TM, visit, 0, unroll=UNROLL)

    def invert(t, carry):
        out[t] = 1.0 / out[t]
        return carry

    lax.fori_loop(0, N_TM, invert, 0, unroll=UNROLL)


def accumulate(meta, parts, num):
    num[...] = jnp.zeros_like(num)

    def visit(t, carry):
        both = parts[t, 64:112, :].astype(F32)
        for p in range(2):
            at, col = meta[t, 4 * p], meta[t, 4 * p + 1]
            mask = lanes(HALO) >= col
            piece = both[HALO * p : HALO * p + HALO]
            num[at] += jnp.where(mask, piece, 0.0)
            num[at + 1] += jnp.where(mask, 0.0, piece)
        return carry

    lax.fori_loop(0, N_TM, visit, 0, unroll=UNROLL)


def update_kernel(meta, parts, scale, high, out, denom, upd, fresh):
    accumulate(meta, parts, upd)

    def visit(t, carry):
        step = upd[t] * scale[t]
        upd[t] = step
        fresh[t] = high[t].astype(F32)[0:HALO] + step
        return carry

    lax.fori_loop(0, N_TM, visit, 0, unroll=UNROLL)

    def store(t, p, piece):
        out[t, CH * p : CH * p + CH, :] = piece

    cut_windows(meta, lambda at: fresh[at], store, denom)


def last_update_kernel(meta, parts, scale, upd, out, num):
    accumulate(meta, parts, num)

    def visit(t, carry):
        total = upd[t] + num[t] * scale[t]
        out[t] = jnp.concatenate([total, jnp.zeros((8, PS), F32)], axis=0).astype(BF16)
        return carry

    lax.fori_loop(0, N_TM, visit, 0, unroll=UNROLL)


def probe_sum_kernel(parts, denom, out):
    total = lax.fori_loop(0, N_TM, lambda t, acc: acc + parts[t, 0:64, :].astype(F32), jnp.zeros((64, PS), F32))
    out[0:64, :] = total.astype(BF16)
    out[64:80, :] = denom[...]


def probe_update_kernel(own, one, two, three, objs, left_out, out, left_out_now):
    total = (own[...].astype(F32) + two[...].astype(F32)) + (one[...].astype(F32) + three[...].astype(F32))
    scale = 1.0 / (total[64:80] + PROBE_REG)
    exact = total[0:64] * jnp.concatenate([scale] * 4, axis=0) + left_out[...]
    step = exact.astype(BF16)
    left_out_now[...] = exact - step.astype(F32)

    def visit(t, carry):
        out[t, 0:32, :] = objs[t]
        out[t, 32:96, :] = step
        return carry

    lax.fori_loop(0, N_TM, visit, 0, unroll=UNROLL)


def pack_kernel(keep, recv, denom, out, denom_out):
    first = lax.axis_index("mode") == 0

    def visit(t, carry):
        mine, theirs = keep[t].astype(F32), recv[t].astype(F32)
        out[t, 0:64, :] = (mine[0:64] + theirs[0:64]).astype(BF16)
        num_mine, num_theirs = mine[64 : 64 + HALO], theirs[64 : 64 + HALO]
        out[t, 64:112, :] = jnp.concatenate(
            [jnp.where(first, num_mine, num_theirs), jnp.where(first, num_theirs, num_mine)], axis=0
        ).astype(BF16)
        return carry

    lax.fori_loop(0, N_TM, visit, 0, unroll=UNROLL)
    theirs = [recv[t, 64:96, :].astype(F32)[HALO:32] for t in range(2)]
    denom_out[...] = (denom[...] + jnp.concatenate(theirs, axis=0)).astype(BF16)


def parts_of(value):
    high, low = split(value)
    return (high, low, high)[:PARTS]


def put_left(ref, row, cols, value):
    for k, part in enumerate(parts_of(value)):
        ref[pl.ds(pl.multiple_of(row + k * PS, CH), CH), cols] = part


def put_right(ref, rows, lane, value):
    for k, part in enumerate(parts_of(value)):
        ref[rows, lane + k * PS : lane + k * PS + HALF] = part


def position_kernel(
    with_update, meta, tables, p_own, p_oth, h_own, h_oth, amp, denom,
    keep, send, power, obj, probe, x_even, x_odd, y_even, y_odd, half_even, half_odd, far_even, far_odd, shifted,
    left, right,
):
    for k in range(4):
        for part, which in enumerate((0, 0, 1)[:PARTS]):
            left[k, :, part * PS : (part + 1) * PS] = tables[which, k]
            right[k, part * PS : (part + 1) * PS, :] = tables[which, k]
    even, even_t, odd, odd_t = range(4)
    core = lax.axis_index("mode")
    first = core == 0
    col, row, alive = (meta[lax.axis_index("tm"), 4 * core + k] for k in (1, 2, 3))
    alive = alive.astype(F32)
    back_col = lax.rem(PS - col, PS)

    def rows_of(i, base=0):
        return pl.ds(pl.multiple_of(i * CH + base, CH), CH)

    def mode_cols(m):
        return slice(m * PS, (m + 1) * PS)

    power[0:8, :] = jnp.zeros((8, PS), F32)
    power[264:272, :] = jnp.zeros((8, PS), F32)

    def stage(i, carry):
        rows = rows_of(i)
        if with_update:
            mine = jnp.where(first, h_own[i, 0:CH, :].astype(F32), h_own[i, CH : 2 * CH, :].astype(F32))
            theirs = jnp.where(first, h_oth[i, 0:CH, :].astype(F32), h_oth[i, CH : 2 * CH, :].astype(F32))
            window = (jnp.where(first, mine, theirs), jnp.where(first, theirs, mine))
        else:
            window = [h_own[2 * i + k].astype(F32) for k in range(2)]
        for k in range(2):
            obj[k, rows, :] = pltpu.roll(window[k], back_col, 1)
        total = jnp.zeros((CH, PS), F32)
        for m in range(4):
            src, chunk = (p_own, h_own) if m < 2 else (p_oth, h_oth)
            for k in range(2):
                value = src[m % 2, k, rows, :]
                if with_update:
                    at = 32 + CH * (2 * (m % 2) + k)
                    value = value + chunk[i, at : at + CH, :].astype(F32)
                probe[m, k, rows, :] = value
                total = total + value * value
        power[pl.ds(pl.multiple_of(i * CH + 8, 8), CH), :] = total
        return carry

    lax.fori_loop(0, N_TM, stage, 0, unroll=UNROLL)

    def wave(m, rows):
        pr, pi = probe[m, 0, rows, :], probe[m, 1, rows, :]
        o_r, o_i = obj[0, rows, :], obj[1, rows, :]
        return pr * o_r - pi * o_i, pr * o_i + pi * o_r

    def forward_rows(i, carry):
        for m in range(4):
            upper, lower = wave(m, rows_of(i)), wave(m, rows_of(i, HALF))
            for k in range(2):
                a, b = upper[k], lower[k]
                put_left(x_even, i * CH + k * HALF, mode_cols(m), a + b)
                put_left(x_odd, i * CH + k * HALF, mode_cols(m), a - b)
        return carry

    lax.fori_loop(0, HALF // CH, forward_rows, 0, unroll=8)
    half_even[...] = dot(left[even], x_even[...])
    half_odd[...] = dot(left[odd], x_odd[...])

    def forward_cols(i, carry):
        for m in range(4):
            for b, half in enumerate((half_even, half_odd)):
                for k in range(2):
                    value = half[rows_of(i, k * HALF), mode_cols(m)]
                    rows = rows_of(i, m * PS + b * HALF)
                    put_right(y_even, rows, k * HALF, value[:, 0:HALF] + value[:, HALF:PS])
                    put_right(y_odd, rows, k * HALF, value[:, 0:HALF] - value[:, HALF:PS])
        return carry

    lax.fori_loop(0, HALF // CH, forward_cols, 0, unroll=8)
    far_even[...] = dot(y_even[...], right[even_t])
    far_odd[...] = dot(y_odd[...], right[odd_t])

    def rescale(i, carry):
        for b, (far, y) in enumerate(((far_even, y_even), (far_odd, y_odd))):
            values = [far[rows_of(i, m * PS), :] for m in range(4)]
            squares = [v[:, 0:HALF] * v[:, 0:HALF] + v[:, HALF:PS] * v[:, HALF:PS] for v in values]
            total = (squares[0] + squares[1]).astype(BF16).astype(F32) + (squares[2] + squares[3]).astype(
                BF16
            ).astype(F32)
            factor = amp[rows_of(i), b * HALF : (b + 1) * HALF] * lax.rsqrt(jnp.maximum(total, FLOOR_VALUE)) - 1.0
            for m in range(4):
                for k in range(2):
                    put_right(y, rows_of(i, m * PS), k * HALF, values[m][:, k * HALF : (k + 1) * HALF] * factor)
        return carry

    lax.fori_loop(0, N_TM, rescale, 0, unroll=UNROLL)
    far_even[...] = dot(y_even[...], right[even])
    far_odd[...] = dot(y_odd[...], right[odd])

    def backward_cols(i, carry):
        for m in range(4):
            for b, x in enumerate((x_even, x_odd)):
                rows = rows_of(i, m * PS + b * HALF)
                one, two = far_even[rows, :], far_odd[rows, :]
                total, diff = one + two, one - two
                for k in range(2):
                    part = slice(k * HALF, (k + 1) * HALF)
                    put_left(x, i * CH + k * HALF, slice(m * PS, m * PS + HALF), total[:, part])
                    put_left(x, i * CH + k * HALF, slice(m * PS + HALF, (m + 1) * PS), diff[:, part])
        return carry

    lax.fori_loop(0, HALF // CH, backward_cols, 0, unroll=8)
    half_even[...] = dot(left[even_t], x_even[...])
    half_odd[...] = dot(left[odd_t], x_odd[...])

    def outputs(i, carry):
        for s in range(2):
            rows = rows_of(i, s * HALF)
            n_re, n_im = jnp.zeros((CH, PS), F32), jnp.zeros((CH, PS), F32)
            for g, target in enumerate((keep, send)):
                g_re, g_im = jnp.zeros((CH, PS), F32), jnp.zeros((CH, PS), F32)
                for mm in range(2):
                    m = 2 * g + mm
                    pr, pi, o_r, o_i = probe[m, 0, rows, :], probe[m, 1, rows, :], obj[0, rows, :], obj[1, rows, :]
                    res = []
                    for k in range(2):
                        at = rows_of(i, k * HALF)
                        one, two = half_even[at, mode_cols(m)], half_odd[at, mode_cols(m)]
                        res.append(one + two if s == 0 else one - two)
                    dr, di = res[0] * alive, res[1] * alive
                    chunk = i + s * (HALF // CH)
                    target[chunk, 2 * mm * CH : (2 * mm + 1) * CH, :] = (o_r * dr + o_i * di).astype(BF16)
                    target[chunk, (2 * mm + 1) * CH : (2 * mm + 2) * CH, :] = (o_r * di - o_i * dr).astype(BF16)
                    g_re = g_re + (pr * dr + pi * di)
                    g_im = g_im + (pr * di - pi * dr)
                n_re = n_re + g_re.astype(BF16).astype(F32)
                n_im = n_im + g_im.astype(BF16).astype(F32)
            at = pl.ds(pl.multiple_of(i * CH + s * HALF + 8, 8), CH)
            shifted[0, at, :] = pltpu.roll(n_re, col, 1)
            shifted[1, at, :] = pltpu.roll(n_im, col, 1)
        return carry

    shifted[:, 0:8, :] = jnp.zeros((2, 8, PS), F32)
    shifted[:, 264:272, :] = jnp.zeros((2, 8, PS), F32)
    lax.fori_loop(0, HALF // CH, outputs, 0, unroll=8)

    def emit(i, carry):
        rows = pl.ds(pl.multiple_of(i * CH, CH), 32)
        pad = jnp.where(i == 0, denom[0:8, :], jnp.where(i == 1, denom[8:16, :], 0.0))
        re, im = (
            jnp.concatenate([shift_rows(shifted[k, rows, :], row), pad], axis=0) for k in range(2)
        )
        keep[i, 64:96, :] = jnp.where(first, re, im).astype(BF16)
        send[i, 64:96, :] = jnp.where(first, im, re).astype(BF16)
        return carry

    lax.fori_loop(0, N_TM, emit, 0, unroll=UNROLL)


def position(with_update, *args):
    part = arr((N_TM, 96, PS), BF16)
    left, right = pltpu.VMEM((PARTS * PS, 4 * PS), BF16), pltpu.VMEM((4 * PS, PARTS * PS), BF16)
    return call(
        functools.partial(position_kernel, with_update),
        (part, part, arr((272, PS), F32)),
        [SM] + [VM] * 7,
        scratch=[
            pltpu.VMEM((2, PS, PS), F32),
            pltpu.VMEM((4, 2, PS, PS), F32),
            left,
            left,
            right,
            right,
            pltpu.VMEM((PS, 4 * PS), F32),
            pltpu.VMEM((PS, 4 * PS), F32),
            pltpu.VMEM((4 * PS, PS), F32),
            pltpu.VMEM((4 * PS, PS), F32),
            pltpu.VMEM((2, 272, PS), F32),
            pltpu.VMEM((4, PS, PARTS * PS), BF16),
            pltpu.VMEM((4, PARTS * PS, PS), BF16),
        ],
        flops=32 * PARTS * 2 * 256 * 256 * 256,
        nbytes=10 << 20,
        vmem=32,
    )(*args)


def final_probe_kernel(p_own, h_one, h_two, out):
    def visit(i, carry):
        rows = pl.ds(pl.multiple_of(i * CH, CH), CH)
        for m in range(2):
            for k in range(2):
                at = 32 + CH * (2 * m + k)
                before = p_own[m, k, rows, :] + h_one[i, at : at + CH, :].astype(F32)
                out[m, k, rows, :] = before + h_two[i, at : at + CH, :].astype(F32)
        return carry

    lax.fori_loop(0, N_TM, visit, 0, unroll=UNROLL)


def final_object_kernel(obj, h_own, h_oth, out):
    core = lax.axis_index("mode")

    def visit(i, carry):
        rows = pl.ds(pl.multiple_of(i * CH, CH), CH)
        out[core, rows, :] = obj[core, rows, :] + h_own[i, 0:CH, :].astype(F32)
        out[1 - core, rows, :] = obj[1 - core, rows, :] + h_oth[i, 0:CH, :].astype(F32)
        return carry

    lax.fori_loop(0, N_TM, visit, 0, unroll=UNROLL)
    last = N_TM - 1
    out[core, 256:264, :] = obj[core, 256:264, :] + h_own[last, 16:32, :].astype(F32)[0:8]
    out[1 - core, 256:264, :] = obj[1 - core, 256:264, :] + h_oth[last, 16:32, :].astype(F32)[0:8]


def body(object_field, probe_modes, amplitudes, anchors, row_offset, col_offset, live_counts):
    tables = jnp.asarray(dft_tables())

    def exchange(x):
        return lax.all_to_all(x, "tm", 0, 0)

    def swap(x):
        return lax.ppermute(x, "mode", SWAP)

    def over_tiles(x):
        n = lax.axis_size("tile")
        return [lax.ppermute(x, "tile", [(i, (i + k) % n) for i in range(n)]) for k in (1, 2, 3)]

    slot = arr((N_TM, 32, PS), BF16)
    denom_shape = arr((CH, PS), F32)
    chunk = (N_TM, HALO, PS)
    high = call(
        prep_kernel,
        slot,
        [pl.BlockSpec(memory_space=pltpu.HBM)] * 5,
        scratch=[
            pltpu.VMEM((BH, PS), F32),
            [pltpu.SMEM(shape, jnp.int32) for shape in ((2,), (2,), (2,), (1, 1))],
            pltpu.SemaphoreType.DMA((5,)),
        ],
        vmem=60,
    )(anchors.reshape(-1), row_offset, col_offset, live_counts.reshape(1, 1), object_field)
    high = exchange(high)
    amp = call(order_kernel, arr((PS, PS), F32), [VM, VM])(jnp.asarray(order_table()), amplitudes)
    high, amp = lax.optimization_barrier((high, amp))
    meta = high[:, HALO, 0:8].astype(jnp.int32)
    windows, denom = call(window_kernel, (arr((2 * N_TM, CH, PS), BF16), denom_shape), [SM, VM])(meta, high)
    windows, own = lax.optimization_barrier((windows, probe_modes))
    probe_other = swap(own)
    h_own = h_oth = lax.all_to_all(windows, ("tm", "mode"), 0, 0)

    left_out = jnp.zeros((64, PS), F32)
    for iteration in range(2):
        if iteration > 0:
            h_oth = swap(h_own)
        keep, send, power = position(
            iteration > 0, meta, tables, probe_modes, probe_other, h_own, h_oth, amp, denom
        )
        recv = swap(send)
        scale = call(weight_kernel, arr(chunk, F32), [SM, VM])(meta, power)
        recv, scale = lax.optimization_barrier((recv, scale))
        parts, denom = call(pack_kernel, (arr((N_TM, 112, PS), BF16), arr((CH, PS), BF16)), [VM] * 3)(
            keep, recv, denom
        )
        parts = exchange(parts)
        probe_part = call(probe_sum_kernel, arr((80, PS), BF16), [VM] * 2)(parts, denom)
        others = over_tiles(probe_part)
        if iteration == 0:
            objs, denom, upd = call(
                update_kernel,
                (slot, denom_shape, arr(chunk, F32)),
                [SM] + [VM] * 3,
                scratch=[pltpu.VMEM(chunk, F32)],
            )(meta, parts, scale, high)
        else:
            objs = call(last_update_kernel, slot, [SM] + [VM] * 3, scratch=[pltpu.VMEM(chunk, F32)])(
                meta, parts, scale, upd
            )
        h_first = h_own
        updates, left_out = call(
            probe_update_kernel, (arr((N_TM, 96, PS), BF16), arr((64, PS), F32)), [VM] * 6
        )(probe_part, *others, objs, left_out)
        h_own = exchange(updates)

    h_oth = swap(h_own)
    probe_out = call(final_probe_kernel, arr((2, 2, PS, PS), F32), [VM] * 3)(probe_modes, h_first, h_own)
    object_out = call(final_object_kernel, arr((2, BH, PS), F32), [VM] * 3)(object_field, h_own, h_oth)
    return (object_out, probe_out)


def solution(mesh):
    placed = (
        P(None, "tile", "tm"),
        P("mode", None, None, None),
        P(("tile", "tm"), None, None),
        P(("tile", "tm"), None),
        P(("tile", "tm")),
        P(("tile", "tm")),
        P(("tile", "tm")),
    )
    return jax.shard_map(
        body,
        mesh=mesh,
        in_specs=placed,
        out_specs=(P(None, "tile", "tm"), P("mode", None, None, None)),
        check_vma=False,
    )
```

```python
import functools

import jax
import jax.numpy as jnp
import ml_dtypes
import numpy as np
from jax import lax
from jax.experimental import pallas as pl
from jax.experimental.pallas import tpu as pltpu
from jax.sharding import PartitionSpec as P

PS = 256
HALF = 128
PARTS = 2
BH = 264
N_TM = 16
UNROLL = 16
CH = 16
HALO = 24
FLOOR_VALUE = 0.5
OBJECT_REG = 1.0
PROBE_REG = 1.0
F32 = jnp.float32
BF16 = jnp.bfloat16
SWAP = [(0, 1), (1, 0)]

VM = pl.BlockSpec(memory_space=pltpu.VMEM)
SM = pl.BlockSpec(memory_space=pltpu.SMEM)


def real_form(matrix):
    return np.block([[matrix.real, -matrix.imag], [matrix.imag, matrix.real]]).astype(np.float32)


def halves(table):
    high = table.astype(ml_dtypes.bfloat16)
    return high, (table - high.astype(np.float32)).astype(ml_dtypes.bfloat16)


def dft_tables():
    n = np.arange(HALF)
    parts = []
    for k in (2 * n, 2 * n + 1):
        table = real_form(np.exp(-2j * np.pi * ((k[:, None] * n[None, :]) % PS) / PS) / np.sqrt(PS))
        parts += [halves(table), halves(table.T)]
    return np.stack([np.stack([p[k] for p in parts]) for k in range(min(PARTS, 2))])


def order_table():
    picked = np.concatenate([np.arange(0, PS, 2), np.arange(1, PS, 2)])
    table = np.zeros((PS, PS), np.float32)
    table[np.arange(PS), picked] = 1.0
    return table.astype(ml_dtypes.bfloat16)


def call(kernel, out_shape, in_specs, scratch=(), flops=0, nbytes=1 << 20, vmem=12):
    many = isinstance(out_shape, (tuple, list))
    return pl.pallas_call(
        kernel,
        out_shape=out_shape,
        in_specs=in_specs,
        out_specs=[VM] * len(out_shape) if many else VM,
        scratch_shapes=list(scratch),
        compiler_params=pltpu.CompilerParams(vmem_limit_bytes=vmem << 20),
        cost_estimate=pl.CostEstimate(flops=flops, bytes_accessed=nbytes, transcendentals=0),
    )


def arr(shape, dtype):
    return jax.ShapeDtypeStruct(shape, dtype)


def lanes(rows):
    return lax.broadcasted_iota(jnp.int32, (rows, PS), 1)


def split(value):
    high = value.astype(BF16)
    return high, (value - high.astype(F32)).astype(BF16)


def dot(a, b):
    return lax.dot_general(a, b, (((1,), (0,)), ((), ())), preferred_element_type=F32)


def prep_kernel(anchors, row_offset, col_offset, live_counts, obj, high, field, ints, sems):
    copies = [pltpu.make_async_copy(obj.at[lax.axis_index("mode")], field, sems.at[0])]
    for k, ref in enumerate((anchors, col_offset, row_offset, live_counts)):
        copies.append(pltpu.make_async_copy(ref, ints[k], sems.at[k + 1]))
    for copy in copies:
        copy.start()
    for copy in copies[1:]:
        copy.wait()
    lane = lanes(8)
    meta = jnp.zeros((8, PS), F32)
    for p in range(2):
        alive = jnp.where(p < ints[3][0, 0], 1, 0)
        for k, value in enumerate((ints[0][p], ints[1][p], ints[2][p], alive)):
            meta = jnp.where(lane == 4 * p + k, value.astype(F32), meta)
    copies[0].wait()
    for i in range(N_TM):
        chunk = field[CH * i : CH * i + HALO, :]
        high[i] = jnp.concatenate([chunk, meta], axis=0).astype(BF16)


def order_kernel(table, amp, out):
    def lines(value, product):
        high, low = split(value)
        return product(high) + product(low)

    rows = lines(amp[lax.axis_index("mode")], lambda x: dot(table[...], x))
    out[...] = lines(rows, lambda x: lax.dot_general(x, table[...], (((1,), (1,)), ((), ())), preferred_element_type=F32))


def cut_windows(meta, load, store, denom):
    def visit(t, total):
        for p in range(2):
            at, col, row, alive = (meta[t, 4 * p + k] for k in range(4))
            both = jnp.where(lanes(HALO) >= col, load(at), load(at + 1))
            both = pltpu.roll(both, lax.rem(HALO - row, HALO), 0)[0:CH].astype(BF16)
            store(t, p, both)
            both = pltpu.roll(both.astype(F32), lax.rem(PS - col, PS), 1)
            total = total + both * both * alive.astype(F32)
        return total

    denom[...] = lax.fori_loop(0, N_TM, visit, jnp.zeros((CH, PS), F32), unroll=4)


def window_kernel(meta, high, out, denom):
    def store(t, p, piece):
        out[2 * t + p] = piece

    cut_windows(meta, lambda at: high[at].astype(F32)[0:HALO], store, denom)


def shift_rows(block, row):
    return pltpu.roll(block, lax.rem(HALO + row, 32), 0)[0:HALO]


def weight_kernel(meta, power, out):
    out[...] = jnp.full_like(out, OBJECT_REG)
    first = pl.multiple_of(lax.axis_index("tm") * CH, CH)

    def visit(t, carry):
        block = power[pl.ds(first, 32), :]
        for p in range(2):
            at, col, row, alive = (meta[t, 4 * p + k] for k in range(4))
            mask = lanes(HALO) >= col
            cover = pltpu.roll(shift_rows(block, row), col, 1) * alive.astype(F32)
            out[at] += jnp.where(mask, cover, 0.0)
            out[at + 1] += jnp.where(mask, 0.0, cover)
        return carry

    lax.fori_loop(0, N_TM, visit, 0, unroll=UNROLL)

    def invert(t, carry):
        out[t] = 1.0 / out[t]
        return carry

    lax.fori_loop(0, N_TM, invert, 0, unroll=UNROLL)


def accumulate(meta, parts, num):
    num[...] = jnp.zeros_like(num)

    def visit(t, carry):
        both = parts[t, 64:112, :].astype(F32)
        for p in range(2):
            at, col = meta[t, 4 * p], meta[t, 4 * p + 1]
            mask = lanes(HALO) >= col
            piece = both[HALO * p : HALO * p + HALO]
            num[at] += jnp.where(mask, piece, 0.0)
            num[at + 1] += jnp.where(mask, 0.0, piece)
        return carry

    lax.fori_loop(0, N_TM, visit, 0, unroll=UNROLL)


def update_kernel(meta, parts, scale, high, out, denom, upd, fresh):
    accumulate(meta, parts, upd)

    def visit(t, carry):
        step = upd[t] * scale[t]
        upd[t] = step
        fresh[t] = high[t].astype(F32)[0:HALO] + step
        return carry

    lax.fori_loop(0, N_TM, visit, 0, unroll=UNROLL)

    def store(t, p, piece):
        out[t, CH * p : CH * p + CH, :] = piece

    cut_windows(meta, lambda at: fresh[at], store, denom)


def last_update_kernel(meta, parts, scale, upd, out, num):
    accumulate(meta, parts, num)

    def visit(t, carry):
        total = upd[t] + num[t] * scale[t]
        out[t] = jnp.concatenate([total, jnp.zeros((8, PS), F32)], axis=0).astype(BF16)
        return carry

    lax.fori_loop(0, N_TM, visit, 0, unroll=UNROLL)


def probe_sum_kernel(parts, denom, out):
    total = lax.fori_loop(0, N_TM, lambda t, acc: acc + parts[t, 0:64, :].astype(F32), jnp.zeros((64, PS), F32))
    out[0:64, :] = total.astype(BF16)
    out[64:80, :] = denom[...]


def probe_update_kernel(own, one, two, three, objs, left_out, out, left_out_now):
    total = (own[...].astype(F32) + two[...].astype(F32)) + (one[...].astype(F32) + three[...].astype(F32))
    scale = 1.0 / (total[64:80] + PROBE_REG)
    exact = total[0:64] * jnp.concatenate([scale] * 4, axis=0) + left_out[...]
    step = exact.astype(BF16)
    left_out_now[...] = exact - step.astype(F32)

    def visit(t, carry):
        out[t, 0:32, :] = objs[t]
        out[t, 32:96, :] = step
        return carry

    lax.fori_loop(0, N_TM, visit, 0, unroll=UNROLL)


def pack_kernel(keep, recv, denom, out, denom_out):
    first = lax.axis_index("mode") == 0

    def visit(t, carry):
        mine, theirs = keep[t].astype(F32), recv[t].astype(F32)
        out[t, 0:64, :] = (mine[0:64] + theirs[0:64]).astype(BF16)
        num_mine, num_theirs = mine[64 : 64 + HALO], theirs[64 : 64 + HALO]
        out[t, 64:112, :] = jnp.concatenate(
            [jnp.where(first, num_mine, num_theirs), jnp.where(first, num_theirs, num_mine)], axis=0
        ).astype(BF16)
        return carry

    lax.fori_loop(0, N_TM, visit, 0, unroll=UNROLL)
    theirs = [recv[t, 64:96, :].astype(F32)[HALO:32] for t in range(2)]
    denom_out[...] = (denom[...] + jnp.concatenate(theirs, axis=0)).astype(BF16)


def parts_of(value):
    high, low = split(value)
    return (high, low, high)[:PARTS]


def put_left(ref, row, cols, value):
    for k, part in enumerate(parts_of(value)):
        ref[pl.ds(pl.multiple_of(row + k * PS, CH), CH), cols] = part


def put_right(ref, rows, lane, value):
    for k, part in enumerate(parts_of(value)):
        ref[rows, lane + k * PS : lane + k * PS + HALF] = part


def position_kernel(
    with_update, meta, tables, p_own, p_oth, h_own, h_oth, amp, denom,
    keep, send, power, obj, probe, x_even, x_odd, y_even, y_odd, half_even, half_odd, far_even, far_odd, shifted,
    left, right,
):
    for k in range(4):
        for part, which in enumerate((0, 0, 1)[:PARTS]):
            left[k, :, part * PS : (part + 1) * PS] = tables[which, k]
            right[k, part * PS : (part + 1) * PS, :] = tables[which, k]
    even, even_t, odd, odd_t = range(4)
    core = lax.axis_index("mode")
    first = core == 0
    col, row, alive = (meta[lax.axis_index("tm"), 4 * core + k] for k in (1, 2, 3))
    alive = alive.astype(F32)
    back_col = lax.rem(PS - col, PS)

    def rows_of(i, base=0):
        return pl.ds(pl.multiple_of(i * CH + base, CH), CH)

    def mode_cols(m):
        return slice(m * PS, (m + 1) * PS)

    power[0:8, :] = jnp.zeros((8, PS), F32)
    power[264:272, :] = jnp.zeros((8, PS), F32)

    def stage(i, carry):
        rows = rows_of(i)
        if with_update:
            mine = jnp.where(first, h_own[i, 0:CH, :].astype(F32), h_own[i, CH : 2 * CH, :].astype(F32))
            theirs = jnp.where(first, h_oth[i, 0:CH, :].astype(F32), h_oth[i, CH : 2 * CH, :].astype(F32))
            window = (jnp.where(first, mine, theirs), jnp.where(first, theirs, mine))
        else:
            window = [h_own[2 * i + k].astype(F32) for k in range(2)]
        for k in range(2):
            obj[k, rows, :] = pltpu.roll(window[k], back_col, 1)
        total = jnp.zeros((CH, PS), F32)
        for m in range(4):
            src, chunk = (p_own, h_own) if m < 2 else (p_oth, h_oth)
            for k in range(2):
                value = src[m % 2, k, rows, :]
                if with_update:
                    at = 32 + CH * (2 * (m % 2) + k)
                    value = value + chunk[i, at : at + CH, :].astype(F32)
                probe[m, k, rows, :] = value
                total = total + value * value
        power[pl.ds(pl.multiple_of(i * CH + 8, 8), CH), :] = total
        return carry

    lax.fori_loop(0, N_TM, stage, 0, unroll=UNROLL)

    def wave(m, rows):
        pr, pi = probe[m, 0, rows, :], probe[m, 1, rows, :]
        o_r, o_i = obj[0, rows, :], obj[1, rows, :]
        return pr * o_r - pi * o_i, pr * o_i + pi * o_r

    def forward_rows(i, carry):
        for m in range(4):
            upper, lower = wave(m, rows_of(i)), wave(m, rows_of(i, HALF))
            for k in range(2):
                a, b = upper[k], lower[k]
                put_left(x_even, i * CH + k * HALF, mode_cols(m), a + b)
                put_left(x_odd, i * CH + k * HALF, mode_cols(m), a - b)
        return carry

    lax.fori_loop(0, HALF // CH, forward_rows, 0, unroll=8)
    half_even[...] = dot(left[even], x_even[...])
    half_odd[...] = dot(left[odd], x_odd[...])

    def forward_cols(i, carry):
        for m in range(4):
            for b, half in enumerate((half_even, half_odd)):
                for k in range(2):
                    value = half[rows_of(i, k * HALF), mode_cols(m)]
                    rows = rows_of(i, m * PS + b * HALF)
                    put_right(y_even, rows, k * HALF, value[:, 0:HALF] + value[:, HALF:PS])
                    put_right(y_odd, rows, k * HALF, value[:, 0:HALF] - value[:, HALF:PS])
        return carry

    lax.fori_loop(0, HALF // CH, forward_cols, 0, unroll=8)
    far_even[...] = dot(y_even[...], right[even_t])
    far_odd[...] = dot(y_odd[...], right[odd_t])

    def rescale(i, carry):
        for b, (far, y) in enumerate(((far_even, y_even), (far_odd, y_odd))):
            values = [far[rows_of(i, m * PS), :] for m in range(4)]
            squares = [v[:, 0:HALF] * v[:, 0:HALF] + v[:, HALF:PS] * v[:, HALF:PS] for v in values]
            total = (squares[0] + squares[1]).astype(BF16).astype(F32) + (squares[2] + squares[3]).astype(
                BF16
            ).astype(F32)
            factor = amp[rows_of(i), b * HALF : (b + 1) * HALF] * lax.rsqrt(jnp.maximum(total, FLOOR_VALUE)) - 1.0
            for m in range(4):
                for k in range(2):
                    put_right(y, rows_of(i, m * PS), k * HALF, values[m][:, k * HALF : (k + 1) * HALF] * factor)
        return carry

    lax.fori_loop(0, N_TM, rescale, 0, unroll=UNROLL)
    far_even[...] = dot(y_even[...], right[even])
    far_odd[...] = dot(y_odd[...], right[odd])

    def backward_cols(i, carry):
        for m in range(4):
            for b, x in enumerate((x_even, x_odd)):
                rows = rows_of(i, m * PS + b * HALF)
                one, two = far_even[rows, :], far_odd[rows, :]
                total, diff = one + two, one - two
                for k in range(2):
                    part = slice(k * HALF, (k + 1) * HALF)
                    put_left(x, i * CH + k * HALF, slice(m * PS, m * PS + HALF), total[:, part])
                    put_left(x, i * CH + k * HALF, slice(m * PS + HALF, (m + 1) * PS), diff[:, part])
        return carry

    lax.fori_loop(0, HALF // CH, backward_cols, 0, unroll=8)
    half_even[...] = dot(left[even_t], x_even[...])
    half_odd[...] = dot(left[odd_t], x_odd[...])

    def outputs(i, carry):
        for s in range(2):
            rows = rows_of(i, s * HALF)
            n_re, n_im = jnp.zeros((CH, PS), F32), jnp.zeros((CH, PS), F32)
            for g, target in enumerate((keep, send)):
                g_re, g_im = jnp.zeros((CH, PS), F32), jnp.zeros((CH, PS), F32)
                for mm in range(2):
                    m = 2 * g + mm
                    pr, pi, o_r, o_i = probe[m, 0, rows, :], probe[m, 1, rows, :], obj[0, rows, :], obj[1, rows, :]
                    res = []
                    for k in range(2):
                        at = rows_of(i, k * HALF)
                        one, two = half_even[at, mode_cols(m)], half_odd[at, mode_cols(m)]
                        res.append(one + two if s == 0 else one - two)
                    dr, di = res[0] * alive, res[1] * alive
                    chunk = i + s * (HALF // CH)
                    target[chunk, 2 * mm * CH : (2 * mm + 1) * CH, :] = (o_r * dr + o_i * di).astype(BF16)
                    target[chunk, (2 * mm + 1) * CH : (2 * mm + 2) * CH, :] = (o_r * di - o_i * dr).astype(BF16)
                    g_re = g_re + (pr * dr + pi * di)
                    g_im = g_im + (pr * di - pi * dr)
                n_re = n_re + g_re.astype(BF16).astype(F32)
                n_im = n_im + g_im.astype(BF16).astype(F32)
            at = pl.ds(pl.multiple_of(i * CH + s * HALF + 8, 8), CH)
            shifted[0, at, :] = pltpu.roll(n_re, col, 1)
            shifted[1, at, :] = pltpu.roll(n_im, col, 1)
        return carry

    shifted[:, 0:8, :] = jnp.zeros((2, 8, PS), F32)
    shifted[:, 264:272, :] = jnp.zeros((2, 8, PS), F32)
    lax.fori_loop(0, HALF // CH, outputs, 0, unroll=8)

    def emit(i, carry):
        rows = pl.ds(pl.multiple_of(i * CH, CH), 32)
        pad = jnp.where(i == 0, denom[0:8, :], jnp.where(i == 1, denom[8:16, :], 0.0))
        re, im = (
            jnp.concatenate([shift_rows(shifted[k, rows, :], row), pad], axis=0) for k in range(2)
        )
        keep[i, 64:96, :] = jnp.where(first, re, im).astype(BF16)
        send[i, 64:96, :] = jnp.where(first, im, re).astype(BF16)
        return carry

    lax.fori_loop(0, N_TM, emit, 0, unroll=UNROLL)


def position(with_update, *args):
    part = arr((N_TM, 96, PS), BF16)
    left, right = pltpu.VMEM((PARTS * PS, 4 * PS), BF16), pltpu.VMEM((4 * PS, PARTS * PS), BF16)
    return call(
        functools.partial(position_kernel, with_update),
        (part, part, arr((272, PS), F32)),
        [SM] + [VM] * 7,
        scratch=[
            pltpu.VMEM((2, PS, PS), F32),
            pltpu.VMEM((4, 2, PS, PS), F32),
            left,
            left,
            right,
            right,
            pltpu.VMEM((PS, 4 * PS), F32),
            pltpu.VMEM((PS, 4 * PS), F32),
            pltpu.VMEM((4 * PS, PS), F32),
            pltpu.VMEM((4 * PS, PS), F32),
            pltpu.VMEM((2, 272, PS), F32),
            pltpu.VMEM((4, PS, PARTS * PS), BF16),
            pltpu.VMEM((4, PARTS * PS, PS), BF16),
        ],
        flops=32 * PARTS * 2 * 256 * 256 * 256,
        nbytes=10 << 20,
        vmem=32,
    )(*args)


def final_probe_kernel(p_own, h_one, h_two, out):
    def visit(i, carry):
        rows = pl.ds(pl.multiple_of(i * CH, CH), CH)
        for m in range(2):
            for k in range(2):
                at = 32 + CH * (2 * m + k)
                before = p_own[m, k, rows, :] + h_one[i, at : at + CH, :].astype(F32)
                out[m, k, rows, :] = before + h_two[i, at : at + CH, :].astype(F32)
        return carry

    lax.fori_loop(0, N_TM, visit, 0, unroll=UNROLL)


def final_object_kernel(obj, h_own, h_oth, out):
    core = lax.axis_index("mode")

    def visit(i, carry):
        rows = pl.ds(pl.multiple_of(i * CH, CH), CH)
        out[core, rows, :] = obj[core, rows, :] + h_own[i, 0:CH, :].astype(F32)
        out[1 - core, rows, :] = obj[1 - core, rows, :] + h_oth[i, 0:CH, :].astype(F32)
        return carry

    lax.fori_loop(0, N_TM, visit, 0, unroll=UNROLL)
    last = N_TM - 1
    out[core, 256:264, :] = obj[core, 256:264, :] + h_own[last, 16:32, :].astype(F32)[0:8]
    out[1 - core, 256:264, :] = obj[1 - core, 256:264, :] + h_oth[last, 16:32, :].astype(F32)[0:8]


def body(object_field, probe_modes, amplitudes, anchors, row_offset, col_offset, live_counts):
    tables = jnp.asarray(dft_tables())

    def exchange(x):
        return lax.all_to_all(x, "tm", 0, 0)

    def swap(x):
        return lax.ppermute(x, "mode", SWAP)

    def over_tiles(x):
        n = lax.axis_size("tile")
        return [lax.ppermute(x, "tile", [(i, (i + k) % n) for i in range(n)]) for k in (1, 2, 3)]

    slot = arr((N_TM, 32, PS), BF16)
    denom_shape = arr((CH, PS), F32)
    chunk = (N_TM, HALO, PS)
    high = call(
        prep_kernel,
        slot,
        [pl.BlockSpec(memory_space=pltpu.HBM)] * 5,
        scratch=[
            pltpu.VMEM((BH, PS), F32),
            [pltpu.SMEM(shape, jnp.int32) for shape in ((2,), (2,), (2,), (1, 1))],
            pltpu.SemaphoreType.DMA((5,)),
        ],
        vmem=60,
    )(anchors.reshape(-1), row_offset, col_offset, live_counts.reshape(1, 1), object_field)
    high = exchange(high)
    amp = call(order_kernel, arr((PS, PS), F32), [VM, VM])(jnp.asarray(order_table()), amplitudes)
    high, amp = lax.optimization_barrier((high, amp))
    meta = high[:, HALO, 0:8].astype(jnp.int32)
    windows, denom = call(window_kernel, (arr((2 * N_TM, CH, PS), BF16), denom_shape), [SM, VM])(meta, high)
    windows, own = lax.optimization_barrier((windows, probe_modes))
    probe_other = swap(own)
    h_own = h_oth = lax.all_to_all(windows, ("tm", "mode"), 0, 0)

    left_out = jnp.zeros((64, PS), F32)
    for iteration in range(2):
        if iteration > 0:
            h_oth = swap(h_own)
        keep, send, power = position(
            iteration > 0, meta, tables, probe_modes, probe_other, h_own, h_oth, amp, denom
        )
        recv = swap(send)
        scale = call(weight_kernel, arr(chunk, F32), [SM, VM])(meta, power)
        recv, scale = lax.optimization_barrier((recv, scale))
        parts, denom = call(pack_kernel, (arr((N_TM, 112, PS), BF16), arr((CH, PS), BF16)), [VM] * 3)(
            keep, recv, denom
        )
        parts = exchange(parts)
        probe_part = call(probe_sum_kernel, arr((80, PS), BF16), [VM] * 2)(parts, denom)
        others = over_tiles(probe_part)
        if iteration == 0:
            objs, denom, upd = call(
                update_kernel,
                (slot, denom_shape, arr(chunk, F32)),
                [SM] + [VM] * 3,
                scratch=[pltpu.VMEM(chunk, F32)],
            )(meta, parts, scale, high)
        else:
            objs = call(last_update_kernel, slot, [SM] + [VM] * 3, scratch=[pltpu.VMEM(chunk, F32)])(
                meta, parts, scale, upd
            )
        h_first = h_own
        updates, left_out = call(
            probe_update_kernel, (arr((N_TM, 96, PS), BF16), arr((64, PS), F32)), [VM] * 6
        )(probe_part, *others, objs, left_out)
        h_own = exchange(updates)

    h_oth = swap(h_own)
    probe_out = call(final_probe_kernel, arr((2, 2, PS, PS), F32), [VM] * 3)(probe_modes, h_first, h_own)
    object_out = call(final_object_kernel, arr((2, BH, PS), F32), [VM] * 3)(object_field, h_own, h_oth)
    return (object_out, probe_out)


def solution(mesh):
    placed = (
        P(None, "tile", "tm"),
        P("mode", None, None, None),
        P(("tile", "tm"), None, None),
        P(("tile", "tm"), None),
        P(("tile", "tm")),
        P(("tile", "tm")),
        P(("tile", "tm")),
    )
    return jax.shard_map(
        body,
        mesh=mesh,
        in_specs=placed,
        out_specs=(P(None, "tile", "tm"), P("mode", None, None, None)),
        check_vma=False,
    )
```

```python
import functools

import jax
import jax.numpy as jnp
import ml_dtypes
import numpy as np
from jax import lax
from jax.experimental import pallas as pl
from jax.experimental.pallas import tpu as pltpu
from jax.sharding import PartitionSpec as P

PS = 256
HALF = 128
PARTS = 1
BH = 264
N_TM = 16
UNROLL = 16
CH = 16
HALO = 24
FLOOR_VALUE = 0.5
OBJECT_REG = 1.0
PROBE_REG = 1.0
F32 = jnp.float32
BF16 = jnp.bfloat16
SWAP = [(0, 1), (1, 0)]

VM = pl.BlockSpec(memory_space=pltpu.VMEM)
SM = pl.BlockSpec(memory_space=pltpu.SMEM)


def real_form(matrix):
    return np.block([[matrix.real, -matrix.imag], [matrix.imag, matrix.real]]).astype(np.float32)


def halves(table):
    high = table.astype(ml_dtypes.bfloat16)
    return high, (table - high.astype(np.float32)).astype(ml_dtypes.bfloat16)


def dft_tables():
    n = np.arange(HALF)
    parts = []
    for k in (2 * n, 2 * n + 1):
        table = real_form(np.exp(-2j * np.pi * ((k[:, None] * n[None, :]) % PS) / PS) / np.sqrt(PS))
        parts += [halves(table), halves(table.T)]
    return np.stack([np.stack([p[k] for p in parts]) for k in range(min(PARTS, 2))])


def order_table():
    picked = np.concatenate([np.arange(0, PS, 2), np.arange(1, PS, 2)])
    table = np.zeros((PS, PS), np.float32)
    table[np.arange(PS), picked] = 1.0
    return table.astype(ml_dtypes.bfloat16)


def call(kernel, out_shape, in_specs, scratch=(), flops=0, nbytes=1 << 20, vmem=12):
    many = isinstance(out_shape, (tuple, list))
    return pl.pallas_call(
        kernel,
        out_shape=out_shape,
        in_specs=in_specs,
        out_specs=[VM] * len(out_shape) if many else VM,
        scratch_shapes=list(scratch),
        compiler_params=pltpu.CompilerParams(vmem_limit_bytes=vmem << 20),
        cost_estimate=pl.CostEstimate(flops=flops, bytes_accessed=nbytes, transcendentals=0),
    )


def arr(shape, dtype):
    return jax.ShapeDtypeStruct(shape, dtype)


def lanes(rows):
    return lax.broadcasted_iota(jnp.int32, (rows, PS), 1)


def split(value):
    high = value.astype(BF16)
    return high, (value - high.astype(F32)).astype(BF16)


def dot(a, b):
    return lax.dot_general(a, b, (((1,), (0,)), ((), ())), preferred_element_type=F32)


def prep_kernel(anchors, row_offset, col_offset, live_counts, obj, high, field, ints, sems):
    copies = [pltpu.make_async_copy(obj.at[lax.axis_index("mode")], field, sems.at[0])]
    for k, ref in enumerate((anchors, col_offset, row_offset, live_counts)):
        copies.append(pltpu.make_async_copy(ref, ints[k], sems.at[k + 1]))
    for copy in copies:
        copy.start()
    for copy in copies[1:]:
        copy.wait()
    lane = lanes(8)
    meta = jnp.zeros((8, PS), F32)
    for p in range(2):
        alive = jnp.where(p < ints[3][0, 0], 1, 0)
        for k, value in enumerate((ints[0][p], ints[1][p], ints[2][p], alive)):
            meta = jnp.where(lane == 4 * p + k, value.astype(F32), meta)
    copies[0].wait()
    for i in range(N_TM):
        chunk = field[CH * i : CH * i + HALO, :]
        high[i] = jnp.concatenate([chunk, meta], axis=0).astype(BF16)


def order_kernel(table, amp, out):
    def lines(value, product):
        high, low = split(value)
        return product(high) + product(low)

    rows = lines(amp[lax.axis_index("mode")], lambda x: dot(table[...], x))
    out[...] = lines(rows, lambda x: lax.dot_general(x, table[...], (((1,), (1,)), ((), ())), preferred_element_type=F32))


def cut_windows(meta, load, store, denom):
    def visit(t, total):
        for p in range(2):
            at, col, row, alive = (meta[t, 4 * p + k] for k in range(4))
            both = jnp.where(lanes(HALO) >= col, load(at), load(at + 1))
            both = pltpu.roll(both, lax.rem(HALO - row, HALO), 0)[0:CH].astype(BF16)
            store(t, p, both)
            both = pltpu.roll(both.astype(F32), lax.rem(PS - col, PS), 1)
            total = total + both * both * alive.astype(F32)
        return total

    denom[...] = lax.fori_loop(0, N_TM, visit, jnp.zeros((CH, PS), F32), unroll=UNROLL)


def window_kernel(meta, high, out, denom):
    def store(t, p, piece):
        out[2 * t + p] = piece

    cut_windows(meta, lambda at: high[at].astype(F32)[0:HALO], store, denom)


def shift_rows(block, row):
    return pltpu.roll(block, lax.rem(HALO + row, 32), 0)[0:HALO]


def weight_kernel(meta, power, out):
    out[...] = jnp.full_like(out, OBJECT_REG)
    first = pl.multiple_of(lax.axis_index("tm") * CH, CH)

    def visit(t, carry):
        block = power[pl.ds(first, 32), :]
        for p in range(2):
            at, col, row, alive = (meta[t, 4 * p + k] for k in range(4))
            mask = lanes(HALO) >= col
            cover = pltpu.roll(shift_rows(block, row), col, 1) * alive.astype(F32)
            out[at] += jnp.where(mask, cover, 0.0)
            out[at + 1] += jnp.where(mask, 0.0, cover)
        return carry

    lax.fori_loop(0, N_TM, visit, 0, unroll=UNROLL)

    def invert(t, carry):
        out[t] = 1.0 / out[t]
        return carry

    lax.fori_loop(0, N_TM, invert, 0, unroll=UNROLL)


def accumulate(meta, parts, num):
    num[...] = jnp.zeros_like(num)

    def visit(t, carry):
        both = parts[t, 64:112, :].astype(F32)
        for p in range(2):
            at, col = meta[t, 4 * p], meta[t, 4 * p + 1]
            mask = lanes(HALO) >= col
            piece = both[HALO * p : HALO * p + HALO]
            num[at] += jnp.where(mask, piece, 0.0)
            num[at + 1] += jnp.where(mask, 0.0, piece)
        return carry

    lax.fori_loop(0, N_TM, visit, 0, unroll=UNROLL)


def update_kernel(meta, parts, scale, high, out, denom, upd, fresh):
    accumulate(meta, parts, upd)

    def visit(t, carry):
        step = upd[t] * scale[t]
        upd[t] = step
        fresh[t] = high[t].astype(F32)[0:HALO] + step
        return carry

    lax.fori_loop(0, N_TM, visit, 0, unroll=UNROLL)

    def store(t, p, piece):
        out[t, CH * p : CH * p + CH, :] = piece

    cut_windows(meta, lambda at: fresh[at], store, denom)


def last_update_kernel(meta, parts, scale, upd, out, num):
    accumulate(meta, parts, num)

    def visit(t, carry):
        total = upd[t] + num[t] * scale[t]
        out[t] = jnp.concatenate([total, jnp.zeros((8, PS), F32)], axis=0).astype(BF16)
        return carry

    lax.fori_loop(0, N_TM, visit, 0, unroll=UNROLL)


def probe_sum_kernel(parts, denom, out):
    total = lax.fori_loop(0, N_TM, lambda t, acc: acc + parts[t, 0:64, :].astype(F32), jnp.zeros((64, PS), F32))
    out[0:64, :] = total.astype(BF16)
    out[64:80, :] = denom[...]


def probe_update_kernel(own, one, two, three, objs, left_out, out, left_out_now):
    total = (own[...].astype(F32) + two[...].astype(F32)) + (one[...].astype(F32) + three[...].astype(F32))
    scale = 1.0 / (total[64:80] + PROBE_REG)
    exact = total[0:64] * jnp.concatenate([scale] * 4, axis=0) + left_out[...]
    step = exact.astype(BF16)
    left_out_now[...] = exact - step.astype(F32)

    def visit(t, carry):
        out[t, 0:32, :] = objs[t]
        out[t, 32:96, :] = step
        return carry

    lax.fori_loop(0, N_TM, visit, 0, unroll=UNROLL)


def pack_kernel(keep, recv, denom, out, denom_out):
    first = lax.axis_index("mode") == 0

    def visit(t, carry):
        mine, theirs = keep[t].astype(F32), recv[t].astype(F32)
        out[t, 0:64, :] = (mine[0:64] + theirs[0:64]).astype(BF16)
        num_mine, num_theirs = mine[64 : 64 + HALO], theirs[64 : 64 + HALO]
        out[t, 64:112, :] = jnp.concatenate(
            [jnp.where(first, num_mine, num_theirs), jnp.where(first, num_theirs, num_mine)], axis=0
        ).astype(BF16)
        return carry

    lax.fori_loop(0, N_TM, visit, 0, unroll=UNROLL)
    theirs = [recv[t, 64:96, :].astype(F32)[HALO:32] for t in range(2)]
    denom_out[...] = (denom[...] + jnp.concatenate(theirs, axis=0)).astype(BF16)


def parts_of(value):
    high, low = split(value)
    return (high, low, high)[:PARTS]


def put_left(ref, row, cols, value):
    for k, part in enumerate(parts_of(value)):
        ref[pl.ds(pl.multiple_of(row + k * PS, CH), CH), cols] = part


def put_right(ref, rows, lane, value):
    for k, part in enumerate(parts_of(value)):
        ref[rows, lane + k * PS : lane + k * PS + HALF] = part


def position_kernel(
    with_update, meta, tables, p_own, p_oth, h_own, h_oth, amp, denom,
    keep, send, power, obj, probe, x_even, x_odd, y_even, y_odd, half_even, half_odd, far_even, far_odd, shifted,
    left, right,
):
    if PARTS == 1:
        left = right = tables.at[0]
    for k in range(4 if PARTS > 1 else 0):
        for part, which in enumerate((0, 0, 1)[:PARTS]):
            left[k, :, part * PS : (part + 1) * PS] = tables[which, k]
            right[k, part * PS : (part + 1) * PS, :] = tables[which, k]
    even, even_t, odd, odd_t = range(4)
    core = lax.axis_index("mode")
    first = core == 0
    col, row, alive = (meta[lax.axis_index("tm"), 4 * core + k] for k in (1, 2, 3))
    alive = alive.astype(F32)
    back_col = lax.rem(PS - col, PS)

    def rows_of(i, base=0):
        return pl.ds(pl.multiple_of(i * CH + base, CH), CH)

    def mode_cols(m):
        return slice(m * PS, (m + 1) * PS)

    power[0:8, :] = jnp.zeros((8, PS), F32)
    power[264:272, :] = jnp.zeros((8, PS), F32)

    def stage(i, carry):
        rows = rows_of(i)
        if with_update:
            mine = jnp.where(first, h_own[i, 0:CH, :].astype(F32), h_own[i, CH : 2 * CH, :].astype(F32))
            theirs = jnp.where(first, h_oth[i, 0:CH, :].astype(F32), h_oth[i, CH : 2 * CH, :].astype(F32))
            window = (jnp.where(first, mine, theirs), jnp.where(first, theirs, mine))
        else:
            window = [h_own[2 * i + k].astype(F32) for k in range(2)]
        for k in range(2):
            obj[k, rows, :] = pltpu.roll(window[k], back_col, 1)
        total = jnp.zeros((CH, PS), F32)
        for m in range(4):
            src, chunk = (p_own, h_own) if m < 2 else (p_oth, h_oth)
            for k in range(2):
                value = src[m % 2, k, rows, :]
                if with_update:
                    at = 32 + CH * (2 * (m % 2) + k)
                    value = value + chunk[i, at : at + CH, :].astype(F32)
                probe[m, k, rows, :] = value
                total = total + value * value
        power[pl.ds(pl.multiple_of(i * CH + 8, 8), CH), :] = total
        return carry

    lax.fori_loop(0, N_TM, stage, 0, unroll=UNROLL)

    def wave(m, rows):
        pr, pi = probe[m, 0, rows, :], probe[m, 1, rows, :]
        o_r, o_i = obj[0, rows, :], obj[1, rows, :]
        return pr * o_r - pi * o_i, pr * o_i + pi * o_r

    def forward_rows(i, carry):
        for m in range(4):
            upper, lower = wave(m, rows_of(i)), wave(m, rows_of(i, HALF))
            for k in range(2):
                a, b = upper[k], lower[k]
                put_left(x_even, i * CH + k * HALF, mode_cols(m), a + b)
                put_left(x_odd, i * CH + k * HALF, mode_cols(m), a - b)
        return carry

    lax.fori_loop(0, HALF // CH, forward_rows, 0, unroll=8)
    half_even[...] = dot(left[even], x_even[...])
    half_odd[...] = dot(left[odd], x_odd[...])

    def forward_cols(i, carry):
        for m in range(4):
            for b, half in enumerate((half_even, half_odd)):
                for k in range(2):
                    value = half[rows_of(i, k * HALF), mode_cols(m)]
                    rows = rows_of(i, m * PS + b * HALF)
                    put_right(y_even, rows, k * HALF, value[:, 0:HALF] + value[:, HALF:PS])
                    put_right(y_odd, rows, k * HALF, value[:, 0:HALF] - value[:, HALF:PS])
        return carry

    lax.fori_loop(0, HALF // CH, forward_cols, 0, unroll=8)
    far_even[...] = dot(y_even[...], right[even_t])
    far_odd[...] = dot(y_odd[...], right[odd_t])

    def rescale(i, carry):
        for b, (far, y) in enumerate(((far_even, y_even), (far_odd, y_odd))):
            values = [far[rows_of(i, m * PS), :] for m in range(4)]
            squares = [v[:, 0:HALF] * v[:, 0:HALF] + v[:, HALF:PS] * v[:, HALF:PS] for v in values]
            total = (squares[0] + squares[1]).astype(BF16).astype(F32) + (squares[2] + squares[3]).astype(
                BF16
            ).astype(F32)
            factor = amp[rows_of(i), b * HALF : (b + 1) * HALF] * lax.rsqrt(jnp.maximum(total, FLOOR_VALUE)) - 1.0
            for m in range(4):
                for k in range(2):
                    put_right(y, rows_of(i, m * PS), k * HALF, values[m][:, k * HALF : (k + 1) * HALF] * factor)
        return carry

    lax.fori_loop(0, N_TM, rescale, 0, unroll=UNROLL)
    far_even[...] = dot(y_even[...], right[even])
    far_odd[...] = dot(y_odd[...], right[odd])

    def backward_cols(i, carry):
        for m in range(4):
            for b, x in enumerate((x_even, x_odd)):
                rows = rows_of(i, m * PS + b * HALF)
                one, two = far_even[rows, :], far_odd[rows, :]
                total, diff = one + two, one - two
                for k in range(2):
                    part = slice(k * HALF, (k + 1) * HALF)
                    put_left(x, i * CH + k * HALF, slice(m * PS, m * PS + HALF), total[:, part])
                    put_left(x, i * CH + k * HALF, slice(m * PS + HALF, (m + 1) * PS), diff[:, part])
        return carry

    lax.fori_loop(0, HALF // CH, backward_cols, 0, unroll=8)
    half_even[...] = dot(left[even_t], x_even[...])
    half_odd[...] = dot(left[odd_t], x_odd[...])

    def outputs(i, carry):
        for s in range(2):
            rows = rows_of(i, s * HALF)
            n_re, n_im = jnp.zeros((CH, PS), F32), jnp.zeros((CH, PS), F32)
            for g, target in enumerate((keep, send)):
                g_re, g_im = jnp.zeros((CH, PS), F32), jnp.zeros((CH, PS), F32)
                for mm in range(2):
                    m = 2 * g + mm
                    pr, pi, o_r, o_i = probe[m, 0, rows, :], probe[m, 1, rows, :], obj[0, rows, :], obj[1, rows, :]
                    res = []
                    for k in range(2):
                        at = rows_of(i, k * HALF)
                        one, two = half_even[at, mode_cols(m)], half_odd[at, mode_cols(m)]
                        res.append(one + two if s == 0 else one - two)
                    dr, di = res[0] * alive, res[1] * alive
                    chunk = i + s * (HALF // CH)
                    target[chunk, 2 * mm * CH : (2 * mm + 1) * CH, :] = (o_r * dr + o_i * di).astype(BF16)
                    target[chunk, (2 * mm + 1) * CH : (2 * mm + 2) * CH, :] = (o_r * di - o_i * dr).astype(BF16)
                    g_re = g_re + (pr * dr + pi * di)
                    g_im = g_im + (pr * di - pi * dr)
                n_re = n_re + g_re.astype(BF16).astype(F32)
                n_im = n_im + g_im.astype(BF16).astype(F32)
            at = pl.ds(pl.multiple_of(i * CH + s * HALF + 8, 8), CH)
            shifted[0, at, :] = pltpu.roll(n_re, col, 1)
            shifted[1, at, :] = pltpu.roll(n_im, col, 1)
        return carry

    shifted[:, 0:8, :] = jnp.zeros((2, 8, PS), F32)
    shifted[:, 264:272, :] = jnp.zeros((2, 8, PS), F32)
    lax.fori_loop(0, HALF // CH, outputs, 0, unroll=8)

    def emit(i, carry):
        rows = pl.ds(pl.multiple_of(i * CH, CH), 32)
        pad = jnp.where(i == 0, denom[0:8, :], jnp.where(i == 1, denom[8:16, :], 0.0))
        re, im = (
            jnp.concatenate([shift_rows(shifted[k, rows, :], row), pad], axis=0) for k in range(2)
        )
        keep[i, 64:96, :] = jnp.where(first, re, im).astype(BF16)
        send[i, 64:96, :] = jnp.where(first, im, re).astype(BF16)
        return carry

    lax.fori_loop(0, N_TM, emit, 0, unroll=UNROLL)


def position(with_update, *args):
    part = arr((N_TM, 96, PS), BF16)
    left, right = pltpu.VMEM((PARTS * PS, 4 * PS), BF16), pltpu.VMEM((4 * PS, PARTS * PS), BF16)
    return call(
        functools.partial(position_kernel, with_update),
        (part, part, arr((272, PS), F32)),
        [SM] + [VM] * 7,
        scratch=[
            pltpu.VMEM((2, PS, PS), F32),
            pltpu.VMEM((4, 2, PS, PS), F32),
            left,
            left,
            right,
            right,
            pltpu.VMEM((PS, 4 * PS), F32),
            pltpu.VMEM((PS, 4 * PS), F32),
            pltpu.VMEM((4 * PS, PS), F32),
            pltpu.VMEM((4 * PS, PS), F32),
            pltpu.VMEM((2, 272, PS), F32),
            pltpu.VMEM((4, PS, PARTS * PS), BF16),
            pltpu.VMEM((4, PARTS * PS, PS), BF16),
        ],
        flops=32 * PARTS * 2 * 256 * 256 * 256,
        nbytes=10 << 20,
        vmem=32,
    )(*args)


def final_probe_kernel(p_own, h_one, h_two, out):
    def visit(i, carry):
        rows = pl.ds(pl.multiple_of(i * CH, CH), CH)
        for m in range(2):
            for k in range(2):
                at = 32 + CH * (2 * m + k)
                before = p_own[m, k, rows, :] + h_one[i, at : at + CH, :].astype(F32)
                out[m, k, rows, :] = before + h_two[i, at : at + CH, :].astype(F32)
        return carry

    lax.fori_loop(0, N_TM, visit, 0, unroll=UNROLL)


def final_object_kernel(obj, h_own, h_oth, out):
    core = lax.axis_index("mode")

    def visit(i, carry):
        rows = pl.ds(pl.multiple_of(i * CH, CH), CH)
        out[core, rows, :] = obj[core, rows, :] + h_own[i, 0:CH, :].astype(F32)
        out[1 - core, rows, :] = obj[1 - core, rows, :] + h_oth[i, 0:CH, :].astype(F32)
        return carry

    lax.fori_loop(0, N_TM, visit, 0, unroll=UNROLL)
    last = N_TM - 1
    out[core, 256:264, :] = obj[core, 256:264, :] + h_own[last, 16:32, :].astype(F32)[0:8]
    out[1 - core, 256:264, :] = obj[1 - core, 256:264, :] + h_oth[last, 16:32, :].astype(F32)[0:8]


def body(object_field, probe_modes, amplitudes, anchors, row_offset, col_offset, live_counts):
    tables = jnp.asarray(dft_tables())

    def exchange(x):
        return lax.all_to_all(x, "tm", 0, 0)

    def swap(x):
        return lax.ppermute(x, "mode", SWAP)

    def over_tiles(x):
        n = lax.axis_size("tile")
        return [lax.ppermute(x, "tile", [(i, (i + k) % n) for i in range(n)]) for k in (1, 2, 3)]

    slot = arr((N_TM, 32, PS), BF16)
    denom_shape = arr((CH, PS), F32)
    chunk = (N_TM, HALO, PS)
    high = call(
        prep_kernel,
        slot,
        [pl.BlockSpec(memory_space=pltpu.HBM)] * 5,
        scratch=[
            pltpu.VMEM((BH, PS), F32),
            [pltpu.SMEM(shape, jnp.int32) for shape in ((2,), (2,), (2,), (1, 1))],
            pltpu.SemaphoreType.DMA((5,)),
        ],
        vmem=60,
    )(anchors.reshape(-1), row_offset, col_offset, live_counts.reshape(1, 1), object_field)
    high = exchange(high)
    amp = call(order_kernel, arr((PS, PS), F32), [VM, VM])(jnp.asarray(order_table()), amplitudes)
    high, amp = lax.optimization_barrier((high, amp))
    meta = high[:, HALO, 0:8].astype(jnp.int32)
    windows, denom = call(window_kernel, (arr((2 * N_TM, CH, PS), BF16), denom_shape), [SM, VM])(meta, high)
    windows, own = lax.optimization_barrier((windows, probe_modes))
    probe_other = swap(own)
    h_own = h_oth = lax.all_to_all(windows, ("tm", "mode"), 0, 0)

    left_out = jnp.zeros((64, PS), F32)
    for iteration in range(2):
        if iteration > 0:
            h_oth = swap(h_own)
        keep, send, power = position(
            iteration > 0, meta, tables, probe_modes, probe_other, h_own, h_oth, amp, denom
        )
        recv = swap(send)
        scale = call(weight_kernel, arr(chunk, F32), [SM, VM])(meta, power)
        recv, scale = lax.optimization_barrier((recv, scale))
        parts, denom = call(pack_kernel, (arr((N_TM, 112, PS), BF16), arr((CH, PS), BF16)), [VM] * 3)(
            keep, recv, denom
        )
        parts = exchange(parts)
        probe_part = call(probe_sum_kernel, arr((80, PS), BF16), [VM] * 2)(parts, denom)
        others = over_tiles(probe_part)
        if iteration == 0:
            objs, denom, upd = call(
                update_kernel,
                (slot, denom_shape, arr(chunk, F32)),
                [SM] + [VM] * 3,
                scratch=[pltpu.VMEM(chunk, F32)],
            )(meta, parts, scale, high)
        else:
            objs = call(last_update_kernel, slot, [SM] + [VM] * 3, scratch=[pltpu.VMEM(chunk, F32)])(
                meta, parts, scale, upd
            )
        h_first = h_own
        updates, left_out = call(
            probe_update_kernel, (arr((N_TM, 96, PS), BF16), arr((64, PS), F32)), [VM] * 6
        )(probe_part, *others, objs, left_out)
        h_own = exchange(updates)

    h_oth = swap(h_own)
    probe_out = call(final_probe_kernel, arr((2, 2, PS, PS), F32), [VM] * 3)(probe_modes, h_first, h_own)
    object_out = call(final_object_kernel, arr((2, BH, PS), F32), [VM] * 3)(object_field, h_own, h_oth)
    return (object_out, probe_out)


def solution(mesh):
    placed = (
        P(None, "tile", "tm"),
        P("mode", None, None, None),
        P(("tile", "tm"), None, None),
        P(("tile", "tm"), None),
        P(("tile", "tm")),
        P(("tile", "tm")),
        P(("tile", "tm")),
    )
    return jax.shard_map(
        body,
        mesh=mesh,
        in_specs=placed,
        out_specs=(P(None, "tile", "tm"), P("mode", None, None, None)),
        check_vma=False,
    )
```

```python
import functools

import jax
import jax.numpy as jnp
import ml_dtypes
import numpy as np
from jax import lax
from jax.experimental import pallas as pl
from jax.experimental.pallas import tpu as pltpu
from jax.sharding import PartitionSpec as P

PS = 256
HALF = 128
PARTS = 1
BH = 264
N_TM = 16
UNROLL = 16
CH = 16
HALO = 24
FLOOR_VALUE = 0.5
OBJECT_REG = 1.0
PROBE_REG = 1.0
F32 = jnp.float32
BF16 = jnp.bfloat16
SWAP = [(0, 1), (1, 0)]

VM = pl.BlockSpec(memory_space=pltpu.VMEM)
SM = pl.BlockSpec(memory_space=pltpu.SMEM)


def real_form(matrix):
    return np.block([[matrix.real, -matrix.imag], [matrix.imag, matrix.real]]).astype(np.float32)


def halves(table):
    high = table.astype(ml_dtypes.bfloat16)
    return high, (table - high.astype(np.float32)).astype(ml_dtypes.bfloat16)


def dft_tables():
    n = np.arange(HALF)
    parts = []
    for k in (2 * n, 2 * n + 1):
        table = real_form(np.exp(-2j * np.pi * ((k[:, None] * n[None, :]) % PS) / PS) / np.sqrt(PS))
        parts += [halves(table), halves(table.T)]
    return np.stack([np.stack([p[k] for p in parts]) for k in range(min(PARTS, 2))])


def order_table():
    picked = np.concatenate([np.arange(0, PS, 2), np.arange(1, PS, 2)])
    table = np.zeros((PS, PS), np.float32)
    table[np.arange(PS), picked] = 1.0
    return table.astype(ml_dtypes.bfloat16)


def call(kernel, out_shape, in_specs, scratch=(), flops=0, nbytes=1 << 20, vmem=12):
    many = isinstance(out_shape, (tuple, list))
    return pl.pallas_call(
        kernel,
        out_shape=out_shape,
        in_specs=in_specs,
        out_specs=[VM] * len(out_shape) if many else VM,
        scratch_shapes=list(scratch),
        compiler_params=pltpu.CompilerParams(vmem_limit_bytes=vmem << 20),
        cost_estimate=pl.CostEstimate(flops=flops, bytes_accessed=nbytes, transcendentals=0),
    )


def arr(shape, dtype):
    return jax.ShapeDtypeStruct(shape, dtype)


def lanes(rows):
    return lax.broadcasted_iota(jnp.int32, (rows, PS), 1)


def split(value):
    high = value.astype(BF16)
    return high, (value - high.astype(F32)).astype(BF16)


def dot(a, b):
    return lax.dot_general(a, b, (((1,), (0,)), ((), ())), preferred_element_type=F32)


def prep_kernel(anchors, row_offset, col_offset, live_counts, obj, high, field, ints, sems):
    copies = [pltpu.make_async_copy(obj.at[lax.axis_index("mode")], field, sems.at[0])]
    for k, ref in enumerate((anchors, col_offset, row_offset, live_counts)):
        copies.append(pltpu.make_async_copy(ref, ints[k], sems.at[k + 1]))
    for copy in copies:
        copy.start()
    for copy in copies[1:]:
        copy.wait()
    lane = lanes(8)
    meta = jnp.zeros((8, PS), F32)
    for p in range(2):
        alive = jnp.where(p < ints[3][0, 0], 1, 0)
        for k, value in enumerate((ints[0][p], ints[1][p], ints[2][p], alive)):
            meta = jnp.where(lane == 4 * p + k, value.astype(F32), meta)
    copies[0].wait()
    for i in range(N_TM):
        chunk = field[CH * i : CH * i + HALO, :]
        high[i] = jnp.concatenate([chunk, meta], axis=0).astype(BF16)


def order_kernel(table, amp, out):
    def lines(value, product):
        high, low = split(value)
        return product(high) + product(low)

    rows = lines(amp[lax.axis_index("mode")], lambda x: dot(table[...], x))
    out[...] = lines(rows, lambda x: lax.dot_general(x, table[...], (((1,), (1,)), ((), ())), preferred_element_type=F32))


def cut_windows(meta, load, store, denom):
    def visit(t, total):
        for p in range(2):
            at, col, row, alive = (meta[t, 4 * p + k] for k in range(4))
            both = jnp.where(lanes(HALO) >= col, load(at), load(at + 1))
            both = pltpu.roll(both, lax.rem(HALO - row, HALO), 0)[0:CH].astype(BF16)
            store(t, p, both)
            both = pltpu.roll(both.astype(F32), lax.rem(PS - col, PS), 1)
            total = total + both * both * alive.astype(F32)
        return total

    denom[...] = lax.fori_loop(0, N_TM, visit, jnp.zeros((CH, PS), F32), unroll=UNROLL)


def window_kernel(meta, high, out, denom):
    def store(t, p, piece):
        out[2 * t + p] = piece

    cut_windows(meta, lambda at: high[at].astype(F32)[0:HALO], store, denom)


def shift_rows(block, row):
    return pltpu.roll(block, lax.rem(HALO + row, 32), 0)[0:HALO]


def weight_kernel(meta, power, out):
    out[...] = jnp.full_like(out, OBJECT_REG)
    first = pl.multiple_of(lax.axis_index("tm") * CH, CH)

    def visit(t, carry):
        block = power[pl.ds(first, 32), :]
        for p in range(2):
            at, col, row, alive = (meta[t, 4 * p + k] for k in range(4))
            mask = lanes(HALO) >= col
            cover = pltpu.roll(shift_rows(block, row), col, 1) * alive.astype(F32)
            out[at] += jnp.where(mask, cover, 0.0)
            out[at + 1] += jnp.where(mask, 0.0, cover)
        return carry

    lax.fori_loop(0, N_TM, visit, 0, unroll=UNROLL)

    def invert(t, carry):
        out[t] = 1.0 / out[t]
        return carry

    lax.fori_loop(0, N_TM, invert, 0, unroll=UNROLL)


def accumulate(meta, parts, num):
    num[...] = jnp.zeros_like(num)

    def visit(t, carry):
        both = parts[t, 64:112, :].astype(F32)
        for p in range(2):
            at, col = meta[t, 4 * p], meta[t, 4 * p + 1]
            mask = lanes(HALO) >= col
            piece = both[HALO * p : HALO * p + HALO]
            num[at] += jnp.where(mask, piece, 0.0)
            num[at + 1] += jnp.where(mask, 0.0, piece)
        return carry

    lax.fori_loop(0, N_TM, visit, 0, unroll=UNROLL)


def update_kernel(meta, parts, scale, high, out, denom, upd, fresh):
    accumulate(meta, parts, upd)

    def visit(t, carry):
        step = upd[t] * scale[t]
        upd[t] = step
        fresh[t] = high[t].astype(F32)[0:HALO] + step
        return carry

    lax.fori_loop(0, N_TM, visit, 0, unroll=UNROLL)

    def store(t, p, piece):
        out[t, CH * p : CH * p + CH, :] = piece

    cut_windows(meta, lambda at: fresh[at], store, denom)


def last_update_kernel(meta, parts, scale, upd, out, num):
    accumulate(meta, parts, num)

    def visit(t, carry):
        total = upd[t] + num[t] * scale[t]
        out[t] = jnp.concatenate([total, jnp.zeros((8, PS), F32)], axis=0).astype(BF16)
        return carry

    lax.fori_loop(0, N_TM, visit, 0, unroll=UNROLL)


def probe_sum_kernel(parts, denom, out):
    total = lax.fori_loop(0, N_TM, lambda t, acc: acc + parts[t, 0:64, :].astype(F32), jnp.zeros((64, PS), F32))
    out[0:64, :] = total.astype(BF16)
    out[64:80, :] = denom[...]


def probe_update_kernel(own, one, two, three, objs, *refs):
    out, left_out_now = refs[-2:]
    total = (own[...].astype(F32) + two[...].astype(F32)) + (one[...].astype(F32) + three[...].astype(F32))
    scale = 1.0 / (total[64:80] + PROBE_REG)
    exact = total[0:64] * jnp.concatenate([scale] * 4, axis=0)
    if len(refs) > 2:
        exact = exact + refs[0][...]
    step = exact.astype(BF16)
    left_out_now[...] = exact - step.astype(F32)

    def visit(t, carry):
        out[t, 0:32, :] = objs[t]
        out[t, 32:96, :] = step
        return carry

    lax.fori_loop(0, N_TM, visit, 0, unroll=UNROLL)


def pack_kernel(keep, recv, denom, out, denom_out):
    first = lax.axis_index("mode") == 0

    def visit(t, carry):
        mine, theirs = keep[t].astype(F32), recv[t].astype(F32)
        out[t, 0:64, :] = (mine[0:64] + theirs[0:64]).astype(BF16)
        num_mine, num_theirs = mine[64 : 64 + HALO], theirs[64 : 64 + HALO]
        out[t, 64:112, :] = jnp.concatenate(
            [jnp.where(first, num_mine, num_theirs), jnp.where(first, num_theirs, num_mine)], axis=0
        ).astype(BF16)
        return carry

    lax.fori_loop(0, N_TM, visit, 0, unroll=UNROLL)
    theirs = [recv[t, 64:96, :].astype(F32)[HALO:32] for t in range(2)]
    denom_out[...] = (denom[...] + jnp.concatenate(theirs, axis=0)).astype(BF16)


def parts_of(value):
    high, low = split(value)
    return (high, low, high)[:PARTS]


def put_left(ref, row, cols, value):
    for k, part in enumerate(parts_of(value)):
        ref[pl.ds(pl.multiple_of(row + k * PS, CH), CH), cols] = part


def put_right(ref, rows, lane, value):
    for k, part in enumerate(parts_of(value)):
        ref[rows, lane + k * PS : lane + k * PS + HALF] = part


def position_kernel(
    with_update, meta, tables, p_own, p_oth, h_own, h_oth, amp, denom,
    keep, send, power, obj, probe, x_even, x_odd, y_even, y_odd, half_even, half_odd, far_even, far_odd, shifted,
    left, right,
):
    if PARTS == 1:
        left = right = tables.at[0]
    for k in range(4 if PARTS > 1 else 0):
        for part, which in enumerate((0, 0, 1)[:PARTS]):
            left[k, :, part * PS : (part + 1) * PS] = tables[which, k]
            right[k, part * PS : (part + 1) * PS, :] = tables[which, k]
    even, even_t, odd, odd_t = range(4)
    core = lax.axis_index("mode")
    first = core == 0
    col, row, alive = (meta[lax.axis_index("tm"), 4 * core + k] for k in (1, 2, 3))
    alive = alive.astype(F32)
    back_col = lax.rem(PS - col, PS)

    def rows_of(i, base=0):
        return pl.ds(pl.multiple_of(i * CH + base, CH), CH)

    def mode_cols(m):
        return slice(m * PS, (m + 1) * PS)

    power[0:8, :] = jnp.zeros((8, PS), F32)
    power[264:272, :] = jnp.zeros((8, PS), F32)

    def stage(i, carry):
        rows = rows_of(i)
        if with_update:
            mine = jnp.where(first, h_own[i, 0:CH, :].astype(F32), h_own[i, CH : 2 * CH, :].astype(F32))
            theirs = jnp.where(first, h_oth[i, 0:CH, :].astype(F32), h_oth[i, CH : 2 * CH, :].astype(F32))
            window = (jnp.where(first, mine, theirs), jnp.where(first, theirs, mine))
        else:
            window = [h_own[2 * i + k].astype(F32) for k in range(2)]
        for k in range(2):
            obj[k, rows, :] = pltpu.roll(window[k], back_col, 1)
        total = jnp.zeros((CH, PS), F32)
        for m in range(4):
            src, chunk = (p_own, h_own) if m < 2 else (p_oth, h_oth)
            for k in range(2):
                value = src[m % 2, k, rows, :]
                if with_update:
                    at = 32 + CH * (2 * (m % 2) + k)
                    value = value + chunk[i, at : at + CH, :].astype(F32)
                probe[m, k, rows, :] = value
                total = total + value * value
        power[pl.ds(pl.multiple_of(i * CH + 8, 8), CH), :] = total
        return carry

    lax.fori_loop(0, N_TM, stage, 0, unroll=UNROLL)

    def wave(m, rows):
        pr, pi = probe[m, 0, rows, :], probe[m, 1, rows, :]
        o_r, o_i = obj[0, rows, :], obj[1, rows, :]
        return pr * o_r - pi * o_i, pr * o_i + pi * o_r

    def forward_rows(i, carry):
        for m in range(4):
            upper, lower = wave(m, rows_of(i)), wave(m, rows_of(i, HALF))
            for k in range(2):
                a, b = upper[k], lower[k]
                put_left(x_even, i * CH + k * HALF, mode_cols(m), a + b)
                put_left(x_odd, i * CH + k * HALF, mode_cols(m), a - b)
        return carry

    lax.fori_loop(0, HALF // CH, forward_rows, 0, unroll=8)
    half_even[...] = dot(left[even], x_even[...])
    half_odd[...] = dot(left[odd], x_odd[...])

    def forward_cols(i, carry):
        for m in range(4):
            for b, half in enumerate((half_even, half_odd)):
                for k in range(2):
                    value = half[rows_of(i, k * HALF), mode_cols(m)]
                    rows = rows_of(i, m * PS + b * HALF)
                    put_right(y_even, rows, k * HALF, value[:, 0:HALF] + value[:, HALF:PS])
                    put_right(y_odd, rows, k * HALF, value[:, 0:HALF] - value[:, HALF:PS])
        return carry

    lax.fori_loop(0, HALF // CH, forward_cols, 0, unroll=8)
    far_even[...] = dot(y_even[...], right[even_t])
    far_odd[...] = dot(y_odd[...], right[odd_t])

    def rescale(i, carry):
        for b, (far, y) in enumerate(((far_even, y_even), (far_odd, y_odd))):
            values = [far[rows_of(i, m * PS), :] for m in range(4)]
            squares = [v[:, 0:HALF] * v[:, 0:HALF] + v[:, HALF:PS] * v[:, HALF:PS] for v in values]
            total = (squares[0] + squares[1]).astype(BF16).astype(F32) + (squares[2] + squares[3]).astype(
                BF16
            ).astype(F32)
            factor = amp[rows_of(i), b * HALF : (b + 1) * HALF] * lax.rsqrt(jnp.maximum(total, FLOOR_VALUE)) - 1.0
            for m in range(4):
                for k in range(2):
                    put_right(y, rows_of(i, m * PS), k * HALF, values[m][:, k * HALF : (k + 1) * HALF] * factor)
        return carry

    lax.fori_loop(0, N_TM, rescale, 0, unroll=UNROLL)
    far_even[...] = dot(y_even[...], right[even])
    far_odd[...] = dot(y_odd[...], right[odd])

    def backward_cols(i, carry):
        for m in range(4):
            for b, x in enumerate((x_even, x_odd)):
                rows = rows_of(i, m * PS + b * HALF)
                one, two = far_even[rows, :], far_odd[rows, :]
                total, diff = one + two, one - two
                for k in range(2):
                    part = slice(k * HALF, (k + 1) * HALF)
                    put_left(x, i * CH + k * HALF, slice(m * PS, m * PS + HALF), total[:, part])
                    put_left(x, i * CH + k * HALF, slice(m * PS + HALF, (m + 1) * PS), diff[:, part])
        return carry

    lax.fori_loop(0, HALF // CH, backward_cols, 0, unroll=8)
    half_even[...] = dot(left[even_t], x_even[...])
    half_odd[...] = dot(left[odd_t], x_odd[...])

    def outputs(i, carry):
        for s in range(2):
            rows = rows_of(i, s * HALF)
            n_re, n_im = jnp.zeros((CH, PS), F32), jnp.zeros((CH, PS), F32)
            for g, target in enumerate((keep, send)):
                g_re, g_im = jnp.zeros((CH, PS), F32), jnp.zeros((CH, PS), F32)
                for mm in range(2):
                    m = 2 * g + mm
                    pr, pi, o_r, o_i = probe[m, 0, rows, :], probe[m, 1, rows, :], obj[0, rows, :], obj[1, rows, :]
                    res = []
                    for k in range(2):
                        at = rows_of(i, k * HALF)
                        one, two = half_even[at, mode_cols(m)], half_odd[at, mode_cols(m)]
                        res.append(one + two if s == 0 else one - two)
                    dr, di = res[0] * alive, res[1] * alive
                    chunk = i + s * (HALF // CH)
                    target[chunk, 2 * mm * CH : (2 * mm + 1) * CH, :] = (o_r * dr + o_i * di).astype(BF16)
                    target[chunk, (2 * mm + 1) * CH : (2 * mm + 2) * CH, :] = (o_r * di - o_i * dr).astype(BF16)
                    g_re = g_re + (pr * dr + pi * di)
                    g_im = g_im + (pr * di - pi * dr)
                n_re = n_re + g_re.astype(BF16).astype(F32)
                n_im = n_im + g_im.astype(BF16).astype(F32)
            at = pl.ds(pl.multiple_of(i * CH + s * HALF + 8, 8), CH)
            shifted[0, at, :] = pltpu.roll(n_re, col, 1)
            shifted[1, at, :] = pltpu.roll(n_im, col, 1)
        return carry

    shifted[:, 0:8, :] = jnp.zeros((2, 8, PS), F32)
    shifted[:, 264:272, :] = jnp.zeros((2, 8, PS), F32)
    lax.fori_loop(0, HALF // CH, outputs, 0, unroll=8)

    def emit(i, carry):
        rows = pl.ds(pl.multiple_of(i * CH, CH), 32)
        pad = jnp.where(i == 0, denom[0:8, :], jnp.where(i == 1, denom[8:16, :], 0.0))
        re, im = (
            jnp.concatenate([shift_rows(shifted[k, rows, :], row), pad], axis=0) for k in range(2)
        )
        keep[i, 64:96, :] = jnp.where(first, re, im).astype(BF16)
        send[i, 64:96, :] = jnp.where(first, im, re).astype(BF16)
        return carry

    lax.fori_loop(0, N_TM, emit, 0, unroll=UNROLL)


def position(with_update, *args):
    part = arr((N_TM, 96, PS), BF16)
    left, right = pltpu.VMEM((PARTS * PS, 4 * PS), BF16), pltpu.VMEM((4 * PS, PARTS * PS), BF16)
    return call(
        functools.partial(position_kernel, with_update),
        (part, part, arr((272, PS), F32)),
        [SM] + [VM] * 7,
        scratch=[
            pltpu.VMEM((2, PS, PS), F32),
            pltpu.VMEM((4, 2, PS, PS), F32),
            left,
            left,
            right,
            right,
            pltpu.VMEM((PS, 4 * PS), F32),
            pltpu.VMEM((PS, 4 * PS), F32),
            pltpu.VMEM((4 * PS, PS), F32),
            pltpu.VMEM((4 * PS, PS), F32),
            pltpu.VMEM((2, 272, PS), F32),
            pltpu.VMEM((4, PS, PARTS * PS), BF16),
            pltpu.VMEM((4, PARTS * PS, PS), BF16),
        ],
        flops=32 * PARTS * 2 * 256 * 256 * 256,
        nbytes=10 << 20,
        vmem=32,
    )(*args)


def final_probe_kernel(p_own, h_one, h_two, out):
    def visit(i, carry):
        rows = pl.ds(pl.multiple_of(i * CH, CH), CH)
        for m in range(2):
            for k in range(2):
                at = 32 + CH * (2 * m + k)
                before = p_own[m, k, rows, :] + h_one[i, at : at + CH, :].astype(F32)
                out[m, k, rows, :] = before + h_two[i, at : at + CH, :].astype(F32)
        return carry

    lax.fori_loop(0, N_TM, visit, 0, unroll=UNROLL)


def final_object_kernel(obj, h_own, h_oth, out):
    core = lax.axis_index("mode")

    def visit(i, carry):
        rows = pl.ds(pl.multiple_of(i * CH, CH), CH)
        out[core, rows, :] = obj[core, rows, :] + h_own[i, 0:CH, :].astype(F32)
        out[1 - core, rows, :] = obj[1 - core, rows, :] + h_oth[i, 0:CH, :].astype(F32)
        return carry

    lax.fori_loop(0, N_TM, visit, 0, unroll=UNROLL)
    last = N_TM - 1
    out[core, 256:264, :] = obj[core, 256:264, :] + h_own[last, 16:32, :].astype(F32)[0:8]
    out[1 - core, 256:264, :] = obj[1 - core, 256:264, :] + h_oth[last, 16:32, :].astype(F32)[0:8]


def body(object_field, probe_modes, amplitudes, anchors, row_offset, col_offset, live_counts):
    tables = jnp.asarray(dft_tables())

    def exchange(x):
        return lax.all_to_all(x, "tm", 0, 0)

    def swap(x):
        return lax.ppermute(x, "mode", SWAP)

    def over_tiles(x):
        n = lax.axis_size("tile")
        return [lax.ppermute(x, "tile", [(i, (i + k) % n) for i in range(n)]) for k in (1, 2, 3)]

    slot = arr((N_TM, 32, PS), BF16)
    denom_shape = arr((CH, PS), F32)
    chunk = (N_TM, HALO, PS)
    high = call(
        prep_kernel,
        slot,
        [pl.BlockSpec(memory_space=pltpu.HBM)] * 5,
        scratch=[
            pltpu.VMEM((BH, PS), F32),
            [pltpu.SMEM(shape, jnp.int32) for shape in ((2,), (2,), (2,), (1, 1))],
            pltpu.SemaphoreType.DMA((5,)),
        ],
        vmem=60,
    )(anchors.reshape(-1), row_offset, col_offset, live_counts.reshape(1, 1), object_field)
    high = exchange(high)
    amp = call(order_kernel, arr((PS, PS), F32), [VM, VM])(jnp.asarray(order_table()), amplitudes)
    high, amp = lax.optimization_barrier((high, amp))
    meta = high[:, HALO, 0:8].astype(jnp.int32)
    windows, denom = call(window_kernel, (arr((2 * N_TM, CH, PS), BF16), denom_shape), [SM, VM])(meta, high)
    windows, own = lax.optimization_barrier((windows, probe_modes))
    probe_other = swap(own)
    h_own = h_oth = lax.all_to_all(windows, ("tm", "mode"), 0, 0)

    left_out = ()
    for iteration in range(2):
        if iteration > 0:
            h_oth = swap(h_own)
        keep, send, power = position(
            iteration > 0, meta, tables, probe_modes, probe_other, h_own, h_oth, amp, denom
        )
        recv = swap(send)
        scale = call(weight_kernel, arr(chunk, F32), [SM, VM])(meta, power)
        recv, scale = lax.optimization_barrier((recv, scale))
        parts, denom = call(pack_kernel, (arr((N_TM, 112, PS), BF16), arr((CH, PS), BF16)), [VM] * 3)(
            keep, recv, denom
        )
        parts = exchange(parts)
        probe_part = call(probe_sum_kernel, arr((80, PS), BF16), [VM] * 2)(parts, denom)
        others = over_tiles(probe_part)
        if iteration == 0:
            objs, denom, upd = call(
                update_kernel,
                (slot, denom_shape, arr(chunk, F32)),
                [SM] + [VM] * 3,
                scratch=[pltpu.VMEM(chunk, F32)],
            )(meta, parts, scale, high)
        else:
            objs = call(last_update_kernel, slot, [SM] + [VM] * 3, scratch=[pltpu.VMEM(chunk, F32)])(
                meta, parts, scale, upd
            )
        h_first = h_own
        updates, rest = call(
            probe_update_kernel, (arr((N_TM, 96, PS), BF16), arr((64, PS), F32)), [VM] * (5 + iteration)
        )(probe_part, *others, objs, *left_out)
        left_out = (rest,)
        h_own = exchange(updates)

    h_oth = swap(h_own)
    probe_out = call(final_probe_kernel, arr((2, 2, PS, PS), F32), [VM] * 3)(probe_modes, h_first, h_own)
    object_out = call(final_object_kernel, arr((2, BH, PS), F32), [VM] * 3)(object_field, h_own, h_oth)
    return (object_out, probe_out)


def solution(mesh):
    placed = (
        P(None, "tile", "tm"),
        P("mode", None, None, None),
        P(("tile", "tm"), None, None),
        P(("tile", "tm"), None),
        P(("tile", "tm")),
        P(("tile", "tm")),
        P(("tile", "tm")),
    )
    return jax.shard_map(
        body,
        mesh=mesh,
        in_specs=placed,
        out_specs=(P(None, "tile", "tm"), P("mode", None, None, None)),
        check_vma=False,
    )
```
